512 devices in a mesh: mode: 8 (over y_hi, core), row: 64 (over z, y_lo, x).
Axes of the slice: x: 4, y: 8 (y_hi: 4, y_lo: 2; y = y_hi * 2 + y_lo), z: 8, core: 2. Of those that a mesh axis runs over, the one named last changes fastest.
Arguments:
- load_windows: bfloat16 [64, 2048, 128], P('row'), may hold values from -6 to 6
- owner_id: int32 [1], replicated, may hold values from 0 to 63
- participation: bfloat16 [24576, 2048], P(('mode', 'row')), may hold values from -0.125 to 0.125
- frequency: float32 [24576], P(('mode', 'row')), may hold values from 0.05 to 1.5
- damping: float32 [24576], P(('mode', 'row')), may hold values from 0.01 to 0.3
- recovery: bfloat16 [8, 64, 24, 4, 128, 128], P('mode', 'row'), may hold values from -0.25 to 0.25
- pattern: int32 [8, 64, 24, 4], P('mode', 'row'), may hold values from 0 to 23, as said below
- plane_table: int32 [64, 8, 64, 8], P('row', 'mode'), may hold values from 0 to 63
Outputs:
- stress: float32 [64, 8, 6, 64, 128], P('row', 'mode')
- plane_range: float32 [64, 8, 64, 8], P('row', 'mode')
The draws below stay inside these ranges and needn't reach their ends.
Inputs may be any that keep to these rules, and one draw needn't show every extreme that they name: `pattern`: the 4 entries of one row block are different mode blocks of its group.
All inputs are finite; a program needn't handle non-finite values.
Results may differ from the reference program's by a relative error of at most 0.0003.
Values may be sent and summed in bfloat16 or wider, within the bound.
No kernel may reach another device: no remote copies, remote signals or barrier semaphores. Data moves between devices by JAX's collectives and lax.ppermute only.
A program may use at most 64 MiB of HBM per device.

```python
import math
import jax
import jax.numpy as jnp
from jax import lax

C = 2048
M = 24576
NT = 128
PLANES = 64
L = 8
MBK = 128
RBK = 128
K = 4
EL_DEV = 64
GB = 24
RB_COL = 24
COLUMNS = 64
SLABS = 8
WINDOWS = 64


def draw_pattern(key, part):
    scores = jax.random.randint(key, (SLABS, COLUMNS, RB_COL, GB), 0, 1 << 20)
    block_index = jnp.arange(SLABS * COLUMNS * RB_COL).reshape(SLABS, COLUMNS, RB_COL)[..., None]
    mode_index = jnp.arange(GB)[None, None, None, :]
    scores = jnp.where((block_index == 0) & (mode_index == GB - 1), -1, scores)
    scores = jnp.where((block_index == 1) & (mode_index == 0), -1, scores)
    keyed = scores * GB + mode_index
    order = jnp.argsort(keyed, axis=-1, stable=True)[..., :K]
    return order.astype(jnp.int32)


def with_ends(values, stream_key, smallest, high):
    longest = values.shape.index(max(values.shape))
    spots = []
    for shift in (0, 1):
        where = [jax.random.randint(jax.random.fold_in(stream_key, axis), (), 0, length) for axis, length in enumerate(values.shape)]
        where[longest] = (where[longest] + shift) % values.shape[longest]
        spots.append(tuple(where))
    return values.at[spots[0]].set(smallest).at[spots[1]].set(high)


def level_of(stream_key, shape, shards, least, largest):
    factor_of = 1.0
    for dim, blocks in shards:
        draws = jax.random.uniform(jax.random.fold_in(jax.random.fold_in(stream_key, 6), dim), (blocks,), jnp.float32, least / len(shards), largest / len(shards))
        factor_of = factor_of * jnp.repeat(jnp.exp(draws), shape[dim] // blocks).reshape((-1,) + (1,) * (len(shape) - 1 - dim))
    return factor_of


def noise(own_key, extent, scale, most, split=(), held_as=jnp.bfloat16):
    drawn = jax.random.normal(own_key, extent, jnp.float32) * scale
    if len(split) > 0:
        drawn = level_of(own_key, extent, split, -0.22, 0.18) * drawn
    return jnp.clip(drawn, min=-most, max=most).astype(held_as)


def setup_inputs(seed: int = 0) -> dict:
    arg_keys = jax.random.split(jax.random.key(seed), 9)
    return {
        "load_windows": noise(arg_keys[0], (WINDOWS, C, NT), 1.0, 6.0, ((0, 64),)),
        "owner_id": jax.random.randint(arg_keys[1], (1,), 0, WINDOWS).astype(jnp.int32),
        "participation": noise(arg_keys[2], (M, C), C ** -0.5, 0.125, ((0, 512),)),
        "frequency": jnp.clip(jnp.exp(math.log(1.5) - 3.4011974 * jax.random.uniform(arg_keys[3], (M,), jnp.float32) ** level_of(arg_keys[3], (M,), ((0, 512),), -0.2, 0.2)), 0.05, 1.5),
        "damping": jnp.clip(jnp.exp(math.log(0.3) - 3.4011974 * jax.random.uniform(arg_keys[4], (M,), jnp.float32) ** level_of(arg_keys[4], (M,), ((0, 512),), -0.2, 0.2)), 0.01, 0.3),
        "recovery": noise(arg_keys[5], (SLABS, COLUMNS, RB_COL, K, RBK, MBK), (K * MBK) ** -0.5, 0.25, ((0, 8), (1, 64))),
        "pattern": draw_pattern(jax.random.fold_in(arg_keys[8], 71), 0),
        "plane_table": with_ends(jax.random.randint(arg_keys[7], (COLUMNS, SLABS, EL_DEV, L), 0, PLANES), jax.random.fold_in(arg_keys[7], 1), 0, PLANES - 1).astype(jnp.int32),
    }


def plane_coeffs():
    index = jnp.arange(PLANES).astype(jnp.float32)
    height = (index + 0.5) / PLANES
    azimuth = index * 2.399963229728653
    radius = jnp.sqrt(1.0 - height * height)
    normal_x = radius * jnp.cos(azimuth)
    normal_y = radius * jnp.sin(azimuth)
    return jnp.stack([normal_x * normal_x, normal_y * normal_y, height * height, 2.0 * normal_x * normal_y, 2.0 * normal_y * height, 2.0 * normal_x * height], axis=-1)

def integrate_block(loading, rates, decays):
    steps = loading.shape[-1]
    later = jnp.arange(steps)[:, None]
    earlier = jnp.arange(steps)[None, :]
    delay = (later - earlier).astype(jnp.float32)
    clipped = jnp.maximum(delay, 0.0)
    impulse = rates[:, None, None] * jnp.exp(-decays[:, None, None] * rates[:, None, None] * clipped) * jnp.sin(rates[:, None, None] * (clipped + 1.0))
    impulse = jnp.where(delay >= 0.0, impulse, 0.0)
    return jnp.einsum('mts,ms->mt', impulse, loading.astype(jnp.float32), precision=lax.Precision.HIGHEST)

def integrate(loading, rates, decays):
    count = loading.shape[0]
    if count > 128 and count % 128 == 0:
        steps = loading.shape[1]
        result = lax.map(lambda items: integrate_block(items[0], items[1], items[2]), (loading.reshape(count // 128, 128, steps), rates.reshape(count // 128, 128), decays.reshape(count // 128, 128)))
        return result.reshape(count, steps)
    return integrate_block(loading, rates, decays)

def reference(load_windows, owner_id, participation, frequency, damping, recovery, pattern, plane_table):
    window = lax.dynamic_index_in_dim(load_windows, owner_id[0], 0, keepdims=False)
    forces = jnp.dot(participation, window, preferred_element_type=jnp.float32)
    modal_hist = integrate(forces, frequency, damping)
    mode_blocks = modal_hist.reshape(SLABS, GB, MBK, NT)

    def column(index):
        picks = lax.dynamic_index_in_dim(pattern, index, 1, keepdims=False)
        coeff_blocks = lax.dynamic_index_in_dim(recovery, index, 1, keepdims=False)
        chosen = jax.vmap(lambda group_blocks, group_picks: group_blocks[group_picks])(mode_blocks, picks)
        summed = jnp.einsum('gbkrc,gbkct->brt', coeff_blocks.astype(jnp.float32), chosen.astype(jnp.float32), precision=lax.Precision.HIGHEST)
        return summed.reshape(SLABS, 6, EL_DEV, NT)
    stress = lax.map(column, jnp.arange(COLUMNS).astype(jnp.int32))
    coeffs = plane_coeffs()[plane_table]
    normal_stress = jnp.einsum('jselq,jsqet->jselt', coeffs, stress, precision=lax.Precision.HIGHEST)
    plane_range = lax.optimization_barrier(jnp.max(normal_stress, axis=-1)) - lax.optimization_barrier(jnp.min(normal_stress, axis=-1))
    return (stress, plane_range)
```

```python
import jax
import jax.numpy as jnp
from jax import lax
from jax.sharding import Mesh
from jax.sharding import PartitionSpec as P

PLANES = 64
ROW = ("z", "yl", "x")


def plane_coeffs():
    index = jnp.arange(PLANES).astype(jnp.float32)
    height = (index + 0.5) / PLANES
    azimuth = index * 2.399963229728653
    radius = jnp.sqrt(1.0 - height * height)
    normal_x = radius * jnp.cos(azimuth)
    normal_y = radius * jnp.sin(azimuth)
    return jnp.stack(
        [
            normal_x * normal_x,
            normal_y * normal_y,
            height * height,
            2.0 * normal_x * normal_y,
            2.0 * normal_y * height,
            2.0 * normal_x * height,
        ],
        axis=-1,
    )


def integrate(loading, rates, decays):
    steps = loading.shape[-1]
    later = jnp.arange(steps)[:, None]
    earlier = jnp.arange(steps)[None, :]
    delay = (later - earlier).astype(jnp.float32)
    clipped = jnp.maximum(delay, 0.0)
    impulse = (
        rates[:, None, None]
        * jnp.exp(-decays[:, None, None] * rates[:, None, None] * clipped)
        * jnp.sin(rates[:, None, None] * (clipped + 1.0))
    )
    impulse = jnp.where(delay >= 0.0, impulse, 0.0)
    return jnp.einsum("mts,ms->mt", impulse, loading, precision=lax.Precision.HIGHEST)


def gather_row(part, count):
    copies = jnp.broadcast_to(part[None], (count,) + part.shape)
    return lax.all_to_all(copies, ROW, 0, 0)


def fetch_window(windows, owner):
    channels, steps = windows.shape[1:]
    count = lax.axis_size(ROW)
    half = channels // 2
    mine = lax.dynamic_slice_in_dim(windows[0], lax.axis_index("core") * half, half, 0)
    offered = lax.all_to_all(mine.reshape(count, half // count, steps), ROW, 0, 0)
    piece = lax.dynamic_index_in_dim(offered, owner, 0, keepdims=False)
    whole_half = gather_row(piece, count).reshape(half, steps)
    return lax.all_gather(whole_half, "core", axis=0, tiled=True)


def sum_over_mode(partial):
    slabs, rows, steps = partial.shape
    by_core = partial.reshape(slabs // 2, 2, rows, steps).transpose(1, 0, 2, 3)
    both = lax.all_to_all(by_core, "core", 0, 0)
    pair = both[0] + both[1]
    parts = lax.all_to_all(pair, "yh", 0, 0)
    return parts.sum(axis=0)


def body(load_windows, owner_id, participation, frequency, damping, recovery, pattern, plane_table):
    window = fetch_window(load_windows, owner_id[0])
    forces = jnp.dot(participation, window, preferred_element_type=jnp.float32)
    modal_hist = integrate(forces, frequency, damping)
    group_hist = gather_row(modal_hist, lax.axis_size(ROW))
    coeff_blocks = recovery[0, 0]
    picks = pattern[0, 0]
    mode_width = coeff_blocks.shape[3]
    steps = modal_hist.shape[1]
    mode_blocks = group_hist.reshape(-1, mode_width, steps)
    elements = plane_table.shape[2]
    chosen = mode_blocks[picks]
    summed = jnp.einsum(
        "bkrc,bkct->brt",
        coeff_blocks.astype(jnp.float32),
        chosen,
        preferred_element_type=jnp.float32,
        precision=lax.Precision.HIGHEST,
    )
    slabs = lax.axis_size(("yh", "core"))
    stress = sum_over_mode(summed.reshape(slabs, 6 * elements, steps)).reshape(6, elements, steps)
    chosen_planes = plane_table[0, 0]
    one_hot = (chosen_planes[..., None] == jnp.arange(PLANES)[None, None, :]).astype(jnp.float32)
    coeffs = jnp.einsum("elp,pq->elq", one_hot, plane_coeffs(), precision=lax.Precision.HIGHEST)
    normal_stress = jnp.einsum("elq,qet->elt", coeffs, stress, precision=lax.Precision.HIGHEST)
    plane_range = jnp.max(normal_stress, axis=-1) - jnp.min(normal_stress, axis=-1)
    return (stress[None, None], plane_range[None, None])


def solution(mesh):
    fine = Mesh(mesh.devices.reshape(4, 2, 8, 2, 4), ("yh", "core") + ROW)
    mode = ("yh", "core")
    placed = (
        P(ROW, None, None),
        P(),
        P(mode + ROW, None),
        P(mode + ROW),
        P(mode + ROW),
        P(mode, ROW, None, None, None, None),
        P(mode, ROW, None, None),
        P(ROW, mode, None, None),
    )
    return jax.shard_map(
        body,
        mesh=fine,
        in_specs=placed,
        out_specs=(P(ROW, mode, None, None, None), P(ROW, mode, None, None)),
        check_vma=False,
    )
```

```python
import jax
import jax.numpy as jnp
from jax import lax
from jax.experimental import pallas as pl
from jax.experimental.pallas import tpu as pltpu
from jax.sharding import Mesh
from jax.sharding import PartitionSpec as P

PLANES = 64
ROW = ("z", "yl", "x")
CODE_ROWS = 8
CHUNKS = 4


def plane_coeffs():
    index = jnp.arange(PLANES).astype(jnp.float32)
    height = (index + 0.5) / PLANES
    azimuth = index * 2.399963229728653
    radius = jnp.sqrt(1.0 - height * height)
    normal_x = radius * jnp.cos(azimuth)
    normal_y = radius * jnp.sin(azimuth)
    return jnp.stack(
        [
            normal_x * normal_x,
            normal_y * normal_y,
            height * height,
            2.0 * normal_x * normal_y,
            2.0 * normal_y * height,
            2.0 * normal_x * height,
        ],
        axis=-1,
    )


def mode_table(rates, decays, steps):
    doublings = steps.bit_length() - 1
    shifts = 2.0 ** jnp.arange(doublings, dtype=jnp.float32)
    angle = rates[:, None] * shifts
    shrink = jnp.exp(-decays[:, None] * rates[:, None] * shifts)
    last = jnp.stack([rates * jnp.sin(rates), rates * jnp.cos(rates)], axis=-1)
    return jnp.concatenate([shrink * jnp.cos(angle), shrink * jnp.sin(angle), last], axis=-1)


def code_scale(code):
    return jnp.exp2(code * (1.0 / 32.0) - 15.0)


def quantize(values):
    largest = jnp.max(jnp.abs(values), axis=-1, keepdims=True)
    code = jnp.ceil(jnp.log2(jnp.maximum(largest, 1e-30)) * 32.0)
    inverse = jnp.exp2(15.0 - code * (1.0 / 32.0))
    whole = jnp.clip(jnp.round(values * inverse), -32767.0, 32767.0).astype(jnp.int32)
    return whole, code


def as_row(column):
    n = column.shape[0]
    at = lax.broadcasted_iota(jnp.int32, (n, 128), 0) == lax.broadcasted_iota(jnp.int32, (n, 128), 1)
    return jnp.sum(jnp.where(at, column, 0.0), axis=0, keepdims=True)


def history_kernel(window_ref, part_ref, table_ref, out_ref):
    forces = jnp.dot(part_ref[...], window_ref[...], preferred_element_type=jnp.float32)
    modes, steps = forces.shape
    doublings = steps.bit_length() - 1
    table = table_ref[...]
    lane = lax.broadcasted_iota(jnp.int32, forces.shape, 1)
    re, im = forces, jnp.zeros_like(forces)
    for d in range(doublings):
        shift = 1 << d
        p_re, p_im = table[:, d : d + 1], table[:, doublings + d : doublings + d + 1]
        keep = lane >= shift
        old_re = jnp.where(keep, pltpu.roll(re, shift, 1), 0.0)
        if d == 0:
            re, im = re + p_re * old_re, p_im * old_re
            continue
        old_im = jnp.where(keep, pltpu.roll(im, shift, 1), 0.0)
        re, im = re + p_re * old_re - p_im * old_im, im + p_re * old_im + p_im * old_re
    hist = table[:, 2 * doublings : 2 * doublings + 1] * re + table[:, 2 * doublings + 1 : 2 * doublings + 2] * im
    whole, code = quantize(hist)
    codes = jnp.broadcast_to(as_row(code), (CODE_ROWS, 128)).astype(jnp.int32)
    block = jnp.concatenate([whole, codes], axis=0).astype(jnp.int16)
    for i in range(out_ref.shape[0]):
        out_ref[i] = block


def make_history(window, participation, table, count):
    modes, channels = participation.shape
    steps = window.shape[1]
    return pl.pallas_call(
        history_kernel,
        out_shape=jax.ShapeDtypeStruct((count, modes + CODE_ROWS, steps), jnp.int16),
        in_specs=[pl.BlockSpec(memory_space=pltpu.VMEM)] * 3,
        out_specs=pl.BlockSpec(memory_space=pltpu.VMEM),
        compiler_params=pltpu.CompilerParams(vmem_limit_bytes=16 << 20),
        cost_estimate=pl.CostEstimate(
            flops=2 * modes * channels * steps, bytes_accessed=2 * (channels * (modes + steps)), transcendentals=0
        ),
        name="history",
    )(window, participation, table)


def recover_kernel(picks_ref, hist_ref, far_ref, out_ref, split_ref, coeff_ref, sems):
    chunks = sems.shape[0]
    per = coeff_ref.shape[0] // chunks
    fetches = [
        pltpu.make_async_copy(far_ref.at[pl.ds(i * per, per)], coeff_ref.at[pl.ds(i * per, per)], sems.at[i])
        for i in range(chunks)
    ]
    for fetch in fetches:
        fetch.start()
    sources, rows, steps = hist_ref.shape
    modes = rows - CODE_ROWS
    sub = lax.broadcasted_iota(jnp.int32, (8, 128), 0)
    tiles = []
    for base in range(0, sources, 8):
        tile = jnp.zeros((8, 128), jnp.int32)
        for i in range(8):
            codes = hist_ref[base + i, modes : modes + CODE_ROWS, :].astype(jnp.int32)[:8]
            tile = jnp.where(sub == i, codes, tile)
        tiles.append(tile)
    scales = code_scale(jnp.concatenate(tiles, axis=0).astype(jnp.float32))
    scales = jnp.concatenate([scales, jnp.zeros((128 - sources, 128), jnp.float32)], axis=0).T
    for s in range(sources):
        value = hist_ref[s, :modes, :].astype(jnp.int32).astype(jnp.float32) * scales[:modes, s : s + 1]
        high = value.astype(jnp.bfloat16)
        low = (value - high.astype(jnp.float32)).astype(jnp.bfloat16)
        split_ref[s * modes : (s + 1) * modes, :steps] = high
        split_ref[s * modes : (s + 1) * modes, steps:] = low
    blocks, picked, height, width = coeff_ref.shape
    slab = blocks // (2 * out_ref.shape[1])
    for b in range(blocks):
        if b % per == 0:
            fetches[b // per].wait()
        left = jnp.concatenate([coeff_ref[b, k] for k in range(picked)], axis=1)
        right = jnp.concatenate(
            [split_ref[pl.ds(pl.multiple_of(picks_ref[b, k] * width, width), width), :] for k in range(picked)], axis=0
        )
        both = jnp.dot(left, right, preferred_element_type=jnp.float32)
        owner = b // slab
        out_ref[owner % 2, owner // 2, (b % slab) * height : (b % slab + 1) * height, :] = both[:, :steps] + both[:, steps:]


def recover(hist, coeff_blocks, picks, groups):
    sources, rows, steps = hist.shape
    blocks, picked, height, width = coeff_blocks.shape
    return pl.pallas_call(
        recover_kernel,
        out_shape=jax.ShapeDtypeStruct((2, groups // 2, blocks // groups * height, steps), jnp.float32),
        in_specs=[
            pl.BlockSpec(memory_space=pltpu.SMEM),
            pl.BlockSpec(memory_space=pltpu.VMEM),
            pl.BlockSpec(memory_space=pltpu.HBM),
        ],
        out_specs=pl.BlockSpec(memory_space=pltpu.VMEM),
        scratch_shapes=[
            pltpu.VMEM((sources * (rows - CODE_ROWS), 2 * steps), jnp.bfloat16),
            pltpu.VMEM(coeff_blocks.shape, jnp.bfloat16),
            pltpu.SemaphoreType.DMA((CHUNKS,)),
        ],
        compiler_params=pltpu.CompilerParams(vmem_limit_bytes=50 << 20),
        cost_estimate=pl.CostEstimate(
            flops=4 * blocks * picked * height * width * steps,
            bytes_accessed=2 * blocks * picked * height * width,
            transcendentals=0,
        ),
        name="recover",
    )(picks, hist, coeff_blocks)


def range_kernel(parts_ref, coeff_ref, stress_ref, range_ref):
    total = parts_ref[0]
    for i in range(1, parts_ref.shape[0]):
        total = total + parts_ref[i]
    components, elements, steps = stress_ref.shape
    stress = total.reshape(components, elements, steps)
    stress_ref[...] = stress
    looked = range_ref.shape[0]
    lane = lax.broadcasted_iota(jnp.int32, (elements, 128), 1)
    coeffs = coeff_ref[...]
    result = jnp.zeros((elements, 128), jnp.float32)
    for p in range(looked):
        normal = coeffs[:, p * components : p * components + 1] * stress[0]
        for q in range(1, components):
            at = p * components + q
            normal = normal + coeffs[:, at : at + 1] * stress[q]
        spread = jnp.max(normal, axis=-1, keepdims=True) - jnp.min(normal, axis=-1, keepdims=True)
        result = jnp.where(lane == p, spread, result)
    range_ref[...] = result.T[:looked, :]


def finish(parts, coeffs, looked):
    groups, rows, steps = parts.shape
    elements = coeffs.shape[0]
    stress, ranges = pl.pallas_call(
        range_kernel,
        out_shape=(
            jax.ShapeDtypeStruct((rows // elements, elements, steps), jnp.float32),
            jax.ShapeDtypeStruct((looked, elements), jnp.float32),
        ),
        in_specs=[pl.BlockSpec(memory_space=pltpu.VMEM)] * 2,
        out_specs=(pl.BlockSpec(memory_space=pltpu.VMEM),) * 2,
        compiler_params=pltpu.CompilerParams(vmem_limit_bytes=8 << 20),
        name="ranges",
    )(parts, coeffs)
    return stress, ranges.T


def gather_row(part, count):
    copies = jnp.broadcast_to(part[None], (count,) + part.shape)
    return lax.all_to_all(copies, ROW, 0, 0)


def fetch_window(windows, owner):
    channels, steps = windows.shape[1:]
    count = lax.axis_size(ROW)
    half = channels // 2
    mine = lax.dynamic_slice_in_dim(windows[0], lax.axis_index("core") * half, half, 0)
    offered = lax.all_to_all(mine.reshape(count, half // count, steps), ROW, 0, 0)
    piece = lax.dynamic_index_in_dim(offered, owner, 0, keepdims=False)
    whole_half = gather_row(piece, count).reshape(half, steps)
    return lax.all_gather(whole_half, "core", axis=0, tiled=True)


def sum_over_mode(by_core):
    both = lax.all_to_all(by_core, "core", 0, 0)
    pair = both[0] + both[1]
    return lax.all_to_all(pair, "yh", 0, 0)


def body(load_windows, owner_id, participation, frequency, damping, recovery, pattern, plane_table):
    steps = load_windows.shape[2]
    chosen_planes = plane_table[0, 0]
    elements, looked = chosen_planes.shape
    one_hot = (chosen_planes[..., None] == jnp.arange(PLANES)[None, None, :]).astype(jnp.float32)
    coeffs = jnp.einsum("elp,pq->elq", one_hot, plane_coeffs(), precision=lax.Precision.HIGHEST)
    coeffs = coeffs.reshape(elements, looked * 6)
    table = mode_table(frequency, damping, steps)
    window = fetch_window(load_windows, owner_id[0])
    copies = make_history(window, participation, table, lax.axis_size(ROW))
    hist = lax.all_to_all(copies, ROW, 0, 0)
    partial = recover(hist, recovery[0, 0], pattern[0, 0], lax.axis_size(("yh", "core")))
    parts = sum_over_mode(partial)
    stress, plane_range = finish(parts, coeffs, looked)
    return (stress[None, None], plane_range[None, None])


def solution(mesh):
    fine = Mesh(mesh.devices.reshape(4, 2, 8, 2, 4), ("yh", "core") + ROW)
    mode = ("yh", "core")
    placed = (
        P(ROW, None, None),
        P(),
        P(mode + ROW, None),
        P(mode + ROW),
        P(mode + ROW),
        P(mode, ROW, None, None, None, None),
        P(mode, ROW, None, None),
        P(ROW, mode, None, None),
    )
    return jax.shard_map(
        body,
        mesh=fine,
        in_specs=placed,
        out_specs=(P(ROW, mode, None, None, None), P(ROW, mode, None, None)),
        check_vma=False,
    )
```

```python
import jax
import jax.numpy as jnp
from jax import lax
from jax.experimental import pallas as pl
from jax.experimental.pallas import tpu as pltpu
from jax.sharding import Mesh
from jax.sharding import PartitionSpec as P

PLANES = 64
ROW = ("z", "yl", "x")
CODE_ROWS = 8
CHUNKS = 4


def plane_coeffs():
    index = jnp.arange(PLANES).astype(jnp.float32)
    height = (index + 0.5) / PLANES
    azimuth = index * 2.399963229728653
    radius = jnp.sqrt(1.0 - height * height)
    normal_x = radius * jnp.cos(azimuth)
    normal_y = radius * jnp.sin(azimuth)
    return jnp.stack(
        [
            normal_x * normal_x,
            normal_y * normal_y,
            height * height,
            2.0 * normal_x * normal_y,
            2.0 * normal_y * height,
            2.0 * normal_x * height,
        ],
        axis=-1,
    )


def mode_table(rates, decays, steps):
    doublings = steps.bit_length() - 1
    shifts = 2.0 ** jnp.arange(doublings, dtype=jnp.float32)
    angle = rates[:, None] * shifts
    shrink = jnp.exp(-decays[:, None] * rates[:, None] * shifts)
    last = jnp.stack([rates * jnp.sin(rates), rates * jnp.cos(rates)], axis=-1)
    return jnp.concatenate([shrink * jnp.cos(angle), shrink * jnp.sin(angle), last], axis=-1)


def code_scale(code):
    return jnp.exp2(code * (1.0 / 32.0) - 15.0)


def quantize(values):
    largest = jnp.max(jnp.abs(values), axis=-1, keepdims=True)
    code = jnp.ceil(jnp.log2(jnp.maximum(largest, 1e-30)) * 32.0)
    inverse = jnp.exp2(15.0 - code * (1.0 / 32.0))
    whole = jnp.clip(jnp.round(values * inverse), -32767.0, 32767.0).astype(jnp.int32)
    return whole, code


def as_row(column):
    n = column.shape[0]
    at = lax.broadcasted_iota(jnp.int32, (n, 128), 0) == lax.broadcasted_iota(jnp.int32, (n, 128), 1)
    return jnp.sum(jnp.where(at, column, 0.0), axis=0, keepdims=True)


def history_kernel(window_ref, part_ref, table_ref, out_ref):
    forces = jnp.dot(part_ref[...], window_ref[...], preferred_element_type=jnp.float32)
    modes, steps = forces.shape
    doublings = steps.bit_length() - 1
    table = table_ref[...]
    lane = lax.broadcasted_iota(jnp.int32, forces.shape, 1)
    re, im = forces, jnp.zeros_like(forces)
    for d in range(doublings):
        shift = 1 << d
        p_re, p_im = table[:, d : d + 1], table[:, doublings + d : doublings + d + 1]
        keep = lane >= shift
        old_re = jnp.where(keep, pltpu.roll(re, shift, 1), 0.0)
        if d == 0:
            re, im = re + p_re * old_re, p_im * old_re
            continue
        old_im = jnp.where(keep, pltpu.roll(im, shift, 1), 0.0)
        re, im = re + p_re * old_re - p_im * old_im, im + p_re * old_im + p_im * old_re
    hist = table[:, 2 * doublings : 2 * doublings + 1] * re + table[:, 2 * doublings + 1 : 2 * doublings + 2] * im
    whole, code = quantize(hist)
    codes = jnp.broadcast_to(as_row(code), (CODE_ROWS, 128)).astype(jnp.int32)
    block = jnp.concatenate([whole, codes], axis=0).astype(jnp.int16)
    for i in range(out_ref.shape[0]):
        out_ref[i] = block


def make_history(window, participation, table, count):
    modes, channels = participation.shape
    steps = window.shape[1]
    return pl.pallas_call(
        history_kernel,
        out_shape=jax.ShapeDtypeStruct((count, modes + CODE_ROWS, steps), jnp.int16),
        in_specs=[pl.BlockSpec(memory_space=pltpu.VMEM)] * 3,
        out_specs=pl.BlockSpec(memory_space=pltpu.VMEM),
        compiler_params=pltpu.CompilerParams(vmem_limit_bytes=16 << 20),
        cost_estimate=pl.CostEstimate(
            flops=2 * modes * channels * steps, bytes_accessed=2 * (channels * (modes + steps)), transcendentals=0
        ),
        name="history",
    )(window, participation, table)


def recover_kernel(picks_ref, hist_ref, far_ref, out_ref, split_ref, coeff_ref, sems):
    chunks = sems.shape[0]
    per = coeff_ref.shape[0] // chunks
    fetches = [
        pltpu.make_async_copy(far_ref.at[pl.ds(i * per, per)], coeff_ref.at[pl.ds(i * per, per)], sems.at[i])
        for i in range(chunks)
    ]
    for fetch in fetches:
        fetch.start()
    sources, rows, steps = hist_ref.shape
    modes = rows - CODE_ROWS
    sub = lax.broadcasted_iota(jnp.int32, (8, 128), 0)
    tiles = []
    for base in range(0, sources, 8):
        tile = jnp.zeros((8, 128), jnp.int32)
        for i in range(8):
            codes = hist_ref[base + i, modes : modes + CODE_ROWS, :].astype(jnp.int32)[:8]
            tile = jnp.where(sub == i, codes, tile)
        tiles.append(tile)
    scales = code_scale(jnp.concatenate(tiles, axis=0).astype(jnp.float32))
    scales = jnp.concatenate([scales, jnp.zeros((128 - sources, 128), jnp.float32)], axis=0).T
    for s in range(sources):
        value = hist_ref[s, :modes, :].astype(jnp.int32).astype(jnp.float32) * scales[:modes, s : s + 1]
        high = value.astype(jnp.bfloat16)
        low = (value - high.astype(jnp.float32)).astype(jnp.bfloat16)
        split_ref[s * modes : (s + 1) * modes, :steps] = high
        split_ref[s * modes : (s + 1) * modes, steps:] = low
    blocks, picked, height, width = coeff_ref.shape
    slab = blocks // (2 * out_ref.shape[1])
    for b in range(blocks):
        if b % per == 0:
            fetches[b // per].wait()
        left = jnp.concatenate([coeff_ref[b, k] for k in range(picked)], axis=1)
        right = jnp.concatenate(
            [split_ref[pl.ds(pl.multiple_of(picks_ref[b, k] * width, width), width), :] for k in range(picked)], axis=0
        )
        both = jnp.dot(left, right, preferred_element_type=jnp.float32)
        owner = b // slab
        out_ref[owner % 2, owner // 2, (b % slab) * height : (b % slab + 1) * height, :] = both[:, :steps] + both[:, steps:]


def recover(hist, coeff_blocks, picks, groups):
    sources, rows, steps = hist.shape
    blocks, picked, height, width = coeff_blocks.shape
    return pl.pallas_call(
        recover_kernel,
        out_shape=jax.ShapeDtypeStruct((2, groups // 2, blocks // groups * height, steps), jnp.float32),
        in_specs=[
            pl.BlockSpec(memory_space=pltpu.SMEM),
            pl.BlockSpec(memory_space=pltpu.VMEM),
            pl.BlockSpec(memory_space=pltpu.HBM),
        ],
        out_specs=pl.BlockSpec(memory_space=pltpu.VMEM),
        scratch_shapes=[
            pltpu.VMEM((sources * (rows - CODE_ROWS), 2 * steps), jnp.bfloat16),
            pltpu.VMEM(coeff_blocks.shape, jnp.bfloat16),
            pltpu.SemaphoreType.DMA((CHUNKS,)),
        ],
        compiler_params=pltpu.CompilerParams(vmem_limit_bytes=50 << 20),
        cost_estimate=pl.CostEstimate(
            flops=4 * blocks * picked * height * width * steps,
            bytes_accessed=2 * blocks * picked * height * width,
            transcendentals=0,
        ),
        name="recover",
    )(picks, hist, coeff_blocks)


def pack_kernel(both_ref, out_ref):
    groups, rows, steps = out_ref.shape
    rows -= CODE_ROWS
    tiles = rows // 128
    at = lax.broadcasted_iota(jnp.int32, (128, 128), 0) == lax.broadcasted_iota(jnp.int32, (128, 128), 1)
    for g in range(groups):
        sums, largest = [], []
        for i in range(tiles):
            here = pl.ds(g * rows + i * 128, 128)
            pair = both_ref[0, here, :] + both_ref[1, here, :]
            top = jnp.max(jnp.abs(pair), axis=-1, keepdims=True)
            sums.append(pair)
            largest.append(jnp.sum(jnp.where(at, top, 0.0), axis=0, keepdims=True))
        largest.append(jnp.zeros((8 - tiles, 128), jnp.float32))
        code = jnp.ceil(jnp.log2(jnp.maximum(jnp.concatenate(largest, axis=0), 1e-30)) * 32.0)
        out_ref[g, rows:, :] = code.astype(jnp.int32).astype(jnp.int16)
        inverse = jnp.exp2(15.0 - code * (1.0 / 32.0))
        inverse = jnp.concatenate([inverse, jnp.zeros((120, 128), jnp.float32)], axis=0).T
        for i in range(tiles):
            whole = jnp.clip(jnp.round(sums[i] * inverse[:, i : i + 1]), -32767.0, 32767.0)
            out_ref[g, i * 128 : (i + 1) * 128, :] = whole.astype(jnp.int32).astype(jnp.int16)


def pack_sums(both, groups):
    rows, steps = both.shape[1:]
    return pl.pallas_call(
        pack_kernel,
        out_shape=jax.ShapeDtypeStruct((groups, rows // groups + CODE_ROWS, steps), jnp.int16),
        in_specs=[pl.BlockSpec(memory_space=pltpu.VMEM)],
        out_specs=pl.BlockSpec(memory_space=pltpu.VMEM),
        compiler_params=pltpu.CompilerParams(vmem_limit_bytes=16 << 20),
        name="pack",
    )(both)


def range_kernel(parts_ref, coeff_ref, stress_ref, range_ref):
    groups, rows, steps = parts_ref.shape
    rows -= CODE_ROWS
    codes = [parts_ref[g, rows:, :].astype(jnp.int32).astype(jnp.float32) for g in range(groups)]
    scales = code_scale(jnp.concatenate(codes, axis=0))
    scales = jnp.concatenate([scales, jnp.zeros((128 - groups * CODE_ROWS, 128), jnp.float32)], axis=0).T
    pieces = []
    for i in range(rows // 128):
        piece = None
        for g in range(groups):
            value = parts_ref[g, i * 128 : (i + 1) * 128, :].astype(jnp.int32).astype(jnp.float32)
            at = g * CODE_ROWS + i
            value = value * scales[:, at : at + 1]
            piece = value if piece is None else piece + value
        pieces.append(piece)
    components, elements, steps = stress_ref.shape
    stress = jnp.concatenate(pieces, axis=0).reshape(components, elements, steps)
    stress_ref[...] = stress
    looked = range_ref.shape[0]
    lane = lax.broadcasted_iota(jnp.int32, (elements, 128), 1)
    coeffs = coeff_ref[...]
    result = jnp.zeros((elements, 128), jnp.float32)
    for p in range(looked):
        normal = coeffs[:, p * components : p * components + 1] * stress[0]
        for q in range(1, components):
            at = p * components + q
            normal = normal + coeffs[:, at : at + 1] * stress[q]
        spread = jnp.max(normal, axis=-1, keepdims=True) - jnp.min(normal, axis=-1, keepdims=True)
        result = jnp.where(lane == p, spread, result)
    range_ref[...] = result.T[:looked, :]


def finish(parts, coeffs, looked):
    groups, rows, steps = parts.shape
    rows -= CODE_ROWS
    elements = coeffs.shape[0]
    stress, ranges = pl.pallas_call(
        range_kernel,
        out_shape=(
            jax.ShapeDtypeStruct((rows // elements, elements, steps), jnp.float32),
            jax.ShapeDtypeStruct((looked, elements), jnp.float32),
        ),
        in_specs=[pl.BlockSpec(memory_space=pltpu.VMEM)] * 2,
        out_specs=(pl.BlockSpec(memory_space=pltpu.VMEM),) * 2,
        compiler_params=pltpu.CompilerParams(vmem_limit_bytes=8 << 20),
        name="ranges",
    )(parts, coeffs)
    return stress, ranges.T


def gather_row(part, count):
    copies = jnp.broadcast_to(part[None], (count,) + part.shape)
    return lax.all_to_all(copies, ROW, 0, 0)


def fetch_window(windows, owner):
    channels, steps = windows.shape[1:]
    count = lax.axis_size(ROW)
    half = channels // 2
    mine = lax.dynamic_slice_in_dim(windows[0], lax.axis_index("core") * half, half, 0)
    offered = lax.all_to_all(mine.reshape(count, half // count, steps), ROW, 0, 0)
    piece = lax.dynamic_index_in_dim(offered, owner, 0, keepdims=False)
    whole_half = gather_row(piece, count).reshape(half, steps)
    return lax.all_gather(whole_half, "core", axis=0, tiled=True)


def sum_over_mode(by_core):
    both = lax.all_to_all(by_core, "core", 0, 0)
    groups, rows, steps = by_core.shape[1:]
    return lax.all_to_all(pack_sums(both.reshape(2, groups * rows, steps), groups), "yh", 0, 0)


def body(load_windows, owner_id, participation, frequency, damping, recovery, pattern, plane_table):
    steps = load_windows.shape[2]
    chosen_planes = plane_table[0, 0]
    elements, looked = chosen_planes.shape
    one_hot = (chosen_planes[..., None] == jnp.arange(PLANES)[None, None, :]).astype(jnp.float32)
    coeffs = jnp.einsum("elp,pq->elq", one_hot, plane_coeffs(), precision=lax.Precision.HIGHEST)
    coeffs = coeffs.reshape(elements, looked * 6)
    table = mode_table(frequency, damping, steps)
    window = fetch_window(load_windows, owner_id[0])
    copies = make_history(window, participation, table, lax.axis_size(ROW))
    hist = lax.all_to_all(copies, ROW, 0, 0)
    partial = recover(hist, recovery[0, 0], pattern[0, 0], lax.axis_size(("yh", "core")))
    parts = sum_over_mode(partial)
    stress, plane_range = finish(parts, coeffs, looked)
    return (stress[None, None], plane_range[None, None])


def solution(mesh):
    fine = Mesh(mesh.devices.reshape(4, 2, 8, 2, 4), ("yh", "core") + ROW)
    mode = ("yh", "core")
    placed = (
        P(ROW, None, None),
        P(),
        P(mode + ROW, None),
        P(mode + ROW),
        P(mode + ROW),
        P(mode, ROW, None, None, None, None),
        P(mode, ROW, None, None),
        P(ROW, mode, None, None),
    )
    return jax.shard_map(
        body,
        mesh=fine,
        in_specs=placed,
        out_specs=(P(ROW, mode, None, None, None), P(ROW, mode, None, None)),
        check_vma=False,
    )
```

```python
import jax
import jax.numpy as jnp
from jax import lax
from jax.experimental import pallas as pl
from jax.experimental.pallas import tpu as pltpu
from jax.sharding import Mesh
from jax.sharding import PartitionSpec as P

PLANES = 64
ROW = ("z", "yl", "x")
CODE_ROWS = 8
LEVELS = 32760.0
CHUNKS = 4


def plane_coeffs():
    index = jnp.arange(PLANES).astype(jnp.float32)
    height = (index + 0.5) / PLANES
    azimuth = index * 2.399963229728653
    radius = jnp.sqrt(1.0 - height * height)
    normal_x = radius * jnp.cos(azimuth)
    normal_y = radius * jnp.sin(azimuth)
    return jnp.stack(
        [
            normal_x * normal_x,
            normal_y * normal_y,
            height * height,
            2.0 * normal_x * normal_y,
            2.0 * normal_y * height,
            2.0 * normal_x * height,
        ],
        axis=-1,
    )


def mode_table(rates, decays, steps):
    doublings = steps.bit_length() - 1
    shifts = 2.0 ** jnp.arange(doublings, dtype=jnp.float32)
    angle = rates[:, None] * shifts
    shrink = jnp.exp(-decays[:, None] * rates[:, None] * shifts)
    last = jnp.stack([rates * jnp.sin(rates), rates * jnp.cos(rates)], axis=-1)
    return jnp.concatenate([shrink * jnp.cos(angle), shrink * jnp.sin(angle), last], axis=-1)


def code_scale(code):
    return jnp.exp2(code * (1.0 / 32.0)) * (1.0 / LEVELS)


def quantize(values):
    largest = jnp.max(jnp.abs(values), axis=-1, keepdims=True)
    code = jnp.ceil(jnp.log2(jnp.maximum(largest, 1e-30)) * 32.0)
    inverse = jnp.exp2(code * (-1.0 / 32.0)) * LEVELS
    whole = jnp.round(values * inverse).astype(jnp.int32)
    return whole, code


def as_row(column):
    n = column.shape[0]
    at = lax.broadcasted_iota(jnp.int32, (n, 128), 0) == lax.broadcasted_iota(jnp.int32, (n, 128), 1)
    return jnp.sum(jnp.where(at, column, 0.0), axis=0, keepdims=True)


def history_kernel(window_ref, part_ref, table_ref, out_ref):
    forces = jnp.dot(part_ref[...], window_ref[...], preferred_element_type=jnp.float32)
    modes, steps = forces.shape
    doublings = steps.bit_length() - 1
    table = table_ref[...]
    lane = lax.broadcasted_iota(jnp.int32, forces.shape, 1)
    re, im = forces, jnp.zeros_like(forces)
    for d in range(doublings):
        shift = 1 << d
        p_re, p_im = table[:, d : d + 1], table[:, doublings + d : doublings + d + 1]
        keep = lane >= shift
        old_re = jnp.where(keep, pltpu.roll(re, shift, 1), 0.0)
        if d == 0:
            re, im = re + p_re * old_re, p_im * old_re
            continue
        old_im = jnp.where(keep, pltpu.roll(im, shift, 1), 0.0)
        re, im = re + p_re * old_re - p_im * old_im, im + p_re * old_im + p_im * old_re
    hist = table[:, 2 * doublings : 2 * doublings + 1] * re + table[:, 2 * doublings + 1 : 2 * doublings + 2] * im
    whole, code = quantize(hist)
    codes = jnp.broadcast_to(as_row(code), (CODE_ROWS, 128)).astype(jnp.int32)
    block = jnp.concatenate([whole, codes], axis=0).astype(jnp.int16)
    for i in range(out_ref.shape[0]):
        out_ref[i] = block


def make_history(window, participation, table, count):
    modes, channels = participation.shape
    steps = window.shape[1]
    return pl.pallas_call(
        history_kernel,
        out_shape=jax.ShapeDtypeStruct((count, modes + CODE_ROWS, steps), jnp.int16),
        in_specs=[pl.BlockSpec(memory_space=pltpu.VMEM)] * 3,
        out_specs=pl.BlockSpec(memory_space=pltpu.VMEM),
        compiler_params=pltpu.CompilerParams(vmem_limit_bytes=16 << 20),
        cost_estimate=pl.CostEstimate(
            flops=2 * modes * channels * steps, bytes_accessed=2 * (channels * (modes + steps)), transcendentals=0
        ),
        name="history",
    )(window, participation, table)


def recover_kernel(picks_ref, hist_ref, far_ref, out_ref, split_ref, coeff_ref, sems):
    chunks = sems.shape[0]
    per = coeff_ref.shape[0] // chunks
    fetches = [
        pltpu.make_async_copy(far_ref.at[pl.ds(i * per, per)], coeff_ref.at[pl.ds(i * per, per)], sems.at[i])
        for i in range(chunks)
    ]
    for fetch in fetches:
        fetch.start()
    across, along, rows, steps = hist_ref.shape
    sources = across * along
    modes = rows - CODE_ROWS
    sub = lax.broadcasted_iota(jnp.int32, (8, 128), 0)
    tiles = []
    for base in range(0, sources, 8):
        tile = jnp.zeros((8, 128), jnp.int32)
        for i in range(8):
            codes = hist_ref[(base + i) % across, (base + i) // across, modes : modes + CODE_ROWS, :].astype(jnp.int32)[:8]
            tile = jnp.where(sub == i, codes, tile)
        tiles.append(tile)
    scales = code_scale(jnp.concatenate(tiles, axis=0).astype(jnp.float32))
    scales = jnp.concatenate([scales, jnp.zeros((128 - sources, 128), jnp.float32)], axis=0).T
    for s in range(sources):
        value = hist_ref[s % across, s // across, :modes, :].astype(jnp.int32).astype(jnp.float32) * scales[:modes, s : s + 1]
        high = value.astype(jnp.bfloat16)
        low = (value - high.astype(jnp.float32)).astype(jnp.bfloat16)
        split_ref[s * modes : (s + 1) * modes, :steps] = high
        split_ref[s * modes : (s + 1) * modes, steps:] = low
    blocks, picked, height, width = coeff_ref.shape
    slab = blocks // (2 * out_ref.shape[1])
    for b in range(blocks):
        if b % per == 0:
            fetches[b // per].wait()
        left = jnp.concatenate([coeff_ref[b, k] for k in range(picked)], axis=1)
        right = jnp.concatenate(
            [split_ref[pl.ds(pl.multiple_of(picks_ref[b, k] * width, width), width), :] for k in range(picked)], axis=0
        )
        both = jnp.dot(left, right, preferred_element_type=jnp.float32)
        owner = b // slab
        out_ref[owner % 2, owner // 2, (b % slab) * height : (b % slab + 1) * height, :] = both[:, :steps] + both[:, steps:]


def recover(hist, coeff_blocks, picks, groups):
    across, along, rows, steps = hist.shape
    sources = across * along
    blocks, picked, height, width = coeff_blocks.shape
    return pl.pallas_call(
        recover_kernel,
        out_shape=jax.ShapeDtypeStruct((2, groups // 2, blocks // groups * height, steps), jnp.float32),
        in_specs=[
            pl.BlockSpec(memory_space=pltpu.SMEM),
            pl.BlockSpec(memory_space=pltpu.VMEM),
            pl.BlockSpec(memory_space=pltpu.HBM),
        ],
        out_specs=pl.BlockSpec(memory_space=pltpu.VMEM),
        scratch_shapes=[
            pltpu.VMEM((sources * (rows - CODE_ROWS), 2 * steps), jnp.bfloat16),
            pltpu.VMEM(coeff_blocks.shape, jnp.bfloat16),
            pltpu.SemaphoreType.DMA((CHUNKS,)),
        ],
        compiler_params=pltpu.CompilerParams(vmem_limit_bytes=50 << 20),
        cost_estimate=pl.CostEstimate(
            flops=4 * blocks * picked * height * width * steps,
            bytes_accessed=2 * blocks * picked * height * width,
            transcendentals=0,
        ),
        name="recover",
    )(picks, hist, coeff_blocks)


def pack_kernel(both_ref, out_ref):
    groups, rows, steps = out_ref.shape
    rows -= CODE_ROWS
    tiles = rows // 128
    at = lax.broadcasted_iota(jnp.int32, (128, 128), 0) == lax.broadcasted_iota(jnp.int32, (128, 128), 1)
    for g in range(groups):
        sums, largest = [], []
        for i in range(tiles):
            here = pl.ds(g * rows + i * 128, 128)
            pair = both_ref[0, here, :] + both_ref[1, here, :]
            top = jnp.max(jnp.abs(pair), axis=-1, keepdims=True)
            sums.append(pair)
            largest.append(jnp.sum(jnp.where(at, top, 0.0), axis=0, keepdims=True))
        largest.append(jnp.zeros((8 - tiles, 128), jnp.float32))
        code = jnp.ceil(jnp.log2(jnp.maximum(jnp.concatenate(largest, axis=0), 1e-30)) * 32.0)
        out_ref[g, rows:, :] = code.astype(jnp.int32).astype(jnp.int16)
        inverse = jnp.exp2(code * (-1.0 / 32.0)) * LEVELS
        inverse = jnp.concatenate([inverse, jnp.zeros((120, 128), jnp.float32)], axis=0).T
        for i in range(tiles):
            whole = jnp.round(sums[i] * inverse[:, i : i + 1])
            out_ref[g, i * 128 : (i + 1) * 128, :] = whole.astype(jnp.int32).astype(jnp.int16)


def pack_sums(both, groups):
    rows, steps = both.shape[1:]
    return pl.pallas_call(
        pack_kernel,
        out_shape=jax.ShapeDtypeStruct((groups, rows // groups + CODE_ROWS, steps), jnp.int16),
        in_specs=[pl.BlockSpec(memory_space=pltpu.VMEM)],
        out_specs=pl.BlockSpec(memory_space=pltpu.VMEM),
        compiler_params=pltpu.CompilerParams(vmem_limit_bytes=16 << 20),
        name="pack",
    )(both)


def range_kernel(parts_ref, coeff_ref, stress_ref, range_ref):
    groups, rows, steps = parts_ref.shape
    rows -= CODE_ROWS
    codes = [parts_ref[g, rows:, :].astype(jnp.int32).astype(jnp.float32) for g in range(groups)]
    scales = code_scale(jnp.concatenate(codes, axis=0))
    scales = jnp.concatenate([scales, jnp.zeros((128 - groups * CODE_ROWS, 128), jnp.float32)], axis=0).T
    pieces = []
    for i in range(rows // 128):
        piece = None
        for g in range(groups):
            value = parts_ref[g, i * 128 : (i + 1) * 128, :].astype(jnp.int32).astype(jnp.float32)
            at = g * CODE_ROWS + i
            value = value * scales[:, at : at + 1]
            piece = value if piece is None else piece + value
        pieces.append(piece)
    components, elements, steps = stress_ref.shape
    stress = jnp.concatenate(pieces, axis=0).reshape(components, elements, steps)
    stress_ref[...] = stress
    looked = range_ref.shape[0]
    lane = lax.broadcasted_iota(jnp.int32, (elements, 128), 1)
    coeffs = coeff_ref[...]
    result = jnp.zeros((elements, 128), jnp.float32)
    for p in range(looked):
        normal = coeffs[:, p * components : p * components + 1] * stress[0]
        for q in range(1, components):
            at = p * components + q
            normal = normal + coeffs[:, at : at + 1] * stress[q]
        spread = jnp.max(normal, axis=-1, keepdims=True) - jnp.min(normal, axis=-1, keepdims=True)
        result = jnp.where(lane == p, spread, result)
    range_ref[...] = result.T[:looked, :]


def finish(parts, coeffs, looked):
    groups, rows, steps = parts.shape
    rows -= CODE_ROWS
    elements = coeffs.shape[0]
    stress, ranges = pl.pallas_call(
        range_kernel,
        out_shape=(
            jax.ShapeDtypeStruct((rows // elements, elements, steps), jnp.float32),
            jax.ShapeDtypeStruct((looked, elements), jnp.float32),
        ),
        in_specs=[pl.BlockSpec(memory_space=pltpu.VMEM)] * 2,
        out_specs=(pl.BlockSpec(memory_space=pltpu.VMEM),) * 2,
        compiler_params=pltpu.CompilerParams(vmem_limit_bytes=8 << 20),
        name="ranges",
    )(parts, coeffs)
    return stress, ranges.T


def gather_over(part, axes):
    copies = jnp.broadcast_to(part[None], (lax.axis_size(axes),) + part.shape)
    return lax.all_to_all(copies, axes, 0, 0)


def fetch_window(windows, owner):
    channels, steps = windows.shape[1:]
    count = lax.axis_size(ROW)
    half = channels // 2
    mine = lax.dynamic_slice_in_dim(windows[0], lax.axis_index("core") * half, half, 0)
    offered = lax.all_to_all(mine.reshape(count, half // count, steps), ROW, 0, 0)
    piece = lax.dynamic_index_in_dim(offered, owner, 0, keepdims=False)
    whole_half = gather_over(piece, ROW).reshape(half, steps)
    return lax.all_gather(whole_half, "core", axis=0, tiled=True)


def sum_over_mode(by_core):
    both = lax.all_to_all(by_core, "core", 0, 0)
    groups, rows, steps = by_core.shape[1:]
    return lax.all_to_all(pack_sums(both.reshape(2, groups * rows, steps), groups), "yh", 0, 0)


def body(load_windows, owner_id, participation, frequency, damping, recovery, pattern, plane_table):
    steps = load_windows.shape[2]
    chosen_planes = plane_table[0, 0]
    elements, looked = chosen_planes.shape
    one_hot = (chosen_planes[..., None] == jnp.arange(PLANES)[None, None, :]).astype(jnp.float32)
    coeffs = jnp.einsum("elp,pq->elq", one_hot, plane_coeffs(), precision=lax.Precision.HIGHEST)
    coeffs = coeffs.reshape(elements, looked * 6)
    table = mode_table(frequency, damping, steps)
    window = fetch_window(load_windows, owner_id[0])
    copies = make_history(window, participation, table, lax.axis_size(ROW[:2]))
    column = lax.all_to_all(copies, ROW[:2], 0, 0)
    hist = gather_over(column, ROW[2])
    partial = recover(hist, recovery[0, 0], pattern[0, 0], lax.axis_size(("yh", "core")))
    parts = sum_over_mode(partial)
    stress, plane_range = finish(parts, coeffs, looked)
    return (stress[None, None], plane_range[None, None])


def solution(mesh):
    fine = Mesh(mesh.devices.reshape(4, 2, 8, 2, 4), ("yh", "core") + ROW)
    mode = ("yh", "core")
    placed = (
        P(ROW, None, None),
        P(),
        P(mode + ROW, None),
        P(mode + ROW),
        P(mode + ROW),
        P(mode, ROW, None, None, None, None),
        P(mode, ROW, None, None),
        P(ROW, mode, None, None),
    )
    return jax.shard_map(
        body,
        mesh=fine,
        in_specs=placed,
        out_specs=(P(ROW, mode, None, None, None), P(ROW, mode, None, None)),
        check_vma=False,
    )
```

```python
import jax
import jax.numpy as jnp
from jax import lax
from jax.experimental import pallas as pl
from jax.experimental.pallas import tpu as pltpu
from jax.sharding import Mesh
from jax.sharding import PartitionSpec as P

ROW = ("z", "yl", "x")
CODE_ROWS = 8
LEVELS = 32760.0
PLANES = 64


def code_scale(code):
    return jnp.exp2(code * (1.0 / 32.0)) * (1.0 / LEVELS)


def quantize(values):
    largest = jnp.max(jnp.abs(values), axis=-1, keepdims=True)
    code = jnp.ceil(jnp.log2(jnp.maximum(largest, 1e-30)) * 32.0)
    inverse = jnp.exp2(code * (-1.0 / 32.0)) * LEVELS
    whole = jnp.round(values * inverse).astype(jnp.int32)
    return whole, code


def as_row(column):
    n = column.shape[0]
    at = lax.broadcasted_iota(jnp.int32, (n, 128), 0) == lax.broadcasted_iota(jnp.int32, (n, 128), 1)
    return jnp.sum(jnp.where(at, column, 0.0), axis=0, keepdims=True)


def mode_table(rates, decays, rows_ref):
    modes = rates.shape[1]
    shifts = (1 << lax.broadcasted_iota(jnp.int32, (8, modes), 0)).astype(jnp.float32)
    angle = rates * shifts
    cos, sin = jnp.cos(angle), jnp.sin(angle)
    shrink = jnp.exp(-decays * rates * shifts)
    rows_ref[0:8, :modes] = shrink * cos
    rows_ref[8:16, :modes] = shrink * sin
    rows_ref[16:24, :modes] = rates * jnp.broadcast_to(sin[0:1], (8, modes))
    rows_ref[24:32, :modes] = rates * jnp.broadcast_to(cos[0:1], (8, modes))
    return rows_ref[...].T[:modes]


def history_kernel(window_ref, part_ref, rate_ref, decay_ref, out_ref, rows_ref):
    forces = jnp.dot(part_ref[...], window_ref[...], preferred_element_type=jnp.float32)
    modes, steps = forces.shape
    doublings = steps.bit_length() - 1
    table = mode_table(rate_ref[...], decay_ref[...], rows_ref)
    lane = lax.broadcasted_iota(jnp.int32, forces.shape, 1)
    re, im = forces, jnp.zeros_like(forces)
    for d in range(doublings):
        shift = 1 << d
        p_re, p_im = table[:, d : d + 1], table[:, 8 + d : 9 + d]
        keep = lane >= shift
        old_re = jnp.where(keep, pltpu.roll(re, shift, 1), 0.0)
        if d == 0:
            re, im = re + p_re * old_re, p_im * old_re
            continue
        old_im = jnp.where(keep, pltpu.roll(im, shift, 1), 0.0)
        re, im = re + p_re * old_re - p_im * old_im, im + p_re * old_im + p_im * old_re
    hist = table[:, 16:17] * re + table[:, 24:25] * im
    whole, code = quantize(hist)
    codes = jnp.broadcast_to(as_row(code), (CODE_ROWS, 128)).astype(jnp.int32)
    block = jnp.concatenate([whole, codes], axis=0).astype(jnp.int16)
    for i in range(out_ref.shape[0]):
        out_ref[i] = block


def make_history(window, participation, frequency, damping, count):
    modes, channels = participation.shape
    steps = window.shape[1]
    return pl.pallas_call(
        history_kernel,
        out_shape=jax.ShapeDtypeStruct((count, modes + CODE_ROWS, steps), jnp.int16),
        in_specs=[pl.BlockSpec(memory_space=pltpu.VMEM)] * 4,
        out_specs=pl.BlockSpec(memory_space=pltpu.VMEM),
        scratch_shapes=[pltpu.VMEM((128, 128), jnp.float32)],
        compiler_params=pltpu.CompilerParams(vmem_limit_bytes=16 << 20),
        cost_estimate=pl.CostEstimate(
            flops=2 * modes * channels * steps, bytes_accessed=2 * (channels * (modes + steps)), transcendentals=0
        ),
        name="history",
    )(window, participation, frequency, damping)


def recover_kernel(picks_ref, core_ref, hist_ref, far_ref, own_ref, other_ref, split_ref, coeff_ref, sems):
    fetches = [[], []]
    for i, side in enumerate([1 - core_ref[0], core_ref[0]]):
        for g in range(coeff_ref.shape[0] // 2):
            slab = 2 * g + side
            fetch = pltpu.make_async_copy(far_ref.at[slab], coeff_ref.at[slab], sems.at[i, g])
            fetch.start()
            fetches[i].append(fetch)
    across, along, rows, steps = hist_ref.shape
    sources = across * along
    modes = rows - CODE_ROWS
    sub = lax.broadcasted_iota(jnp.int32, (8, 128), 0)
    tiles = []
    for base in range(0, sources, 8):
        tile = jnp.zeros((8, 128), jnp.int32)
        for i in range(8):
            codes = hist_ref[(base + i) % across, (base + i) // across, modes : modes + CODE_ROWS, :].astype(jnp.int32)[:8]
            tile = jnp.where(sub == i, codes, tile)
        tiles.append(tile)
    scales = code_scale(jnp.concatenate(tiles, axis=0).astype(jnp.float32))
    scales = jnp.concatenate([scales, jnp.zeros((128 - sources, 128), jnp.float32)], axis=0).T
    for s in range(sources):
        value = hist_ref[s % across, s // across, :modes, :].astype(jnp.int32).astype(jnp.float32) * scales[:modes, s : s + 1]
        high = value.astype(jnp.bfloat16)
        low = (value - high.astype(jnp.float32)).astype(jnp.bfloat16)
        split_ref[s * modes : (s + 1) * modes, :steps] = high
        split_ref[s * modes : (s + 1) * modes, steps:] = low
    slabs, per_slab, picked, height, width = coeff_ref.shape
    core = core_ref[0]
    for i, (ref, side) in enumerate([(other_ref, 1 - core), (own_ref, core)]):
        for g in range(slabs // 2):
            slab = 2 * g + side
            fetches[i][g].wait()
            for r in range(per_slab):
                left = jnp.concatenate([coeff_ref[slab, r, k] for k in range(picked)], axis=1)
                starts = [pl.multiple_of(picks_ref[k, slab * per_slab + r] * width, width) for k in range(picked)]
                right = jnp.concatenate([split_ref[pl.ds(start, width), :] for start in starts], axis=0)
                both = jnp.dot(left, right, preferred_element_type=jnp.float32)
                ref[g, r * height : (r + 1) * height, :] = both[:, :steps] + both[:, steps:]


def recover(hist, coeff_blocks, picks, core, groups):
    across, along, rows, steps = hist.shape
    blocks, picked, height, width = coeff_blocks.shape
    slabs = coeff_blocks.reshape(groups, blocks // groups, picked, height, width)
    half = jax.ShapeDtypeStruct((groups // 2, blocks // groups * height, steps), jnp.float32)
    return pl.pallas_call(
        recover_kernel,
        out_shape=(half, half),
        in_specs=[
            pl.BlockSpec(memory_space=pltpu.SMEM),
            pl.BlockSpec(memory_space=pltpu.SMEM),
            pl.BlockSpec(memory_space=pltpu.VMEM),
            pl.BlockSpec(memory_space=pl.ANY),
        ],
        out_specs=(pl.BlockSpec(memory_space=pltpu.VMEM),) * 2,
        scratch_shapes=[
            pltpu.VMEM((across * along * (rows - CODE_ROWS), 2 * steps), jnp.bfloat16),
            pltpu.VMEM(slabs.shape, jnp.bfloat16),
            pltpu.SemaphoreType.DMA((2, groups // 2)),
        ],
        compiler_params=pltpu.CompilerParams(vmem_limit_bytes=24 << 20),
        cost_estimate=pl.CostEstimate(
            flops=4 * blocks * picked * height * width * steps,
            bytes_accessed=2 * blocks * picked * height * width,
            transcendentals=0,
        ),
        name="recover",
    )(picks, core, hist, pltpu.with_memory_space_constraint(slabs, pltpu.HBM))


def pack_kernel(own_ref, come_ref, out_ref):
    groups, rows, steps = out_ref.shape
    rows -= CODE_ROWS
    tiles = rows // 128
    at = lax.broadcasted_iota(jnp.int32, (128, 128), 0) == lax.broadcasted_iota(jnp.int32, (128, 128), 1)
    for g in range(groups):
        sums, largest = [], []
        for i in range(tiles):
            here = pl.ds(i * 128, 128)
            pair = own_ref[g, here, :] + come_ref[g, here, :]
            top = jnp.max(jnp.abs(pair), axis=-1, keepdims=True)
            sums.append(pair)
            largest.append(jnp.sum(jnp.where(at, top, 0.0), axis=0, keepdims=True))
        largest.append(jnp.zeros((8 - tiles, 128), jnp.float32))
        code = jnp.ceil(jnp.log2(jnp.maximum(jnp.concatenate(largest, axis=0), 1e-30)) * 32.0)
        out_ref[g, rows:, :] = code.astype(jnp.int32).astype(jnp.int16)
        inverse = jnp.exp2(code * (-1.0 / 32.0)) * LEVELS
        inverse = jnp.concatenate([inverse, jnp.zeros((120, 128), jnp.float32)], axis=0).T
        for i in range(tiles):
            whole = jnp.round(sums[i] * inverse[:, i : i + 1])
            out_ref[g, i * 128 : (i + 1) * 128, :] = whole.astype(jnp.int32).astype(jnp.int16)


def pack_sums(own, come):
    groups, rows, steps = own.shape
    return pl.pallas_call(
        pack_kernel,
        out_shape=jax.ShapeDtypeStruct((groups, rows + CODE_ROWS, steps), jnp.int16),
        in_specs=[pl.BlockSpec(memory_space=pltpu.VMEM)] * 2,
        out_specs=pl.BlockSpec(memory_space=pltpu.VMEM),
        compiler_params=pltpu.CompilerParams(vmem_limit_bytes=16 << 20),
        name="pack",
    )(own, come)


def plane_columns(planes, rows_ref):
    looked, elements = planes.shape
    index = planes.astype(jnp.float32)
    height = (index + 0.5) * (1.0 / PLANES)
    azimuth = index * 2.399963229728653
    radius = jnp.sqrt(1.0 - height * height)
    normal_x = radius * jnp.cos(azimuth)
    normal_y = radius * jnp.sin(azimuth)
    coeffs = [
        normal_x * normal_x,
        normal_y * normal_y,
        height * height,
        2.0 * normal_x * normal_y,
        2.0 * normal_y * height,
        2.0 * normal_x * height,
    ]
    for q, coeff in enumerate(coeffs):
        rows_ref[q * looked : (q + 1) * looked, :elements] = coeff
    return rows_ref[...].T[:elements]


def range_kernel(parts_ref, plane_ref, stress_ref, range_ref, rows_ref):
    groups, rows, steps = parts_ref.shape
    rows -= CODE_ROWS
    codes = [parts_ref[g, rows:, :].astype(jnp.int32).astype(jnp.float32) for g in range(groups)]
    scales = code_scale(jnp.concatenate(codes, axis=0))
    scales = jnp.concatenate([scales, jnp.zeros((128 - groups * CODE_ROWS, 128), jnp.float32)], axis=0).T
    pieces = []
    for i in range(rows // 128):
        piece = None
        for g in range(groups):
            value = parts_ref[g, i * 128 : (i + 1) * 128, :].astype(jnp.int32).astype(jnp.float32)
            at = g * CODE_ROWS + i
            value = value * scales[:, at : at + 1]
            piece = value if piece is None else piece + value
        pieces.append(piece)
    components, elements, steps = stress_ref.shape
    stress = jnp.concatenate(pieces, axis=0).reshape(components, elements, steps)
    stress_ref[...] = stress
    looked = range_ref.shape[0]
    lane = lax.broadcasted_iota(jnp.int32, (elements, 128), 1)
    coeffs = plane_columns(plane_ref[...], rows_ref)
    result = jnp.zeros((elements, 128), jnp.float32)
    for p in range(looked):
        normal = coeffs[:, p : p + 1] * stress[0]
        for q in range(1, components):
            at = q * looked + p
            normal = normal + coeffs[:, at : at + 1] * stress[q]
        spread = jnp.max(normal, axis=-1, keepdims=True) - jnp.min(normal, axis=-1, keepdims=True)
        result = jnp.where(lane == p, spread, result)
    range_ref[...] = result.T[:looked, :]


def finish(parts, planes):
    groups, rows, steps = parts.shape
    rows -= CODE_ROWS
    looked, elements = planes.shape
    stress, ranges = pl.pallas_call(
        range_kernel,
        out_shape=(
            jax.ShapeDtypeStruct((rows // elements, elements, steps), jnp.float32),
            jax.ShapeDtypeStruct((looked, elements), jnp.float32),
        ),
        in_specs=[pl.BlockSpec(memory_space=pltpu.VMEM)] * 2,
        out_specs=(pl.BlockSpec(memory_space=pltpu.VMEM),) * 2,
        scratch_shapes=[pltpu.VMEM((128, 128), jnp.float32)],
        compiler_params=pltpu.CompilerParams(vmem_limit_bytes=8 << 20),
        name="ranges",
    )(parts, planes)
    return stress, ranges.T


def gather_over(part, axes):
    copies = jnp.broadcast_to(part[None], (lax.axis_size(axes),) + part.shape)
    return lax.all_to_all(copies, axes, 0, 0)


def stage_kernel(core_ref, owner_ref, whole_ref, *refs):
    count = (len(refs) - 3) // 2
    far, (half_ref, *near, same_ref, sems) = refs[:count], refs[count:]
    rows = half_ref.shape[0]
    start = pl.multiple_of(core_ref[0] * rows, rows)
    fetches = [pltpu.make_async_copy(whole_ref.at[pl.ds(start, rows)], half_ref, sems.at[count])]
    fetches += [pltpu.make_async_copy(a, b, sems.at[i]) for i, (a, b) in enumerate(zip(far, near))]
    for fetch in fetches:
        fetch.start()
    same_ref[0] = owner_ref[0]
    for fetch in fetches:
        fetch.wait()


def stage(whole, core, owner, *others):
    channels, steps = whole.shape
    copied = [jax.ShapeDtypeStruct((channels // 2, steps), whole.dtype)]
    copied += [jax.ShapeDtypeStruct(x.shape, x.dtype) for x in others]
    return pl.pallas_call(
        stage_kernel,
        out_shape=(*copied, jax.ShapeDtypeStruct(owner.shape, owner.dtype)),
        in_specs=[pl.BlockSpec(memory_space=pltpu.SMEM)] * 2 + [pl.BlockSpec(memory_space=pl.ANY)] * len(copied),
        out_specs=(pl.BlockSpec(memory_space=pltpu.VMEM),) * len(copied) + (pl.BlockSpec(memory_space=pltpu.SMEM),),
        scratch_shapes=[pltpu.SemaphoreType.DMA((len(copied),))],
        compiler_params=pltpu.CompilerParams(vmem_limit_bytes=8 << 20),
        name="stage",
    )(core, owner, *(pltpu.with_memory_space_constraint(x, pltpu.HBM) for x in (whole, *others)))


def pick_kernel(owner_ref, offered_ref, out_ref):
    piece = offered_ref[owner_ref[0]]
    for i in range(out_ref.shape[0]):
        out_ref[i] = piece


def pick_piece(offered, owner):
    return pl.pallas_call(
        pick_kernel,
        out_shape=jax.ShapeDtypeStruct(offered.shape, offered.dtype),
        in_specs=[pl.BlockSpec(memory_space=pltpu.SMEM), pl.BlockSpec(memory_space=pltpu.VMEM)],
        out_specs=pl.BlockSpec(memory_space=pltpu.VMEM),
        compiler_params=pltpu.CompilerParams(vmem_limit_bytes=8 << 20),
        name="pick",
    )(owner, offered)


def fetch_window(half, owner):
    count = lax.axis_size(ROW)
    pieces = half.reshape(count, half.shape[0] // count, half.shape[1])
    offered = lax.all_to_all(pieces, ROW, 0, 0)
    whole_half = lax.all_to_all(pick_piece(offered, owner), ROW, 0, 0).reshape(half.shape)
    return lax.all_gather(whole_half, "core", axis=0, tiled=True)


def body(load_windows, owner_id, participation, frequency, damping, recovery, pattern, plane_table):
    core = lax.axis_index("core")[None].astype(jnp.int32)
    half, part, rates, decays, owner = stage(
        load_windows[0], core, owner_id, participation, frequency[None], damping[None]
    )
    window = fetch_window(half, owner)
    copies = make_history(window, part, rates, decays, lax.axis_size(ROW[:2]))
    column = lax.all_to_all(copies, ROW[:2], 0, 0)
    hist = gather_over(column, ROW[2])
    own, other = recover(hist, recovery[0, 0], pattern[0, 0].T, core, lax.axis_size(("yh", "core")))
    come = lax.ppermute(other, "core", [(0, 1), (1, 0)])
    parts = lax.all_to_all(pack_sums(own, come), "yh", 0, 0)
    stress, plane_range = finish(parts, plane_table[0, 0].T)
    return (stress[None, None], plane_range[None, None])


def solution(mesh):
    fine = Mesh(mesh.devices.reshape(4, 2, 8, 2, 4), ("yh", "core") + ROW)
    mode = ("yh", "core")
    placed = (
        P(ROW, None, None),
        P(),
        P(mode + ROW, None),
        P(mode + ROW),
        P(mode + ROW),
        P(mode, ROW, None, None, None, None),
        P(mode, ROW, None, None),
        P(ROW, mode, None, None),
    )
    return jax.shard_map(
        body,
        mesh=fine,
        in_specs=placed,
        out_specs=(P(ROW, mode, None, None, None), P(ROW, mode, None, None)),
        check_vma=False,
    )
```

```python
import jax
import jax.numpy as jnp
from jax import lax
from jax.experimental import pallas as pl
from jax.experimental.pallas import tpu as pltpu
from jax.sharding import Mesh
from jax.sharding import PartitionSpec as P

ROW = ("z", "yl", "x")
CODE_ROWS = 8
LEVELS = 32760.0
PLANES = 64


def code_scale(code):
    return jnp.exp2(code * (1.0 / 32.0)) * (1.0 / LEVELS)


def quantize(values):
    largest = jnp.max(jnp.abs(values), axis=-1, keepdims=True)
    code = jnp.ceil(jnp.log2(jnp.maximum(largest, 1e-30)) * 32.0)
    inverse = jnp.exp2(code * (-1.0 / 32.0)) * LEVELS
    whole = jnp.round(values * inverse).astype(jnp.int32)
    return whole, code


def as_row(column):
    n = column.shape[0]
    at = lax.broadcasted_iota(jnp.int32, (n, 128), 0) == lax.broadcasted_iota(jnp.int32, (n, 128), 1)
    return jnp.sum(jnp.where(at, column, 0.0), axis=0, keepdims=True)


def mode_table(rates, decays, rows_ref):
    modes = rates.shape[1]
    shifts = (1 << lax.broadcasted_iota(jnp.int32, (8, modes), 0)).astype(jnp.float32)
    angle = rates * shifts
    cos, sin = jnp.cos(angle), jnp.sin(angle)
    shrink = jnp.exp(-decays * rates * shifts)
    rows_ref[0:8, :modes] = shrink * cos
    rows_ref[8:16, :modes] = shrink * sin
    rows_ref[16:24, :modes] = rates * jnp.broadcast_to(sin[0:1], (8, modes))
    rows_ref[24:32, :modes] = rates * jnp.broadcast_to(cos[0:1], (8, modes))
    return rows_ref[...].T[:modes]


def history_kernel(window_ref, part_ref, rate_ref, decay_ref, out_ref, rows_ref):
    forces = jnp.dot(part_ref[...], window_ref[...], preferred_element_type=jnp.float32)
    modes, steps = forces.shape
    doublings = steps.bit_length() - 1
    table = mode_table(rate_ref[...], decay_ref[...], rows_ref)
    lane = lax.broadcasted_iota(jnp.int32, forces.shape, 1)
    re, im = forces, jnp.zeros_like(forces)
    for d in range(doublings):
        shift = 1 << d
        p_re, p_im = table[:, d : d + 1], table[:, 8 + d : 9 + d]
        keep = lane >= shift
        old_re = jnp.where(keep, pltpu.roll(re, shift, 1), 0.0)
        if d == 0:
            re, im = re + p_re * old_re, p_im * old_re
            continue
        old_im = jnp.where(keep, pltpu.roll(im, shift, 1), 0.0)
        re, im = re + p_re * old_re - p_im * old_im, im + p_re * old_im + p_im * old_re
    hist = table[:, 16:17] * re + table[:, 24:25] * im
    whole, code = quantize(hist)
    codes = jnp.broadcast_to(as_row(code), (CODE_ROWS, 128)).astype(jnp.int32)
    block = jnp.concatenate([whole, codes], axis=0).astype(jnp.int16)
    for i in range(out_ref.shape[0]):
        out_ref[i] = block


def make_history(window, participation, frequency, damping, count):
    modes, channels = participation.shape
    steps = window.shape[1]
    return pl.pallas_call(
        history_kernel,
        out_shape=jax.ShapeDtypeStruct((count, modes + CODE_ROWS, steps), jnp.int16),
        in_specs=[pl.BlockSpec(memory_space=pltpu.VMEM)] * 4,
        out_specs=pl.BlockSpec(memory_space=pltpu.VMEM),
        scratch_shapes=[pltpu.VMEM((128, 128), jnp.float32)],
        compiler_params=pltpu.CompilerParams(vmem_limit_bytes=16 << 20),
        cost_estimate=pl.CostEstimate(
            flops=2 * modes * channels * steps, bytes_accessed=2 * (channels * (modes + steps)), transcendentals=0
        ),
        name="history",
    )(window, participation, frequency, damping)


def product(picks_ref, side, coeff_ref, split_ref, out_ref, fetches):
    groups, per_slab, picked, height, width = coeff_ref.shape
    steps = out_ref.shape[2]
    for g in range(groups):
        if fetches:
            fetches[g].wait()
        for r in range(per_slab):
            block = (2 * g + side) * per_slab + r
            left = jnp.concatenate([coeff_ref[g, r, k] for k in range(picked)], axis=1)
            starts = [pl.multiple_of(picks_ref[k, block] * width, width) for k in range(picked)]
            right = jnp.concatenate([split_ref[pl.ds(start, width), :] for start in starts], axis=0)
            both = jnp.dot(left, right, preferred_element_type=jnp.float32)
            out_ref[g, r * height : (r + 1) * height, :] = both[:, :steps] + both[:, steps:]


def first_kernel(hist_ref, picks_far, far_ref, other_ref, split_ref, mine_ref, theirs_ref, picks_ref, sems, picks_sem):
    core = lax.axis_index("core")
    groups = mine_ref.shape[0]
    fetches = [[], []]
    fetch_picks = pltpu.make_async_copy(picks_far, picks_ref, picks_sem)
    fetch_picks.start()
    for i, (near, side) in enumerate([(theirs_ref, 1 - core), (mine_ref, core)]):
        for g in range(groups):
            fetch = pltpu.make_async_copy(far_ref.at[2 * g + side], near.at[g], sems.at[i, g])
            fetch.start()
            fetches[i].append(fetch)
    across, along, rows, steps = hist_ref.shape
    sources = across * along
    modes = rows - CODE_ROWS
    sub = lax.broadcasted_iota(jnp.int32, (8, 128), 0)
    tiles = []
    for base in range(0, sources, 8):
        tile = jnp.zeros((8, 128), jnp.int32)
        for i in range(8):
            s = base + i
            codes = hist_ref[s % across, s // across, modes : modes + CODE_ROWS, :].astype(jnp.int32)[:8]
            tile = jnp.where(sub == i, codes, tile)
        tiles.append(tile)
    scales = code_scale(jnp.concatenate(tiles, axis=0).astype(jnp.float32))
    scales = jnp.concatenate([scales, jnp.zeros((128 - sources, 128), jnp.float32)], axis=0).T
    for s in range(sources):
        value = hist_ref[s % across, s // across, :modes, :].astype(jnp.int32).astype(jnp.float32)
        value = value * scales[:modes, s : s + 1]
        high = value.astype(jnp.bfloat16)
        low = (value - high.astype(jnp.float32)).astype(jnp.bfloat16)
        split_ref[s * modes : (s + 1) * modes, :steps] = high
        split_ref[s * modes : (s + 1) * modes, steps:] = low
    fetch_picks.wait()
    product(picks_ref, 1 - core, theirs_ref, split_ref, other_ref, fetches[0])
    for fetch in fetches[1]:
        fetch.wait()


def second_kernel(split_ref, mine_ref, plane_ref, picks_far, own_ref, coeffs_ref, picks_ref, rows_ref, picks_sem):
    fetch_picks = pltpu.make_async_copy(picks_far, picks_ref, picks_sem)
    fetch_picks.start()
    coeffs_ref[...] = plane_columns(plane_ref[...], rows_ref)
    fetch_picks.wait()
    product(picks_ref, lax.axis_index("core"), mine_ref, split_ref, own_ref, [])


def far(x):
    return pltpu.with_memory_space_constraint(x, pltpu.HBM)


def recover(hist, coeff_blocks, picks, planes, groups):
    across, along, rows, steps = hist.shape
    blocks, picked, height, width = coeff_blocks.shape
    slabs = coeff_blocks.reshape(groups, blocks // groups, picked, height, width)
    half = jax.ShapeDtypeStruct((groups // 2, blocks // groups * height, steps), jnp.float32)
    half_slabs = (groups // 2,) + slabs.shape[1:]
    cost = pl.CostEstimate(
        flops=2 * blocks * picked * height * width * steps,
        bytes_accessed=blocks * picked * height * width,
        transcendentals=0,
    )
    near, away = pl.BlockSpec(memory_space=pltpu.VMEM), pl.BlockSpec(memory_space=pl.ANY)
    scratch = [pltpu.SMEM(picks.shape, picks.dtype)]
    other, split, mine = pl.pallas_call(
        first_kernel,
        out_shape=(
            half,
            jax.ShapeDtypeStruct((across * along * (rows - CODE_ROWS), 2 * steps), jnp.bfloat16),
            jax.ShapeDtypeStruct(half_slabs, slabs.dtype),
        ),
        in_specs=[near, away, away],
        out_specs=(near,) * 3,
        scratch_shapes=[pltpu.VMEM(half_slabs, slabs.dtype)]
        + scratch
        + [pltpu.SemaphoreType.DMA((2, groups // 2)), pltpu.SemaphoreType.DMA],
        compiler_params=pltpu.CompilerParams(vmem_limit_bytes=24 << 20),
        cost_estimate=cost,
        name="first",
    )(hist, far(picks), far(slabs))
    come = lax.ppermute(other, "core", [(0, 1), (1, 0)])
    own, coeffs = pl.pallas_call(
        second_kernel,
        out_shape=(half, jax.ShapeDtypeStruct((planes.shape[1], 128), jnp.float32)),
        in_specs=[near, near, near, away],
        out_specs=(near,) * 2,
        scratch_shapes=scratch + [pltpu.VMEM((128, 128), jnp.float32), pltpu.SemaphoreType.DMA],
        compiler_params=pltpu.CompilerParams(vmem_limit_bytes=24 << 20),
        cost_estimate=cost,
        name="second",
    )(split, mine, planes, far(picks))
    return own, come, coeffs


def pack_kernel(own_ref, come_ref, out_ref):
    groups, rows, steps = out_ref.shape
    rows -= CODE_ROWS
    tiles = rows // 128
    at = lax.broadcasted_iota(jnp.int32, (128, 128), 0) == lax.broadcasted_iota(jnp.int32, (128, 128), 1)
    for g in range(groups):
        sums, largest = [], []
        for i in range(tiles):
            here = pl.ds(i * 128, 128)
            pair = own_ref[g, here, :] + come_ref[g, here, :]
            top = jnp.max(jnp.abs(pair), axis=-1, keepdims=True)
            sums.append(pair)
            largest.append(jnp.sum(jnp.where(at, top, 0.0), axis=0, keepdims=True))
        largest.append(jnp.zeros((8 - tiles, 128), jnp.float32))
        code = jnp.ceil(jnp.log2(jnp.maximum(jnp.concatenate(largest, axis=0), 1e-30)) * 32.0)
        out_ref[g, rows:, :] = code.astype(jnp.int32).astype(jnp.int16)
        inverse = jnp.exp2(code * (-1.0 / 32.0)) * LEVELS
        inverse = jnp.concatenate([inverse, jnp.zeros((120, 128), jnp.float32)], axis=0).T
        for i in range(tiles):
            whole = jnp.round(sums[i] * inverse[:, i : i + 1])
            out_ref[g, i * 128 : (i + 1) * 128, :] = whole.astype(jnp.int32).astype(jnp.int16)


def pack_sums(own, come):
    groups, rows, steps = own.shape
    return pl.pallas_call(
        pack_kernel,
        out_shape=jax.ShapeDtypeStruct((groups, rows + CODE_ROWS, steps), jnp.int16),
        in_specs=[pl.BlockSpec(memory_space=pltpu.VMEM)] * 2,
        out_specs=pl.BlockSpec(memory_space=pltpu.VMEM),
        compiler_params=pltpu.CompilerParams(vmem_limit_bytes=16 << 20),
        name="pack",
    )(own, come)


def plane_columns(planes, rows_ref):
    looked, elements = planes.shape
    index = planes.astype(jnp.float32)
    height = (index + 0.5) * (1.0 / PLANES)
    azimuth = index * 2.399963229728653
    radius = jnp.sqrt(1.0 - height * height)
    normal_x = radius * jnp.cos(azimuth)
    normal_y = radius * jnp.sin(azimuth)
    coeffs = [
        normal_x * normal_x,
        normal_y * normal_y,
        height * height,
        2.0 * normal_x * normal_y,
        2.0 * normal_y * height,
        2.0 * normal_x * height,
    ]
    for q, coeff in enumerate(coeffs):
        rows_ref[q * looked : (q + 1) * looked, :elements] = coeff
    return rows_ref[...].T[:elements]


def range_kernel(parts_ref, coeffs_ref, far_ref, range_ref, stress_ref, sem):
    groups, rows, steps = parts_ref.shape
    rows -= CODE_ROWS
    codes = [parts_ref[g, rows:, :].astype(jnp.int32).astype(jnp.float32) for g in range(groups)]
    scales = code_scale(jnp.concatenate(codes, axis=0))
    scales = jnp.concatenate([scales, jnp.zeros((128 - groups * CODE_ROWS, 128), jnp.float32)], axis=0).T
    pieces = []
    for i in range(rows // 128):
        piece = None
        for g in range(groups):
            value = parts_ref[g, i * 128 : (i + 1) * 128, :].astype(jnp.int32).astype(jnp.float32)
            at = g * CODE_ROWS + i
            value = value * scales[:, at : at + 1]
            piece = value if piece is None else piece + value
        pieces.append(piece)
    components, elements, steps = stress_ref.shape
    stress = jnp.concatenate(pieces, axis=0).reshape(components, elements, steps)
    stress_ref[...] = stress
    leave = pltpu.make_async_copy(stress_ref, far_ref, sem)
    leave.start()
    looked = range_ref.shape[0]
    lane = lax.broadcasted_iota(jnp.int32, (elements, 128), 1)
    coeffs = coeffs_ref[...]
    result = jnp.zeros((elements, 128), jnp.float32)
    for p in range(looked):
        normal = coeffs[:, p : p + 1] * stress[0]
        for q in range(1, components):
            at = q * looked + p
            normal = normal + coeffs[:, at : at + 1] * stress[q]
        spread = jnp.max(normal, axis=-1, keepdims=True) - jnp.min(normal, axis=-1, keepdims=True)
        result = jnp.where(lane == p, spread, result)
    range_ref[...] = result.T[:looked, :]
    leave.wait()


def finish(parts, coeffs, looked):
    groups, rows, steps = parts.shape
    rows -= CODE_ROWS
    elements = coeffs.shape[0]
    stress_shape = (rows // elements, elements, steps)
    stress, ranges = pl.pallas_call(
        range_kernel,
        out_shape=(
            jax.ShapeDtypeStruct(stress_shape, jnp.float32),
            jax.ShapeDtypeStruct((looked, elements), jnp.float32),
        ),
        in_specs=[pl.BlockSpec(memory_space=pltpu.VMEM)] * 2,
        out_specs=(pl.BlockSpec(memory_space=pl.ANY), pl.BlockSpec(memory_space=pltpu.VMEM)),
        scratch_shapes=[pltpu.VMEM(stress_shape, jnp.float32), pltpu.SemaphoreType.DMA],
        compiler_params=pltpu.CompilerParams(vmem_limit_bytes=8 << 20),
        name="ranges",
    )(parts, coeffs)
    return stress, ranges.T


def gather_over(part, axes):
    copies = jnp.broadcast_to(part[None], (lax.axis_size(axes),) + part.shape)
    return lax.all_to_all(copies, axes, 0, 0)


def stage_kernel(owner_far, whole_ref, *refs):
    count = (len(refs) - 4) // 2
    away, (half_ref, *near, tile_ref, owner_ref, sems) = refs[:count], refs[count:]
    rows = half_ref.shape[0]
    start = pl.multiple_of(lax.axis_index("core") * rows, rows)
    fetches = [pltpu.make_async_copy(owner_far, owner_ref, sems.at[count + 1])]
    fetches += [pltpu.make_async_copy(whole_ref.at[pl.ds(start, rows)], half_ref, sems.at[count])]
    fetches += [pltpu.make_async_copy(a, b, sems.at[i]) for i, (a, b) in enumerate(zip(away, near))]
    for fetch in fetches:
        fetch.start()
    for fetch in fetches:
        fetch.wait()
    tile_ref[...] = jnp.full(tile_ref.shape, owner_ref[0], jnp.int32)


def stage(owner, whole, *others):
    channels, steps = whole.shape
    copied = [jax.ShapeDtypeStruct((channels // 2, steps), whole.dtype)]
    copied += [jax.ShapeDtypeStruct(x.shape, x.dtype) for x in others]
    return pl.pallas_call(
        stage_kernel,
        out_shape=(*copied, jax.ShapeDtypeStruct((8, 128), jnp.int32)),
        in_specs=[pl.BlockSpec(memory_space=pl.ANY)] * (1 + len(copied)),
        out_specs=(pl.BlockSpec(memory_space=pltpu.VMEM),) * (1 + len(copied)),
        scratch_shapes=[pltpu.SMEM(owner.shape, jnp.int32), pltpu.SemaphoreType.DMA((len(copied) + 1,))],
        compiler_params=pltpu.CompilerParams(vmem_limit_bytes=8 << 20),
        name="stage",
    )(owner, *(far(x) for x in (whole, *others)))


def pick_kernel(tile_ref, offered_ref, out_ref):
    piece = offered_ref[jnp.max(tile_ref[...])]
    for i in range(out_ref.shape[0]):
        out_ref[i] = piece


def pick_piece(offered, tile):
    return pl.pallas_call(
        pick_kernel,
        out_shape=jax.ShapeDtypeStruct(offered.shape, offered.dtype),
        in_specs=[pl.BlockSpec(memory_space=pltpu.VMEM)] * 2,
        out_specs=pl.BlockSpec(memory_space=pltpu.VMEM),
        compiler_params=pltpu.CompilerParams(vmem_limit_bytes=8 << 20),
        name="pick",
    )(tile, offered)


def fetch_window(half, tile):
    count = lax.axis_size(ROW)
    pieces = half.reshape(count, half.shape[0] // count, half.shape[1])
    offered = lax.all_to_all(pieces, ROW, 0, 0)
    whole_half = lax.all_to_all(pick_piece(offered, tile), ROW, 0, 0).reshape(half.shape)
    return lax.all_gather(whole_half, "core", axis=0, tiled=True)


def body(load_windows, owner_id, participation, frequency, damping, recovery, pattern, plane_table):
    planes = plane_table[0, 0].T
    half, part, rates, decays, planes, tile = stage(
        owner_id, load_windows[0], participation, frequency[None], damping[None], planes
    )
    window = fetch_window(half, tile)
    copies = make_history(window, part, rates, decays, lax.axis_size(ROW[:2]))
    column = lax.all_to_all(copies, ROW[:2], 0, 0)
    hist = gather_over(column, ROW[2])
    own, come, coeffs = recover(hist, recovery[0, 0], pattern[0, 0].T, planes, lax.axis_size(("yh", "core")))
    parts = lax.all_to_all(pack_sums(own, come), "yh", 0, 0)
    stress, plane_range = finish(parts, coeffs, planes.shape[0])
    return (stress[None, None], plane_range[None, None])


def solution(mesh):
    fine = Mesh(mesh.devices.reshape(4, 2, 8, 2, 4), ("yh", "core") + ROW)
    mode = ("yh", "core")
    placed = (
        P(ROW, None, None),
        P(),
        P(mode + ROW, None),
        P(mode + ROW),
        P(mode + ROW),
        P(mode, ROW, None, None, None, None),
        P(mode, ROW, None, None),
        P(ROW, mode, None, None),
    )
    return jax.shard_map(
        body,
        mesh=fine,
        in_specs=placed,
        out_specs=(P(ROW, mode, None, None, None), P(ROW, mode, None, None)),
        check_vma=False,
    )
```

```python
import jax
import jax.numpy as jnp
from jax import lax
from jax.experimental import pallas as pl
from jax.experimental.pallas import tpu as pltpu
from jax.sharding import Mesh
from jax.sharding import PartitionSpec as P

ROW = ("z", "yl", "x")
CODE_ROWS = 8
LEVELS = 32760.0
PLANES = 64


def code_scale(code):
    return jnp.exp2(code * (1.0 / 32.0)) * (1.0 / LEVELS)


def quantize(values):
    largest = jnp.max(jnp.abs(values), axis=-1, keepdims=True)
    code = jnp.ceil(jnp.log2(jnp.maximum(largest, 1e-30)) * 32.0)
    inverse = jnp.exp2(code * (-1.0 / 32.0)) * LEVELS
    whole = jnp.round(values * inverse).astype(jnp.int32)
    return whole, code


def as_row(column):
    n = column.shape[0]
    at = lax.broadcasted_iota(jnp.int32, (n, 128), 0) == lax.broadcasted_iota(jnp.int32, (n, 128), 1)
    return jnp.sum(jnp.where(at, column, 0.0), axis=0, keepdims=True)


def mode_table(rates, decays, rows_ref):
    modes = rates.shape[1]
    shifts = (1 << lax.broadcasted_iota(jnp.int32, (8, modes), 0)).astype(jnp.float32)
    angle = rates * shifts
    cos, sin = jnp.cos(angle), jnp.sin(angle)
    shrink = jnp.exp(-decays * rates * shifts)
    rows_ref[0:8, :modes] = shrink * cos
    rows_ref[8:16, :modes] = shrink * sin
    rows_ref[16:24, :modes] = rates * jnp.broadcast_to(sin[0:1], (8, modes))
    rows_ref[24:32, :modes] = rates * jnp.broadcast_to(cos[0:1], (8, modes))
    return rows_ref[...].T[:modes]


def history_kernel(window_ref, part_ref, rate_ref, decay_ref, out_ref, rows_ref):
    forces = jnp.dot(part_ref[...], window_ref[...], preferred_element_type=jnp.float32)
    modes, steps = forces.shape
    doublings = steps.bit_length() - 1
    table = mode_table(rate_ref[...], decay_ref[...], rows_ref)
    lane = lax.broadcasted_iota(jnp.int32, forces.shape, 1)
    re, im = forces, jnp.zeros_like(forces)
    for d in range(doublings):
        shift = 1 << d
        p_re, p_im = table[:, d : d + 1], table[:, 8 + d : 9 + d]
        keep = lane >= shift
        old_re = jnp.where(keep, pltpu.roll(re, shift, 1), 0.0)
        if d == 0:
            re, im = re + p_re * old_re, p_im * old_re
            continue
        old_im = jnp.where(keep, pltpu.roll(im, shift, 1), 0.0)
        re, im = re + p_re * old_re - p_im * old_im, im + p_re * old_im + p_im * old_re
    hist = table[:, 16:17] * re + table[:, 24:25] * im
    whole, code = quantize(hist)
    codes = jnp.broadcast_to(as_row(code), (CODE_ROWS, 128)).astype(jnp.int32)
    block = jnp.concatenate([whole, codes], axis=0).astype(jnp.int16)
    for i in range(out_ref.shape[0]):
        out_ref[i] = block


def make_history(window, participation, frequency, damping, count):
    modes, channels = participation.shape
    steps = window.shape[1]
    return pl.pallas_call(
        history_kernel,
        out_shape=jax.ShapeDtypeStruct((count, modes + CODE_ROWS, steps), jnp.int16),
        in_specs=[pl.BlockSpec(memory_space=pltpu.VMEM)] * 4,
        out_specs=pl.BlockSpec(memory_space=pltpu.VMEM),
        scratch_shapes=[pltpu.VMEM((128, 128), jnp.float32)],
        compiler_params=pltpu.CompilerParams(vmem_limit_bytes=16 << 20),
        cost_estimate=pl.CostEstimate(
            flops=2 * modes * channels * steps, bytes_accessed=2 * (channels * (modes + steps)), transcendentals=0
        ),
        name="history",
    )(window, participation, frequency, damping)


def product(picks_ref, side, coeff_ref, split_ref, out_ref, fetches):
    groups, per_slab, picked, height, width = coeff_ref.shape
    steps = out_ref.shape[2]
    for g in range(groups):
        if fetches:
            fetches[g].wait()
        for r in range(per_slab):
            block = (2 * g + side) * per_slab + r
            left = jnp.concatenate([coeff_ref[g, r, k] for k in range(picked)], axis=1)
            starts = [pl.multiple_of(picks_ref[k, block] * width, width) for k in range(picked)]
            right = jnp.concatenate([split_ref[pl.ds(start, width), :] for start in starts], axis=0)
            both = jnp.dot(left, right, preferred_element_type=jnp.float32)
            out_ref[g, r * height : (r + 1) * height, :] = both[:, :steps] + both[:, steps:]


def first_kernel(hist_ref, picks_far, far_ref, other_ref, split_ref, mine_ref, theirs_ref, picks_ref, sems, picks_sem):
    core = lax.axis_index("core")
    groups = mine_ref.shape[0]
    fetches = [[], []]
    fetch_picks = pltpu.make_async_copy(picks_far, picks_ref, picks_sem)
    fetch_picks.start()
    for i, (near, side) in enumerate([(theirs_ref, 1 - core), (mine_ref, core)]):
        for g in range(groups):
            fetch = pltpu.make_async_copy(far_ref.at[2 * g + side], near.at[g], sems.at[i, g])
            fetch.start()
            fetches[i].append(fetch)
    across, along, rows, steps = hist_ref.shape
    sources = across * along
    modes = rows - CODE_ROWS
    sub = lax.broadcasted_iota(jnp.int32, (8, 128), 0)
    tiles = []
    for base in range(0, sources, 8):
        tile = jnp.zeros((8, 128), jnp.int32)
        for i in range(8):
            s = base + i
            codes = hist_ref[s % across, s // across, modes : modes + CODE_ROWS, :].astype(jnp.int32)[:8]
            tile = jnp.where(sub == i, codes, tile)
        tiles.append(tile)
    scales = code_scale(jnp.concatenate(tiles, axis=0).astype(jnp.float32))
    scales = jnp.concatenate([scales, jnp.zeros((128 - sources, 128), jnp.float32)], axis=0).T
    for s in range(sources):
        value = hist_ref[s % across, s // across, :modes, :].astype(jnp.int32).astype(jnp.float32)
        value = value * scales[:modes, s : s + 1]
        high = value.astype(jnp.bfloat16)
        low = (value - high.astype(jnp.float32)).astype(jnp.bfloat16)
        split_ref[s * modes : (s + 1) * modes, :steps] = high
        split_ref[s * modes : (s + 1) * modes, steps:] = low
    fetch_picks.wait()
    product(picks_ref, 1 - core, theirs_ref, split_ref, other_ref, fetches[0])
    for fetch in fetches[1]:
        fetch.wait()


def second_kernel(split_ref, mine_ref, plane_ref, picks_far, own_ref, coeffs_ref, picks_ref, rows_ref, picks_sem):
    fetch_picks = pltpu.make_async_copy(picks_far, picks_ref, picks_sem)
    fetch_picks.start()
    plane_rows(plane_ref[...], rows_ref, coeffs_ref)
    fetch_picks.wait()
    product(picks_ref, lax.axis_index("core"), mine_ref, split_ref, own_ref, [])


def far(x):
    return pltpu.with_memory_space_constraint(x, pltpu.HBM)


def recover(hist, coeff_blocks, picks, planes, groups):
    across, along, rows, steps = hist.shape
    blocks, picked, height, width = coeff_blocks.shape
    slabs = coeff_blocks.reshape(groups, blocks // groups, picked, height, width)
    half = jax.ShapeDtypeStruct((groups // 2, blocks // groups * height, steps), jnp.float32)
    half_slabs = (groups // 2,) + slabs.shape[1:]
    cost = pl.CostEstimate(
        flops=2 * blocks * picked * height * width * steps,
        bytes_accessed=blocks * picked * height * width,
        transcendentals=0,
    )
    near, away = pl.BlockSpec(memory_space=pltpu.VMEM), pl.BlockSpec(memory_space=pl.ANY)
    scratch = [pltpu.SMEM(picks.shape, picks.dtype)]
    other, split, mine = pl.pallas_call(
        first_kernel,
        out_shape=(
            half,
            jax.ShapeDtypeStruct((across * along * (rows - CODE_ROWS), 2 * steps), jnp.bfloat16),
            jax.ShapeDtypeStruct(half_slabs, slabs.dtype),
        ),
        in_specs=[near, away, away],
        out_specs=(near,) * 3,
        scratch_shapes=[pltpu.VMEM(half_slabs, slabs.dtype)]
        + scratch
        + [pltpu.SemaphoreType.DMA((2, groups // 2)), pltpu.SemaphoreType.DMA],
        compiler_params=pltpu.CompilerParams(vmem_limit_bytes=24 << 20),
        cost_estimate=cost,
        name="first",
    )(hist, far(picks), far(slabs))
    come = lax.ppermute(other, "core", [(0, 1), (1, 0)])
    own, coeffs = pl.pallas_call(
        second_kernel,
        out_shape=(half, jax.ShapeDtypeStruct((6 * planes.shape[0], 128), jnp.float32)),
        in_specs=[near, near, near, away],
        out_specs=(near,) * 2,
        scratch_shapes=scratch + [pltpu.VMEM((6 * planes.shape[0], 128), jnp.float32), pltpu.SemaphoreType.DMA],
        compiler_params=pltpu.CompilerParams(vmem_limit_bytes=24 << 20),
        cost_estimate=cost,
        name="second",
    )(split, mine, planes, far(picks))
    return own, come, coeffs


def pack_kernel(own_ref, come_ref, out_ref):
    groups, rows, steps = out_ref.shape
    rows -= CODE_ROWS
    tiles = rows // 128
    for g in range(groups):
        sums, largest = [], []
        for i in range(tiles):
            here = pl.ds(i * 128, 128)
            turned = (own_ref[g, here, :] + come_ref[g, here, :]).T
            sums.append(turned)
            largest.append(jnp.max(jnp.abs(turned), axis=0, keepdims=True))
        largest.append(jnp.zeros((8 - tiles, 128), jnp.float32))
        code = jnp.ceil(jnp.log2(jnp.maximum(jnp.concatenate(largest, axis=0), 1e-30)) * 32.0)
        out_ref[g, rows:, :] = code.astype(jnp.int32).astype(jnp.int16)
        inverse = jnp.exp2(code * (-1.0 / 32.0)) * LEVELS
        for i in range(tiles):
            whole = jnp.round(sums[i] * inverse[i : i + 1])
            out_ref[g, i * 128 : (i + 1) * 128, :] = whole.astype(jnp.int32).astype(jnp.int16)


def pack_sums(own, come):
    groups, rows, steps = own.shape
    return pl.pallas_call(
        pack_kernel,
        out_shape=jax.ShapeDtypeStruct((groups, rows + CODE_ROWS, steps), jnp.int16),
        in_specs=[pl.BlockSpec(memory_space=pltpu.VMEM)] * 2,
        out_specs=pl.BlockSpec(memory_space=pltpu.VMEM),
        compiler_params=pltpu.CompilerParams(vmem_limit_bytes=16 << 20),
        name="pack",
    )(own, come)


def plane_rows(planes, pad_ref, out_ref):
    looked, elements = planes.shape
    index = planes.astype(jnp.float32)
    height = (index + 0.5) * (1.0 / PLANES)
    azimuth = index * 2.399963229728653
    radius = jnp.sqrt(1.0 - height * height)
    normal_x = radius * jnp.cos(azimuth)
    normal_y = radius * jnp.sin(azimuth)
    coeffs = [
        normal_x * normal_x,
        normal_y * normal_y,
        height * height,
        2.0 * normal_x * normal_y,
        2.0 * normal_y * height,
        2.0 * normal_x * height,
    ]
    pad_ref[...] = jnp.zeros_like(pad_ref)
    lane = lax.broadcasted_iota(jnp.int32, (looked, 128), 1)
    for q, coeff in enumerate(coeffs):
        pad_ref[q * looked : (q + 1) * looked, :elements] = coeff
        left = pad_ref[q * looked : (q + 1) * looked, :]
        right = pltpu.roll(pltpu.roll(left, elements, 1), looked // 2, 0)
        out_ref[q * looked : (q + 1) * looked, :] = jnp.where(lane < elements, left, right)


def range_kernel(parts_ref, coeffs_ref, stress_ref, range_ref):
    groups, rows, steps = parts_ref.shape
    rows -= CODE_ROWS
    components, elements, steps = stress_ref.shape
    looked = range_ref.shape[0]
    scales = [code_scale(parts_ref[g, rows:, :].astype(jnp.int32).astype(jnp.float32)) for g in range(groups)]
    low = lax.broadcasted_iota(jnp.int32, (steps, 128), 1) < elements
    twice = []
    for i in range(rows // 128):
        total = None
        for g in range(groups):
            value = parts_ref[g, i * 128 : (i + 1) * 128, :].astype(jnp.int32).astype(jnp.float32)
            value = value * scales[g][i : i + 1]
            total = value if total is None else total + value
        upright = total.T
        stress_ref[2 * i] = upright[:elements]
        stress_ref[2 * i + 1] = upright[elements:]
        swapped = pltpu.roll(total, elements, 1)
        twice.append(jnp.where(low, total, swapped))
        twice.append(jnp.where(low, swapped, total))
    spreads = []
    for k in range(looked // 2):
        normal = coeffs_ref[k : k + 1, :] * twice[0]
        for q in range(1, components):
            normal = normal + coeffs_ref[q * looked + k : q * looked + k + 1, :] * twice[q]
        spreads.append(jnp.max(normal, axis=0, keepdims=True) - jnp.min(normal, axis=0, keepdims=True))
    spread = jnp.concatenate(spreads + spreads, axis=0)
    first = lax.broadcasted_iota(jnp.int32, (looked, 128), 0) < looked // 2
    range_ref[...] = jnp.where(first, spread, pltpu.roll(spread, elements, 1))[:, :elements]


def finish(parts, coeffs, looked):
    groups, rows, steps = parts.shape
    rows -= CODE_ROWS
    elements = 128 // 2
    stress, ranges = pl.pallas_call(
        range_kernel,
        out_shape=(
            jax.ShapeDtypeStruct((rows // elements, elements, steps), jnp.float32),
            jax.ShapeDtypeStruct((looked, elements), jnp.float32),
        ),
        in_specs=[pl.BlockSpec(memory_space=pltpu.VMEM)] * 2,
        out_specs=(pl.BlockSpec(memory_space=pltpu.VMEM),) * 2,
        compiler_params=pltpu.CompilerParams(vmem_limit_bytes=8 << 20),
        name="ranges",
    )(parts, coeffs)
    return stress, ranges.T


def gather_over(part, axes):
    copies = jnp.broadcast_to(part[None], (lax.axis_size(axes),) + part.shape)
    return lax.all_to_all(copies, axes, 0, 0)


def stage_kernel(owner_ref, whole_ref, *refs):
    count = (len(refs) - 3) // 2
    away, (half_ref, *near, tile_ref, sems) = refs[:count], refs[count:]
    rows = half_ref.shape[0]
    start = pl.multiple_of(lax.axis_index("core") * rows, rows)
    fetches = [pltpu.make_async_copy(whole_ref.at[pl.ds(start, rows)], half_ref, sems.at[count])]
    fetches += [pltpu.make_async_copy(a, b, sems.at[i]) for i, (a, b) in enumerate(zip(away, near))]
    for fetch in fetches:
        fetch.start()
    tile_ref[...] = jnp.full(tile_ref.shape, owner_ref[0], jnp.int32)
    for fetch in fetches:
        fetch.wait()


def stage(owner, whole, *others):
    channels, steps = whole.shape
    copied = [jax.ShapeDtypeStruct((channels // 2, steps), whole.dtype)]
    copied += [jax.ShapeDtypeStruct(x.shape, x.dtype) for x in others]
    return pl.pallas_call(
        stage_kernel,
        out_shape=(*copied, jax.ShapeDtypeStruct((8, 128), jnp.int32)),
        in_specs=[pl.BlockSpec(memory_space=pltpu.SMEM)] + [pl.BlockSpec(memory_space=pl.ANY)] * len(copied),
        out_specs=(pl.BlockSpec(memory_space=pltpu.VMEM),) * (1 + len(copied)),
        scratch_shapes=[pltpu.SemaphoreType.DMA((len(copied),))],
        compiler_params=pltpu.CompilerParams(vmem_limit_bytes=8 << 20),
        name="stage",
    )(owner, *(far(x) for x in (whole, *others)))


def pick_kernel(tile_ref, offered_ref, out_ref):
    piece = offered_ref[jnp.max(tile_ref[...])]
    for i in range(out_ref.shape[0]):
        out_ref[i] = piece


def pick_piece(offered, tile):
    return pl.pallas_call(
        pick_kernel,
        out_shape=jax.ShapeDtypeStruct(offered.shape, offered.dtype),
        in_specs=[pl.BlockSpec(memory_space=pltpu.VMEM)] * 2,
        out_specs=pl.BlockSpec(memory_space=pltpu.VMEM),
        compiler_params=pltpu.CompilerParams(vmem_limit_bytes=8 << 20),
        name="pick",
    )(tile, offered)


def fetch_window(half, tile):
    count = lax.axis_size(ROW)
    pieces = half.reshape(count, half.shape[0] // count, half.shape[1])
    offered = lax.all_to_all(pieces, ROW, 0, 0)
    whole_half = lax.all_to_all(pick_piece(offered, tile), ROW, 0, 0).reshape(half.shape)
    return lax.all_gather(whole_half, "core", axis=0, tiled=True)


def body(load_windows, owner_id, participation, frequency, damping, recovery, pattern, plane_table):
    planes = plane_table[0, 0].T
    half, part, rates, decays, planes, tile = stage(
        owner_id, load_windows[0], participation, frequency[None], damping[None], planes
    )
    window = fetch_window(half, tile)
    copies = make_history(window, part, rates, decays, lax.axis_size(ROW[:2]))
    column = lax.all_to_all(copies, ROW[:2], 0, 0)
    hist = gather_over(column, ROW[2])
    own, come, coeffs = recover(hist, recovery[0, 0], pattern[0, 0].T, planes, lax.axis_size(("yh", "core")))
    parts = lax.all_to_all(pack_sums(own, come), "yh", 0, 0)
    stress, plane_range = finish(parts, coeffs, planes.shape[0])
    return (stress[None, None], plane_range[None, None])


def solution(mesh):
    fine = Mesh(mesh.devices.reshape(4, 2, 8, 2, 4), ("yh", "core") + ROW)
    mode = ("yh", "core")
    placed = (
        P(ROW, None, None),
        P(),
        P(mode + ROW, None),
        P(mode + ROW),
        P(mode + ROW),
        P(mode, ROW, None, None, None, None),
        P(mode, ROW, None, None),
        P(ROW, mode, None, None),
    )
    return jax.shard_map(
        body,
        mesh=fine,
        in_specs=placed,
        out_specs=(P(ROW, mode, None, None, None), P(ROW, mode, None, None)),
        check_vma=False,
    )
```

```python
import functools

import jax
import jax.numpy as jnp
from jax import lax
from jax.experimental import pallas as pl
from jax.experimental.pallas import tpu as pltpu
from jax.sharding import Mesh
from jax.sharding import PartitionSpec as P

ROW = ("z", "yl", "x")
CODE_ROWS = 8
LEVELS = 32760.0
PLANES = 64


def code_scale(code):
    return jnp.exp2(code * (1.0 / 32.0)) * (1.0 / LEVELS)


def quantize(values):
    largest = jnp.max(jnp.abs(values), axis=-1, keepdims=True)
    code = jnp.ceil(jnp.log2(jnp.maximum(largest, 1e-30)) * 32.0)
    inverse = jnp.exp2(code * (-1.0 / 32.0)) * LEVELS
    whole = jnp.round(values * inverse).astype(jnp.int32)
    return whole, code


def as_row(column):
    n = column.shape[0]
    at = lax.broadcasted_iota(jnp.int32, (n, 128), 0) == lax.broadcasted_iota(jnp.int32, (n, 128), 1)
    return jnp.sum(jnp.where(at, column, 0.0), axis=0, keepdims=True)


def mode_table(rates, decays, rows_ref):
    modes = rates.shape[1]
    shifts = (1 << lax.broadcasted_iota(jnp.int32, (8, modes), 0)).astype(jnp.float32)
    angle = rates * shifts
    cos, sin = jnp.cos(angle), jnp.sin(angle)
    shrink = jnp.exp(-decays * rates * shifts)
    rows_ref[0:8, :modes] = shrink * cos
    rows_ref[8:16, :modes] = shrink * sin
    rows_ref[16:24, :modes] = rates * jnp.broadcast_to(sin[0:1], (8, modes))
    rows_ref[24:32, :modes] = rates * jnp.broadcast_to(cos[0:1], (8, modes))
    return rows_ref[...].T[:modes]


def history_kernel(window_ref, part_ref, rate_ref, decay_ref, out_ref, rows_ref):
    forces = jnp.dot(part_ref[...], window_ref[...], preferred_element_type=jnp.float32)
    modes, steps = forces.shape
    doublings = steps.bit_length() - 1
    table = mode_table(rate_ref[...], decay_ref[...], rows_ref)
    lane = lax.broadcasted_iota(jnp.int32, forces.shape, 1)
    re, im = forces, jnp.zeros_like(forces)
    for d in range(doublings):
        shift = 1 << d
        p_re, p_im = table[:, d : d + 1], table[:, 8 + d : 9 + d]
        keep = lane >= shift
        old_re = jnp.where(keep, pltpu.roll(re, shift, 1), 0.0)
        if d == 0:
            re, im = re + p_re * old_re, p_im * old_re
            continue
        old_im = jnp.where(keep, pltpu.roll(im, shift, 1), 0.0)
        re, im = re + p_re * old_re - p_im * old_im, im + p_re * old_im + p_im * old_re
    hist = table[:, 16:17] * re + table[:, 24:25] * im
    whole, code = quantize(hist)
    codes = jnp.broadcast_to(as_row(code), (CODE_ROWS, 128)).astype(jnp.int32)
    block = jnp.concatenate([whole, codes], axis=0).astype(jnp.int16)
    for i in range(out_ref.shape[0]):
        out_ref[i] = block


def make_history(window, participation, frequency, damping, count):
    modes, channels = participation.shape
    steps = window.shape[1]
    return pl.pallas_call(
        history_kernel,
        out_shape=jax.ShapeDtypeStruct((count, modes + CODE_ROWS, steps), jnp.int16),
        in_specs=[pl.BlockSpec(memory_space=pltpu.VMEM)] * 4,
        out_specs=pl.BlockSpec(memory_space=pltpu.VMEM),
        scratch_shapes=[pltpu.VMEM((128, 128), jnp.float32)],
        compiler_params=pltpu.CompilerParams(vmem_limit_bytes=16 << 20),
        cost_estimate=pl.CostEstimate(
            flops=2 * modes * channels * steps, bytes_accessed=2 * (channels * (modes + steps)), transcendentals=0
        ),
        name="history",
    )(window, participation, frequency, damping)


def product(picks_ref, side, coeff_ref, split_ref, out_ref, fetches):
    groups, per_slab, picked, height, width = coeff_ref.shape
    steps = out_ref.shape[2]
    for g in range(groups):
        if fetches:
            fetches[g].wait()
        for r in range(per_slab):
            block = (2 * g + side) * per_slab + r
            left = jnp.concatenate([coeff_ref[g, r, k] for k in range(picked)], axis=1)
            starts = [pl.multiple_of(picks_ref[k, block] * width, width) for k in range(picked)]
            right = jnp.concatenate([split_ref[pl.ds(start, width), :] for start in starts], axis=0)
            both = jnp.dot(left, right, preferred_element_type=jnp.float32)
            out_ref[g, r * height : (r + 1) * height, :] = both[:, :steps] + both[:, steps:]


def first_kernel(hist_ref, picks_far, far_ref, other_ref, split_ref, mine_ref, theirs_ref, picks_ref, sems, picks_sem):
    core = lax.axis_index("core")
    groups = mine_ref.shape[0]
    fetches = [[], []]
    fetch_picks = pltpu.make_async_copy(picks_far, picks_ref, picks_sem)
    fetch_picks.start()
    for i, (near, side) in enumerate([(theirs_ref, 1 - core), (mine_ref, core)]):
        for g in range(groups):
            fetch = pltpu.make_async_copy(far_ref.at[2 * g + side], near.at[g], sems.at[i, g])
            fetch.start()
            fetches[i].append(fetch)
    across, along, rows, steps = hist_ref.shape
    sources = across * along
    modes = rows - CODE_ROWS
    sub = lax.broadcasted_iota(jnp.int32, (8, 128), 0)
    tiles = []
    for base in range(0, sources, 8):
        tile = jnp.zeros((8, 128), jnp.int32)
        for i in range(8):
            s = base + i
            codes = hist_ref[s % across, s // across, modes : modes + CODE_ROWS, :].astype(jnp.int32)[:8]
            tile = jnp.where(sub == i, codes, tile)
        tiles.append(tile)
    scales = code_scale(jnp.concatenate(tiles, axis=0).astype(jnp.float32))
    scales = jnp.concatenate([scales, jnp.zeros((128 - sources, 128), jnp.float32)], axis=0).T
    for s in range(sources):
        value = hist_ref[s % across, s // across, :modes, :].astype(jnp.int32).astype(jnp.float32)
        value = value * scales[:modes, s : s + 1]
        high = value.astype(jnp.bfloat16)
        low = (value - high.astype(jnp.float32)).astype(jnp.bfloat16)
        split_ref[s * modes : (s + 1) * modes, :steps] = high
        split_ref[s * modes : (s + 1) * modes, steps:] = low
    fetch_picks.wait()
    product(picks_ref, 1 - core, theirs_ref, split_ref, other_ref, fetches[0])
    for fetch in fetches[1]:
        fetch.wait()


def second_kernel(split_ref, mine_ref, plane_ref, picks_far, own_ref, coeffs_ref, picks_ref, rows_ref, picks_sem):
    fetch_picks = pltpu.make_async_copy(picks_far, picks_ref, picks_sem)
    fetch_picks.start()
    plane_rows(plane_ref[...], rows_ref, coeffs_ref)
    fetch_picks.wait()
    product(picks_ref, lax.axis_index("core"), mine_ref, split_ref, own_ref, [])


def far(x):
    return pltpu.with_memory_space_constraint(x, pltpu.HBM)


def recover(hist, coeff_blocks, picks, planes, groups):
    across, along, rows, steps = hist.shape
    blocks, picked, height, width = coeff_blocks.shape
    slabs = coeff_blocks.reshape(groups, blocks // groups, picked, height, width)
    half = jax.ShapeDtypeStruct((groups // 2, blocks // groups * height, steps), jnp.float32)
    half_slabs = (groups // 2,) + slabs.shape[1:]
    cost = pl.CostEstimate(
        flops=2 * blocks * picked * height * width * steps,
        bytes_accessed=blocks * picked * height * width,
        transcendentals=0,
    )
    near, away = pl.BlockSpec(memory_space=pltpu.VMEM), pl.BlockSpec(memory_space=pl.ANY)
    scratch = [pltpu.SMEM(picks.shape, picks.dtype)]
    other, split, mine = pl.pallas_call(
        first_kernel,
        out_shape=(
            half,
            jax.ShapeDtypeStruct((across * along * (rows - CODE_ROWS), 2 * steps), jnp.bfloat16),
            jax.ShapeDtypeStruct(half_slabs, slabs.dtype),
        ),
        in_specs=[near, away, away],
        out_specs=(near,) * 3,
        scratch_shapes=[pltpu.VMEM(half_slabs, slabs.dtype)]
        + scratch
        + [pltpu.SemaphoreType.DMA((2, groups // 2)), pltpu.SemaphoreType.DMA],
        compiler_params=pltpu.CompilerParams(vmem_limit_bytes=24 << 20),
        cost_estimate=cost,
        name="first",
    )(hist, far(picks), far(slabs))
    come = lax.ppermute(other, "core", [(0, 1), (1, 0)])
    own, coeffs = pl.pallas_call(
        second_kernel,
        out_shape=(half, jax.ShapeDtypeStruct((6 * planes.shape[0], 128), jnp.float32)),
        in_specs=[near, near, near, away],
        out_specs=(near,) * 2,
        scratch_shapes=scratch + [pltpu.VMEM((6 * planes.shape[0], 128), jnp.float32), pltpu.SemaphoreType.DMA],
        compiler_params=pltpu.CompilerParams(vmem_limit_bytes=24 << 20),
        cost_estimate=cost,
        name="second",
    )(split, mine, planes, far(picks))
    return own, come, coeffs


def pack_kernel(own_ref, come_ref, out_ref):
    groups, rows, steps = out_ref.shape
    rows -= CODE_ROWS
    tiles = rows // 128
    for g in range(groups):
        sums, largest = [], []
        for i in range(tiles):
            here = pl.ds(i * 128, 128)
            turned = (own_ref[g, here, :] + come_ref[g, here, :]).T
            sums.append(turned)
            largest.append(jnp.max(jnp.abs(turned), axis=0, keepdims=True))
        largest.append(jnp.zeros((8 - tiles, 128), jnp.float32))
        code = jnp.ceil(jnp.log2(jnp.maximum(jnp.concatenate(largest, axis=0), 1e-30)) * 32.0)
        out_ref[g, rows:, :] = code.astype(jnp.int32).astype(jnp.int16)
        inverse = jnp.exp2(code * (-1.0 / 32.0)) * LEVELS
        for i in range(tiles):
            whole = jnp.round(sums[i] * inverse[i : i + 1])
            out_ref[g, i * 128 : (i + 1) * 128, :] = whole.astype(jnp.int32).astype(jnp.int16)


def pack_sums(own, come):
    groups, rows, steps = own.shape
    return pl.pallas_call(
        pack_kernel,
        out_shape=jax.ShapeDtypeStruct((groups, rows + CODE_ROWS, steps), jnp.int16),
        in_specs=[pl.BlockSpec(memory_space=pltpu.VMEM)] * 2,
        out_specs=pl.BlockSpec(memory_space=pltpu.VMEM),
        compiler_params=pltpu.CompilerParams(vmem_limit_bytes=16 << 20),
        name="pack",
    )(own, come)


def plane_rows(planes, pad_ref, out_ref):
    looked, elements = planes.shape
    index = planes.astype(jnp.float32)
    height = (index + 0.5) * (1.0 / PLANES)
    azimuth = index * 2.399963229728653
    radius = jnp.sqrt(1.0 - height * height)
    normal_x = radius * jnp.cos(azimuth)
    normal_y = radius * jnp.sin(azimuth)
    coeffs = [
        normal_x * normal_x,
        normal_y * normal_y,
        height * height,
        2.0 * normal_x * normal_y,
        2.0 * normal_y * height,
        2.0 * normal_x * height,
    ]
    pad_ref[...] = jnp.zeros_like(pad_ref)
    lane = lax.broadcasted_iota(jnp.int32, (looked, 128), 1)
    for q, coeff in enumerate(coeffs):
        pad_ref[q * looked : (q + 1) * looked, :elements] = coeff
        left = pad_ref[q * looked : (q + 1) * looked, :]
        right = pltpu.roll(pltpu.roll(left, elements, 1), looked // 2, 0)
        out_ref[q * looked : (q + 1) * looked, :] = jnp.where(lane < elements, left, right)


def range_kernel(parts_ref, coeffs_ref, stress_ref, range_ref):
    groups, rows, steps = parts_ref.shape
    rows -= CODE_ROWS
    components, elements, steps = stress_ref.shape
    looked = range_ref.shape[0]
    scales = [code_scale(parts_ref[g, rows:, :].astype(jnp.int32).astype(jnp.float32)) for g in range(groups)]
    low = lax.broadcasted_iota(jnp.int32, (steps, 128), 1) < elements
    twice = []
    for i in range(rows // 128):
        total = None
        for g in range(groups):
            value = parts_ref[g, i * 128 : (i + 1) * 128, :].astype(jnp.int32).astype(jnp.float32)
            value = value * scales[g][i : i + 1]
            total = value if total is None else total + value
        upright = total.T
        stress_ref[2 * i] = upright[:elements]
        stress_ref[2 * i + 1] = upright[elements:]
        swapped = pltpu.roll(total, elements, 1)
        twice.append(jnp.where(low, total, swapped))
        twice.append(jnp.where(low, swapped, total))
    spreads = []
    for k in range(looked // 2):
        normal = coeffs_ref[k : k + 1, :] * twice[0]
        for q in range(1, components):
            normal = normal + coeffs_ref[q * looked + k : q * looked + k + 1, :] * twice[q]
        spreads.append(jnp.max(normal, axis=0, keepdims=True) - jnp.min(normal, axis=0, keepdims=True))
    spread = jnp.concatenate(spreads + spreads, axis=0)
    first = lax.broadcasted_iota(jnp.int32, (looked, 128), 0) < looked // 2
    range_ref[...] = jnp.where(first, spread, pltpu.roll(spread, elements, 1))[:, :elements]


def finish(parts, coeffs, looked):
    groups, rows, steps = parts.shape
    rows -= CODE_ROWS
    elements = 128 // 2
    stress, ranges = pl.pallas_call(
        range_kernel,
        out_shape=(
            jax.ShapeDtypeStruct((rows // elements, elements, steps), jnp.float32),
            jax.ShapeDtypeStruct((looked, elements), jnp.float32),
        ),
        in_specs=[pl.BlockSpec(memory_space=pltpu.VMEM)] * 2,
        out_specs=(pl.BlockSpec(memory_space=pltpu.VMEM),) * 2,
        compiler_params=pltpu.CompilerParams(vmem_limit_bytes=8 << 20),
        name="ranges",
    )(parts, coeffs)
    return stress, ranges.T


def gather_over(part, axes):
    copies = jnp.broadcast_to(part[None], (lax.axis_size(axes),) + part.shape)
    return lax.all_to_all(copies, axes, 0, 0)


def stage_kernel(owner_ref, whole_ref, *refs):
    count = (len(refs) - 3) // 2
    away, (half_ref, *near, tile_ref, sems) = refs[:count], refs[count:]
    rows = half_ref.shape[0]
    start = pl.multiple_of(lax.axis_index("core") * rows, rows)
    fetches = [pltpu.make_async_copy(whole_ref.at[pl.ds(start, rows)], half_ref, sems.at[count])]
    fetches += [pltpu.make_async_copy(a, b, sems.at[i]) for i, (a, b) in enumerate(zip(away, near))]
    for fetch in fetches:
        fetch.start()
    tile_ref[...] = jnp.full(tile_ref.shape, owner_ref[0], jnp.int32)
    for fetch in fetches:
        fetch.wait()


def stage(owner, whole, *others):
    channels, steps = whole.shape
    copied = [jax.ShapeDtypeStruct((channels // 2, steps), whole.dtype)]
    copied += [jax.ShapeDtypeStruct(x.shape, x.dtype) for x in others]
    return pl.pallas_call(
        stage_kernel,
        out_shape=(*copied, jax.ShapeDtypeStruct((8, 128), jnp.int32)),
        in_specs=[pl.BlockSpec(memory_space=pltpu.SMEM)] + [pl.BlockSpec(memory_space=pl.ANY)] * len(copied),
        out_specs=(pl.BlockSpec(memory_space=pltpu.VMEM),) * (1 + len(copied)),
        scratch_shapes=[pltpu.SemaphoreType.DMA((len(copied),))],
        compiler_params=pltpu.CompilerParams(vmem_limit_bytes=8 << 20),
        name="stage",
    )(owner, *(far(x) for x in (whole, *others)))


def pick_kernel(shift, tile_ref, offered_ref, out_ref):
    owner = jnp.max(tile_ref[...])
    piece = offered_ref[lax.rem(lax.shift_right_logical(owner, shift), offered_ref.shape[0])]
    for i in range(out_ref.shape[0]):
        out_ref[i] = piece


def pick_piece(offered, tile, shift):
    return pl.pallas_call(
        functools.partial(pick_kernel, shift),
        out_shape=jax.ShapeDtypeStruct(offered.shape, offered.dtype),
        in_specs=[pl.BlockSpec(memory_space=pltpu.VMEM)] * 2,
        out_specs=pl.BlockSpec(memory_space=pltpu.VMEM),
        compiler_params=pltpu.CompilerParams(vmem_limit_bytes=8 << 20),
        name="pick",
    )(tile, offered)


def fetch_window(half, tile, owner):
    plane = lax.axis_size(ROW[1:])
    shift = plane.bit_length() - 1
    pieces = half.reshape(plane, half.shape[0] // plane, half.shape[1])
    mine = lax.axis_index(ROW[0]) == lax.shift_right_logical(owner, shift)
    offered = lax.cond(mine, lambda x: lax.all_to_all(x, ROW[1:], 0, 0), lambda x: x, pieces)
    offered = lax.all_to_all(pick_piece(offered, tile, 0), ROW[0], 0, 0)
    whole_half = lax.all_to_all(pick_piece(offered, tile, shift), ROW[1:], 0, 0).reshape(half.shape)
    return lax.all_gather(whole_half, "core", axis=0, tiled=True)


def body(load_windows, owner_id, participation, frequency, damping, recovery, pattern, plane_table):
    planes = plane_table[0, 0].T
    half, part, rates, decays, planes, tile = stage(
        owner_id, load_windows[0], participation, frequency[None], damping[None], planes
    )
    window = fetch_window(half, tile, owner_id[0])
    copies = make_history(window, part, rates, decays, lax.axis_size(ROW[:2]))
    column = lax.all_to_all(copies, ROW[:2], 0, 0)
    hist = gather_over(column, ROW[2])
    own, come, coeffs = recover(hist, recovery[0, 0], pattern[0, 0].T, planes, lax.axis_size(("yh", "core")))
    parts = lax.all_to_all(pack_sums(own, come), "yh", 0, 0)
    stress, plane_range = finish(parts, coeffs, planes.shape[0])
    return (stress[None, None], plane_range[None, None])


def solution(mesh):
    fine = Mesh(mesh.devices.reshape(4, 2, 8, 2, 4), ("yh", "core") + ROW)
    mode = ("yh", "core")
    placed = (
        P(ROW, None, None),
        P(),
        P(mode + ROW, None),
        P(mode + ROW),
        P(mode + ROW),
        P(mode, ROW, None, None, None, None),
        P(mode, ROW, None, None),
        P(ROW, mode, None, None),
    )
    return jax.shard_map(
        body,
        mesh=fine,
        in_specs=placed,
        out_specs=(P(ROW, mode, None, None, None), P(ROW, mode, None, None)),
        check_vma=False,
    )
```

```python
import functools

import jax
import jax.numpy as jnp
from jax import lax
from jax.experimental import pallas as pl
from jax.experimental.pallas import tpu as pltpu
from jax.sharding import Mesh
from jax.sharding import PartitionSpec as P

ROW = ("z", "yl", "x")
CODE_ROWS = 8
LEVELS = 32760.0
PLANES = 64


def code_scale(code):
    return jnp.exp2(code * (1.0 / 32.0)) * (1.0 / LEVELS)


def quantize(values):
    largest = jnp.max(jnp.abs(values), axis=-1, keepdims=True)
    code = jnp.ceil(jnp.log2(jnp.maximum(largest, 1e-30)) * 32.0)
    inverse = jnp.exp2(code * (-1.0 / 32.0)) * LEVELS
    whole = jnp.round(values * inverse).astype(jnp.int32)
    return whole, code


def as_row(column):
    n = column.shape[0]
    at = lax.broadcasted_iota(jnp.int32, (n, 128), 0) == lax.broadcasted_iota(jnp.int32, (n, 128), 1)
    return jnp.sum(jnp.where(at, column, 0.0), axis=0, keepdims=True)


def mode_table(rates, decays, rows_ref):
    modes = rates.shape[1]
    shifts = (1 << lax.broadcasted_iota(jnp.int32, (8, modes), 0)).astype(jnp.float32)
    angle = rates * shifts
    cos, sin = jnp.cos(angle), jnp.sin(angle)
    shrink = jnp.exp(-decays * rates * shifts)
    rows_ref[0:8, :modes] = shrink * cos
    rows_ref[8:16, :modes] = shrink * sin
    rows_ref[16:24, :modes] = rates * jnp.broadcast_to(sin[0:1], (8, modes))
    rows_ref[24:32, :modes] = rates * jnp.broadcast_to(cos[0:1], (8, modes))
    return rows_ref[...].T[:modes]


def history_kernel(window_ref, part_ref, rate_ref, decay_ref, out_ref, rows_ref):
    forces = jnp.dot(part_ref[...], window_ref[...], preferred_element_type=jnp.float32)
    modes, steps = forces.shape
    doublings = steps.bit_length() - 1
    table = mode_table(rate_ref[...], decay_ref[...], rows_ref)
    lane = lax.broadcasted_iota(jnp.int32, forces.shape, 1)
    re, im = forces, jnp.zeros_like(forces)
    for d in range(doublings):
        shift = 1 << d
        p_re, p_im = table[:, d : d + 1], table[:, 8 + d : 9 + d]
        keep = lane >= shift
        old_re = jnp.where(keep, pltpu.roll(re, shift, 1), 0.0)
        if d == 0:
            re, im = re + p_re * old_re, p_im * old_re
            continue
        old_im = jnp.where(keep, pltpu.roll(im, shift, 1), 0.0)
        re, im = re + p_re * old_re - p_im * old_im, im + p_re * old_im + p_im * old_re
    hist = table[:, 16:17] * re + table[:, 24:25] * im
    whole, code = quantize(hist)
    codes = jnp.broadcast_to(as_row(code), (CODE_ROWS, 128)).astype(jnp.int32)
    block = jnp.concatenate([whole, codes], axis=0).astype(jnp.int16)
    for i in range(out_ref.shape[0]):
        out_ref[i] = block


def make_history(window, participation, frequency, damping, count):
    modes, channels = participation.shape
    steps = window.shape[1]
    return pl.pallas_call(
        history_kernel,
        out_shape=jax.ShapeDtypeStruct((count, modes + CODE_ROWS, steps), jnp.int16),
        in_specs=[pl.BlockSpec(memory_space=pltpu.VMEM)] * 4,
        out_specs=pl.BlockSpec(memory_space=pltpu.VMEM),
        scratch_shapes=[pltpu.VMEM((128, 128), jnp.float32)],
        compiler_params=pltpu.CompilerParams(vmem_limit_bytes=16 << 20),
        cost_estimate=pl.CostEstimate(
            flops=2 * modes * channels * steps, bytes_accessed=2 * (channels * (modes + steps)), transcendentals=0
        ),
        name="history",
    )(window, participation, frequency, damping)


def product(picks_ref, side, coeff_ref, split_ref, out_ref, fetches):
    groups, per_slab, picked, height, width = coeff_ref.shape
    steps = out_ref.shape[2]
    for g in range(groups):
        if fetches:
            fetches[g].wait()
        for r in range(per_slab):
            block = (2 * g + side) * per_slab + r
            left = jnp.concatenate([coeff_ref[g, r, k] for k in range(picked)], axis=1)
            starts = [pl.multiple_of(picks_ref[k, block] * width, width) for k in range(picked)]
            right = jnp.concatenate([split_ref[pl.ds(start, width), :] for start in starts], axis=0)
            both = jnp.dot(left, right, preferred_element_type=jnp.float32)
            out_ref[g, r * height : (r + 1) * height, :] = both[:, :steps] + both[:, steps:]


def first_kernel(hist_ref, picks_far, far_ref, other_ref, split_ref, mine_ref, theirs_ref, picks_ref, sems, picks_sem):
    core = lax.axis_index("core")
    groups = mine_ref.shape[0]
    fetches = [[], []]
    fetch_picks = pltpu.make_async_copy(picks_far, picks_ref, picks_sem)
    fetch_picks.start()
    for i, (near, side) in enumerate([(theirs_ref, 1 - core), (mine_ref, core)]):
        for g in range(groups):
            fetch = pltpu.make_async_copy(far_ref.at[2 * g + side], near.at[g], sems.at[i, g])
            fetch.start()
            fetches[i].append(fetch)
    across, along, rows, steps = hist_ref.shape
    sources = across * along
    modes = rows - CODE_ROWS
    sub = lax.broadcasted_iota(jnp.int32, (8, 128), 0)
    tiles = []
    for base in range(0, sources, 8):
        tile = jnp.zeros((8, 128), jnp.int32)
        for i in range(8):
            s = base + i
            codes = hist_ref[s % across, s // across, modes : modes + CODE_ROWS, :].astype(jnp.int32)[:8]
            tile = jnp.where(sub == i, codes, tile)
        tiles.append(tile)
    scales = code_scale(jnp.concatenate(tiles, axis=0).astype(jnp.float32))
    scales = jnp.concatenate([scales, jnp.zeros((128 - sources, 128), jnp.float32)], axis=0).T
    for s in range(sources):
        value = hist_ref[s % across, s // across, :modes, :].astype(jnp.int32).astype(jnp.float32)
        value = value * scales[:modes, s : s + 1]
        high = value.astype(jnp.bfloat16)
        low = (value - high.astype(jnp.float32)).astype(jnp.bfloat16)
        split_ref[s * modes : (s + 1) * modes, :steps] = high
        split_ref[s * modes : (s + 1) * modes, steps:] = low
    fetch_picks.wait()
    product(picks_ref, 1 - core, theirs_ref, split_ref, other_ref, fetches[0])
    for fetch in fetches[1]:
        fetch.wait()


def second_kernel(split_ref, mine_ref, plane_ref, picks_far, own_ref, coeffs_ref, picks_ref, rows_ref, picks_sem):
    fetch_picks = pltpu.make_async_copy(picks_far, picks_ref, picks_sem)
    fetch_picks.start()
    plane_rows(plane_ref[...], rows_ref, coeffs_ref)
    fetch_picks.wait()
    product(picks_ref, lax.axis_index("core"), mine_ref, split_ref, own_ref, [])


def far(x):
    return pltpu.with_memory_space_constraint(x, pltpu.HBM)


def recover(hist, coeff_blocks, picks, planes, groups):
    across, along, rows, steps = hist.shape
    blocks, picked, height, width = coeff_blocks.shape
    slabs = coeff_blocks.reshape(groups, blocks // groups, picked, height, width)
    half = jax.ShapeDtypeStruct((groups // 2, blocks // groups * height, steps), jnp.float32)
    half_slabs = (groups // 2,) + slabs.shape[1:]
    cost = pl.CostEstimate(
        flops=2 * blocks * picked * height * width * steps,
        bytes_accessed=blocks * picked * height * width,
        transcendentals=0,
    )
    near, away = pl.BlockSpec(memory_space=pltpu.VMEM), pl.BlockSpec(memory_space=pl.ANY)
    scratch = [pltpu.SMEM(picks.shape, picks.dtype)]
    other, split, mine = pl.pallas_call(
        first_kernel,
        out_shape=(
            half,
            jax.ShapeDtypeStruct((across * along * (rows - CODE_ROWS), 2 * steps), jnp.bfloat16),
            jax.ShapeDtypeStruct(half_slabs, slabs.dtype),
        ),
        in_specs=[near, away, away],
        out_specs=(near,) * 3,
        scratch_shapes=[pltpu.VMEM(half_slabs, slabs.dtype)]
        + scratch
        + [pltpu.SemaphoreType.DMA((2, groups // 2)), pltpu.SemaphoreType.DMA],
        compiler_params=pltpu.CompilerParams(vmem_limit_bytes=24 << 20),
        cost_estimate=cost,
        name="first",
    )(hist, far(picks), far(slabs))
    come = lax.ppermute(other, "core", [(0, 1), (1, 0)])
    own, coeffs = pl.pallas_call(
        second_kernel,
        out_shape=(half, jax.ShapeDtypeStruct((6 * planes.shape[0], 128), jnp.float32)),
        in_specs=[near, near, near, away],
        out_specs=(near,) * 2,
        scratch_shapes=scratch + [pltpu.VMEM((6 * planes.shape[0], 128), jnp.float32), pltpu.SemaphoreType.DMA],
        compiler_params=pltpu.CompilerParams(vmem_limit_bytes=24 << 20),
        cost_estimate=cost,
        name="second",
    )(split, mine, planes, far(picks))
    return own, come, coeffs


def pack_kernel(own_ref, come_ref, out_ref):
    groups, rows, steps = out_ref.shape
    rows -= CODE_ROWS
    tiles = rows // 128
    for g in range(groups):
        sums, largest = [], []
        for i in range(tiles):
            here = pl.ds(i * 128, 128)
            turned = (own_ref[g, here, :] + come_ref[g, here, :]).T
            sums.append(turned)
            largest.append(jnp.max(jnp.abs(turned), axis=0, keepdims=True))
        largest.append(jnp.zeros((8 - tiles, 128), jnp.float32))
        code = jnp.ceil(jnp.log2(jnp.maximum(jnp.concatenate(largest, axis=0), 1e-30)) * 32.0)
        out_ref[g, rows:, :] = code.astype(jnp.int32).astype(jnp.int16)
        inverse = jnp.exp2(code * (-1.0 / 32.0)) * LEVELS
        for i in range(tiles):
            whole = jnp.round(sums[i] * inverse[i : i + 1])
            out_ref[g, i * 128 : (i + 1) * 128, :] = whole.astype(jnp.int32).astype(jnp.int16)


def pack_sums(own, come):
    groups, rows, steps = own.shape
    return pl.pallas_call(
        pack_kernel,
        out_shape=jax.ShapeDtypeStruct((groups, rows + CODE_ROWS, steps), jnp.int16),
        in_specs=[pl.BlockSpec(memory_space=pltpu.VMEM)] * 2,
        out_specs=pl.BlockSpec(memory_space=pltpu.VMEM),
        compiler_params=pltpu.CompilerParams(vmem_limit_bytes=16 << 20),
        name="pack",
    )(own, come)


def plane_rows(planes, pad_ref, out_ref):
    looked, elements = planes.shape
    index = planes.astype(jnp.float32)
    height = (index + 0.5) * (1.0 / PLANES)
    azimuth = index * 2.399963229728653
    radius = jnp.sqrt(1.0 - height * height)
    normal_x = radius * jnp.cos(azimuth)
    normal_y = radius * jnp.sin(azimuth)
    coeffs = [
        normal_x * normal_x,
        normal_y * normal_y,
        height * height,
        2.0 * normal_x * normal_y,
        2.0 * normal_y * height,
        2.0 * normal_x * height,
    ]
    pad_ref[...] = jnp.zeros_like(pad_ref)
    lane = lax.broadcasted_iota(jnp.int32, (looked, 128), 1)
    for q, coeff in enumerate(coeffs):
        pad_ref[q * looked : (q + 1) * looked, :elements] = coeff
        left = pad_ref[q * looked : (q + 1) * looked, :]
        right = pltpu.roll(pltpu.roll(left, elements, 1), looked // 2, 0)
        out_ref[q * looked : (q + 1) * looked, :] = jnp.where(lane < elements, left, right)


def range_kernel(parts_ref, coeffs_ref, stress_ref, range_ref):
    groups, rows, steps = parts_ref.shape
    rows -= CODE_ROWS
    components, elements, steps = stress_ref.shape
    looked = range_ref.shape[0]
    scales = [code_scale(parts_ref[g, rows:, :].astype(jnp.int32).astype(jnp.float32)) for g in range(groups)]
    low = lax.broadcasted_iota(jnp.int32, (steps, 128), 1) < elements
    twice = []
    for i in range(rows // 128):
        total = None
        for g in range(groups):
            value = parts_ref[g, i * 128 : (i + 1) * 128, :].astype(jnp.int32).astype(jnp.float32)
            value = value * scales[g][i : i + 1]
            total = value if total is None else total + value
        upright = total.T
        stress_ref[2 * i] = upright[:elements]
        stress_ref[2 * i + 1] = upright[elements:]
        swapped = pltpu.roll(total, elements, 1)
        twice.append(jnp.where(low, total, swapped))
        twice.append(jnp.where(low, swapped, total))
    spreads = []
    for k in range(looked // 2):
        normal = coeffs_ref[k : k + 1, :] * twice[0]
        for q in range(1, components):
            normal = normal + coeffs_ref[q * looked + k : q * looked + k + 1, :] * twice[q]
        spreads.append(jnp.max(normal, axis=0, keepdims=True) - jnp.min(normal, axis=0, keepdims=True))
    spread = jnp.concatenate(spreads + spreads, axis=0)
    first = lax.broadcasted_iota(jnp.int32, (looked, 128), 0) < looked // 2
    range_ref[...] = jnp.where(first, spread, pltpu.roll(spread, elements, 1))[:, :elements]


def finish(parts, coeffs, looked):
    groups, rows, steps = parts.shape
    rows -= CODE_ROWS
    elements = 128 // 2
    stress, ranges = pl.pallas_call(
        range_kernel,
        out_shape=(
            jax.ShapeDtypeStruct((rows // elements, elements, steps), jnp.float32),
            jax.ShapeDtypeStruct((looked, elements), jnp.float32),
        ),
        in_specs=[pl.BlockSpec(memory_space=pltpu.VMEM)] * 2,
        out_specs=(pl.BlockSpec(memory_space=pltpu.VMEM),) * 2,
        compiler_params=pltpu.CompilerParams(vmem_limit_bytes=8 << 20),
        name="ranges",
    )(parts, coeffs)
    return stress, ranges.T


def gather_over(part, axes):
    copies = jnp.broadcast_to(part[None], (lax.axis_size(axes),) + part.shape)
    return lax.all_to_all(copies, axes, 0, 0)


def stage_kernel(owner_ref, whole_ref, *refs):
    count = (len(refs) - 3) // 2
    away, (half_ref, *near, tile_ref, sems) = refs[:count], refs[count:]
    rows = half_ref.shape[0]
    start = pl.multiple_of(lax.axis_index("core") * rows, rows)
    fetches = [pltpu.make_async_copy(whole_ref.at[pl.ds(start, rows)], half_ref, sems.at[count])]
    fetches += [pltpu.make_async_copy(a, b, sems.at[i]) for i, (a, b) in enumerate(zip(away, near))]
    for fetch in fetches:
        fetch.start()
    tile_ref[...] = jnp.full(tile_ref.shape, owner_ref[0], jnp.int32)
    for fetch in fetches:
        fetch.wait()


def stage(owner, whole, *others):
    channels, steps = whole.shape
    copied = [jax.ShapeDtypeStruct((channels // 2, steps), whole.dtype)]
    copied += [jax.ShapeDtypeStruct(x.shape, x.dtype) for x in others]
    return pl.pallas_call(
        stage_kernel,
        out_shape=(*copied, jax.ShapeDtypeStruct((8, 128), jnp.int32)),
        in_specs=[pl.BlockSpec(memory_space=pltpu.SMEM)] + [pl.BlockSpec(memory_space=pl.ANY)] * len(copied),
        out_specs=(pl.BlockSpec(memory_space=pltpu.VMEM),) * (1 + len(copied)),
        scratch_shapes=[pltpu.SemaphoreType.DMA((len(copied),))],
        compiler_params=pltpu.CompilerParams(vmem_limit_bytes=8 << 20),
        name="stage",
    )(owner, *(far(x) for x in (whole, *others)))


def pick_kernel(shift, tile_ref, offered_ref, out_ref):
    owner = jnp.max(tile_ref[...])
    piece = offered_ref[lax.rem(lax.shift_right_logical(owner, shift), offered_ref.shape[0])]
    for i in range(out_ref.shape[0]):
        out_ref[i] = piece


def pick_piece(offered, tile, shift, count):
    return pl.pallas_call(
        functools.partial(pick_kernel, shift),
        out_shape=jax.ShapeDtypeStruct((count,) + offered.shape[1:], offered.dtype),
        in_specs=[pl.BlockSpec(memory_space=pltpu.VMEM)] * 2,
        out_specs=pl.BlockSpec(memory_space=pltpu.VMEM),
        compiler_params=pltpu.CompilerParams(vmem_limit_bytes=8 << 20),
        name="pick",
    )(tile, offered)


def fetch_window(half, tile, owner):
    plane, along = lax.axis_size(ROW[1:]), lax.axis_size(ROW[0])
    shift = plane.bit_length() - 1
    near = ("core",) + ROW[1:]

    def scatter(pieces, tile):
        return pick_piece(lax.all_to_all(pieces, ROW[1:], 0, 0), tile, 0, along)

    pieces = half.reshape(plane, half.shape[0] // plane, half.shape[1])
    mine = lax.axis_index(ROW[0]) == lax.shift_right_logical(owner, shift)
    copies = lax.cond(mine, scatter, lambda pieces, tile: pieces, pieces, tile)
    offered = lax.all_to_all(copies, ROW[0], 0, 0)
    window = lax.all_to_all(pick_piece(offered, tile, shift, lax.axis_size(near)), near, 0, 0)
    return window.reshape(-1, half.shape[1])


def body(load_windows, owner_id, participation, frequency, damping, recovery, pattern, plane_table):
    planes = plane_table[0, 0].T
    half, part, rates, decays, planes, tile = stage(
        owner_id, load_windows[0], participation, frequency[None], damping[None], planes
    )
    window = fetch_window(half, tile, owner_id[0])
    copies = make_history(window, part, rates, decays, lax.axis_size(ROW[:2]))
    column = lax.all_to_all(copies, ROW[:2], 0, 0)
    hist = gather_over(column, ROW[2])
    own, come, coeffs = recover(hist, recovery[0, 0], pattern[0, 0].T, planes, lax.axis_size(("yh", "core")))
    parts = lax.all_to_all(pack_sums(own, come), "yh", 0, 0)
    stress, plane_range = finish(parts, coeffs, planes.shape[0])
    return (stress[None, None], plane_range[None, None])


def solution(mesh):
    fine = Mesh(mesh.devices.reshape(4, 2, 8, 2, 4), ("yh", "core") + ROW)
    mode = ("yh", "core")
    placed = (
        P(ROW, None, None),
        P(),
        P(mode + ROW, None),
        P(mode + ROW),
        P(mode + ROW),
        P(mode, ROW, None, None, None, None),
        P(mode, ROW, None, None),
        P(ROW, mode, None, None),
    )
    return jax.shard_map(
        body,
        mesh=fine,
        in_specs=placed,
        out_specs=(P(ROW, mode, None, None, None), P(ROW, mode, None, None)),
        check_vma=False,
    )
```

```python
import functools

import jax
import jax.numpy as jnp
from jax import lax
from jax.experimental import pallas as pl
from jax.experimental.pallas import tpu as pltpu
from jax.sharding import Mesh
from jax.sharding import PartitionSpec as P

ROW = ("z", "yl", "x")
FIRST, THEN = ROW[:1], ROW[1:]
CODE_ROWS = 8
LEVELS = 32760.0
PLANES = 64


def code_scale(code):
    return jnp.exp2(code * (1.0 / 32.0)) * (1.0 / LEVELS)


def quantize(values):
    largest = jnp.max(jnp.abs(values), axis=-1, keepdims=True)
    code = jnp.ceil(jnp.log2(jnp.maximum(largest, 1e-30)) * 32.0)
    inverse = jnp.exp2(code * (-1.0 / 32.0)) * LEVELS
    whole = jnp.round(values * inverse).astype(jnp.int32)
    return whole, code


def as_row(column):
    n = column.shape[0]
    at = lax.broadcasted_iota(jnp.int32, (n, 128), 0) == lax.broadcasted_iota(jnp.int32, (n, 128), 1)
    return jnp.sum(jnp.where(at, column, 0.0), axis=0, keepdims=True)


def mode_table(rates, decays, rows_ref):
    modes = rates.shape[1]
    shifts = (1 << lax.broadcasted_iota(jnp.int32, (8, modes), 0)).astype(jnp.float32)
    angle = rates * shifts
    cos, sin = jnp.cos(angle), jnp.sin(angle)
    shrink = jnp.exp(-decays * rates * shifts)
    rows_ref[0:8, :modes] = shrink * cos
    rows_ref[8:16, :modes] = shrink * sin
    rows_ref[16:24, :modes] = rates * jnp.broadcast_to(sin[0:1], (8, modes))
    rows_ref[24:32, :modes] = rates * jnp.broadcast_to(cos[0:1], (8, modes))
    return rows_ref[...].T[:modes]


def history_kernel(window_ref, *refs):
    away, (out_ref, *near, rows_ref, sems) = refs[:3], refs[3:]
    fetches = [pltpu.make_async_copy(a, b, sems.at[i]) for i, (a, b) in enumerate(zip(away, near))]
    for fetch in fetches:
        fetch.start()
    part_ref, rate_ref, decay_ref = near
    fetches[1].wait()
    fetches[2].wait()
    table = mode_table(rate_ref[...], decay_ref[...], rows_ref)
    fetches[0].wait()
    forces = jnp.dot(part_ref[...], window_ref[...], preferred_element_type=jnp.float32)
    modes, steps = forces.shape
    doublings = steps.bit_length() - 1
    lane = lax.broadcasted_iota(jnp.int32, forces.shape, 1)
    re, im = forces, jnp.zeros_like(forces)
    for d in range(doublings):
        shift = 1 << d
        p_re, p_im = table[:, d : d + 1], table[:, 8 + d : 9 + d]
        keep = lane >= shift
        old_re = jnp.where(keep, pltpu.roll(re, shift, 1), 0.0)
        if d == 0:
            re, im = re + p_re * old_re, p_im * old_re
            continue
        old_im = jnp.where(keep, pltpu.roll(im, shift, 1), 0.0)
        re, im = re + p_re * old_re - p_im * old_im, im + p_re * old_im + p_im * old_re
    hist = table[:, 16:17] * re + table[:, 24:25] * im
    whole, code = quantize(hist)
    codes = jnp.broadcast_to(as_row(code), (CODE_ROWS, 128)).astype(jnp.int32)
    block = jnp.concatenate([whole, codes], axis=0).astype(jnp.int16)
    for i in range(out_ref.shape[0]):
        out_ref[i] = block


def make_history(window, participation, frequency, damping, count):
    modes, channels = participation.shape
    steps = window.shape[1]
    return pl.pallas_call(
        history_kernel,
        out_shape=jax.ShapeDtypeStruct((count, modes + CODE_ROWS, steps), jnp.int16),
        in_specs=[pl.BlockSpec(memory_space=pltpu.VMEM)] + [pl.BlockSpec(memory_space=pl.ANY)] * 3,
        out_specs=pl.BlockSpec(memory_space=pltpu.VMEM),
        scratch_shapes=[
            pltpu.VMEM(participation.shape, participation.dtype),
            pltpu.VMEM(frequency.shape, frequency.dtype),
            pltpu.VMEM(damping.shape, damping.dtype),
            pltpu.VMEM((128, 128), jnp.float32),
            pltpu.SemaphoreType.DMA((3,)),
        ],
        compiler_params=pltpu.CompilerParams(vmem_limit_bytes=16 << 20),
        cost_estimate=pl.CostEstimate(
            flops=2 * modes * channels * steps, bytes_accessed=2 * (channels * (modes + steps)), transcendentals=0
        ),
        name="history",
    )(window, *(far(x) for x in (participation, frequency, damping)))


def product(picks_ref, side, coeff_ref, split_ref, out_ref, fetches):
    groups, per_slab, picked, height, width = coeff_ref.shape
    steps = out_ref.shape[2]
    for g in range(groups):
        if fetches:
            fetches[g].wait()
        for r in range(per_slab):
            block = (2 * g + side) * per_slab + r
            left = jnp.concatenate([coeff_ref[g, r, k] for k in range(picked)], axis=1)
            starts = [pl.multiple_of(picks_ref[k, block] * width, width) for k in range(picked)]
            right = jnp.concatenate([split_ref[pl.ds(start, width), :] for start in starts], axis=0)
            both = jnp.dot(left, right, preferred_element_type=jnp.float32)
            out_ref[g, r * height : (r + 1) * height, :] = both[:, :steps] + both[:, steps:]


def first_kernel(hist_ref, picks_far, far_ref, other_ref, split_ref, mine_ref, theirs_ref, picks_ref, sems, picks_sem):
    core = lax.axis_index("core")
    groups = mine_ref.shape[0]
    fetches = [[], []]
    fetch_picks = pltpu.make_async_copy(picks_far, picks_ref, picks_sem)
    fetch_picks.start()
    for i, (near, side) in enumerate([(theirs_ref, 1 - core), (mine_ref, core)]):
        for g in range(groups):
            fetch = pltpu.make_async_copy(far_ref.at[2 * g + side], near.at[g], sems.at[i, g])
            fetch.start()
            fetches[i].append(fetch)
    across, along, rows, steps = hist_ref.shape
    sources = across * along
    modes = rows - CODE_ROWS
    sub = lax.broadcasted_iota(jnp.int32, (8, 128), 0)
    tiles = []
    for base in range(0, sources, 8):
        tile = jnp.zeros((8, 128), jnp.int32)
        for i in range(8):
            s = base + i
            codes = hist_ref[s % across, s // across, modes : modes + CODE_ROWS, :].astype(jnp.int32)[:8]
            tile = jnp.where(sub == i, codes, tile)
        tiles.append(tile)
    scales = code_scale(jnp.concatenate(tiles, axis=0).astype(jnp.float32))
    scales = jnp.concatenate([scales, jnp.zeros((128 - sources, 128), jnp.float32)], axis=0).T
    for s in range(sources):
        value = hist_ref[s % across, s // across, :modes, :].astype(jnp.int32).astype(jnp.float32)
        value = value * scales[:modes, s : s + 1]
        high = value.astype(jnp.bfloat16)
        low = (value - high.astype(jnp.float32)).astype(jnp.bfloat16)
        split_ref[s * modes : (s + 1) * modes, :steps] = high
        split_ref[s * modes : (s + 1) * modes, steps:] = low
    fetch_picks.wait()
    product(picks_ref, 1 - core, theirs_ref, split_ref, other_ref, fetches[0])
    for fetch in fetches[1]:
        fetch.wait()


def second_kernel(
    split_ref, mine_ref, planes_far, picks_far, own_ref, coeffs_ref, picks_ref, plane_ref, rows_ref, picks_sem, planes_sem
):
    fetch_picks = pltpu.make_async_copy(picks_far, picks_ref, picks_sem)
    fetch_planes = pltpu.make_async_copy(planes_far, plane_ref, planes_sem)
    fetch_picks.start()
    fetch_planes.start()
    fetch_planes.wait()
    plane_rows(plane_ref[...], rows_ref, coeffs_ref)
    fetch_picks.wait()
    product(picks_ref, lax.axis_index("core"), mine_ref, split_ref, own_ref, [])


def far(x):
    return pltpu.with_memory_space_constraint(x, pltpu.HBM)


def recover(hist, coeff_blocks, picks, planes, groups):
    across, along, rows, steps = hist.shape
    blocks, picked, height, width = coeff_blocks.shape
    slabs = coeff_blocks.reshape(groups, blocks // groups, picked, height, width)
    half = jax.ShapeDtypeStruct((groups // 2, blocks // groups * height, steps), jnp.float32)
    half_slabs = (groups // 2,) + slabs.shape[1:]
    cost = pl.CostEstimate(
        flops=2 * blocks * picked * height * width * steps,
        bytes_accessed=blocks * picked * height * width,
        transcendentals=0,
    )
    near, away = pl.BlockSpec(memory_space=pltpu.VMEM), pl.BlockSpec(memory_space=pl.ANY)
    scratch = [pltpu.SMEM(picks.shape, picks.dtype)]
    other, split, mine = pl.pallas_call(
        first_kernel,
        out_shape=(
            half,
            jax.ShapeDtypeStruct((across * along * (rows - CODE_ROWS), 2 * steps), jnp.bfloat16),
            jax.ShapeDtypeStruct(half_slabs, slabs.dtype),
        ),
        in_specs=[near, away, away],
        out_specs=(near,) * 3,
        scratch_shapes=[pltpu.VMEM(half_slabs, slabs.dtype)]
        + scratch
        + [pltpu.SemaphoreType.DMA((2, groups // 2)), pltpu.SemaphoreType.DMA],
        compiler_params=pltpu.CompilerParams(vmem_limit_bytes=24 << 20),
        cost_estimate=cost,
        name="first",
    )(hist, far(picks), far(slabs))
    come = lax.ppermute(other, "core", [(0, 1), (1, 0)])
    own, coeffs = pl.pallas_call(
        second_kernel,
        out_shape=(half, jax.ShapeDtypeStruct((6 * planes.shape[0], 128), jnp.float32)),
        in_specs=[near, near, away, away],
        out_specs=(near,) * 2,
        scratch_shapes=scratch
        + [
            pltpu.VMEM(planes.shape, planes.dtype),
            pltpu.VMEM((6 * planes.shape[0], 128), jnp.float32),
            pltpu.SemaphoreType.DMA,
            pltpu.SemaphoreType.DMA,
        ],
        compiler_params=pltpu.CompilerParams(vmem_limit_bytes=24 << 20),
        cost_estimate=cost,
        name="second",
    )(split, mine, far(planes), far(picks))
    return own, come, coeffs


def pack_kernel(own_ref, come_ref, out_ref):
    groups, rows, steps = out_ref.shape
    rows -= CODE_ROWS
    tiles = rows // 128
    for g in range(groups):
        sums, largest = [], []
        for i in range(tiles):
            here = pl.ds(i * 128, 128)
            turned = (own_ref[g, here, :] + come_ref[g, here, :]).T
            sums.append(turned)
            largest.append(jnp.max(jnp.abs(turned), axis=0, keepdims=True))
        largest.append(jnp.zeros((8 - tiles, 128), jnp.float32))
        code = jnp.ceil(jnp.log2(jnp.maximum(jnp.concatenate(largest, axis=0), 1e-30)) * 32.0)
        out_ref[g, rows:, :] = code.astype(jnp.int32).astype(jnp.int16)
        inverse = jnp.exp2(code * (-1.0 / 32.0)) * LEVELS
        for i in range(tiles):
            whole = jnp.round(sums[i] * inverse[i : i + 1])
            out_ref[g, i * 128 : (i + 1) * 128, :] = whole.astype(jnp.int32).astype(jnp.int16)


def pack_sums(own, come):
    groups, rows, steps = own.shape
    return pl.pallas_call(
        pack_kernel,
        out_shape=jax.ShapeDtypeStruct((groups, rows + CODE_ROWS, steps), jnp.int16),
        in_specs=[pl.BlockSpec(memory_space=pltpu.VMEM)] * 2,
        out_specs=pl.BlockSpec(memory_space=pltpu.VMEM),
        compiler_params=pltpu.CompilerParams(vmem_limit_bytes=16 << 20),
        name="pack",
    )(own, come)


def plane_rows(planes, pad_ref, out_ref):
    looked, elements = planes.shape
    index = planes.astype(jnp.float32)
    height = (index + 0.5) * (1.0 / PLANES)
    azimuth = index * 2.399963229728653
    radius = jnp.sqrt(1.0 - height * height)
    normal_x = radius * jnp.cos(azimuth)
    normal_y = radius * jnp.sin(azimuth)
    coeffs = [
        normal_x * normal_x,
        normal_y * normal_y,
        height * height,
        2.0 * normal_x * normal_y,
        2.0 * normal_y * height,
        2.0 * normal_x * height,
    ]
    pad_ref[...] = jnp.zeros_like(pad_ref)
    lane = lax.broadcasted_iota(jnp.int32, (looked, 128), 1)
    for q, coeff in enumerate(coeffs):
        pad_ref[q * looked : (q + 1) * looked, :elements] = coeff
        left = pad_ref[q * looked : (q + 1) * looked, :]
        right = pltpu.roll(pltpu.roll(left, elements, 1), looked // 2, 0)
        out_ref[q * looked : (q + 1) * looked, :] = jnp.where(lane < elements, left, right)


def range_kernel(parts_ref, coeffs_ref, stress_ref, range_ref):
    groups, rows, steps = parts_ref.shape
    rows -= CODE_ROWS
    components, elements, steps = stress_ref.shape
    looked = range_ref.shape[0]
    scales = [code_scale(parts_ref[g, rows:, :].astype(jnp.int32).astype(jnp.float32)) for g in range(groups)]
    low = lax.broadcasted_iota(jnp.int32, (steps, 128), 1) < elements
    twice = []
    for i in range(rows // 128):
        total = None
        for g in range(groups):
            value = parts_ref[g, i * 128 : (i + 1) * 128, :].astype(jnp.int32).astype(jnp.float32)
            value = value * scales[g][i : i + 1]
            total = value if total is None else total + value
        upright = total.T
        stress_ref[2 * i] = upright[:elements]
        stress_ref[2 * i + 1] = upright[elements:]
        swapped = pltpu.roll(total, elements, 1)
        twice.append(jnp.where(low, total, swapped))
        twice.append(jnp.where(low, swapped, total))
    spreads = []
    for k in range(looked // 2):
        normal = coeffs_ref[k : k + 1, :] * twice[0]
        for q in range(1, components):
            normal = normal + coeffs_ref[q * looked + k : q * looked + k + 1, :] * twice[q]
        spreads.append(jnp.max(normal, axis=0, keepdims=True) - jnp.min(normal, axis=0, keepdims=True))
    spread = jnp.concatenate(spreads + spreads, axis=0)
    first = lax.broadcasted_iota(jnp.int32, (looked, 128), 0) < looked // 2
    range_ref[...] = jnp.where(first, spread, pltpu.roll(spread, elements, 1))[:, :elements]


def finish(parts, coeffs, looked):
    groups, rows, steps = parts.shape
    rows -= CODE_ROWS
    elements = 128 // 2
    stress, ranges = pl.pallas_call(
        range_kernel,
        out_shape=(
            jax.ShapeDtypeStruct((rows // elements, elements, steps), jnp.float32),
            jax.ShapeDtypeStruct((looked, elements), jnp.float32),
        ),
        in_specs=[pl.BlockSpec(memory_space=pltpu.VMEM)] * 2,
        out_specs=(pl.BlockSpec(memory_space=pltpu.VMEM),) * 2,
        compiler_params=pltpu.CompilerParams(vmem_limit_bytes=8 << 20),
        name="ranges",
    )(parts, coeffs)
    return stress, ranges.T


def gather_over(part, axes):
    copies = jnp.broadcast_to(part[None], (lax.axis_size(axes),) + part.shape)
    return lax.all_to_all(copies, axes, 0, 0)


def half_kernel(whole_ref, half_ref, sem):
    rows = half_ref.shape[0]
    start = pl.multiple_of(lax.axis_index("core") * rows, rows)
    fetch = pltpu.make_async_copy(whole_ref.at[pl.ds(start, rows)], half_ref, sem)
    fetch.start()
    fetch.wait()


def take_half(whole):
    channels, steps = whole.shape
    return pl.pallas_call(
        half_kernel,
        out_shape=jax.ShapeDtypeStruct((channels // 2, steps), whole.dtype),
        in_specs=[pl.BlockSpec(memory_space=pl.ANY)],
        out_specs=pl.BlockSpec(memory_space=pltpu.VMEM),
        scratch_shapes=[pltpu.SemaphoreType.DMA],
        compiler_params=pltpu.CompilerParams(vmem_limit_bytes=8 << 20),
        name="half",
    )(far(whole))


def pick_kernel(shift, owner_ref, offered_ref, out_ref):
    piece = offered_ref[lax.rem(lax.shift_right_logical(owner_ref[0], shift), offered_ref.shape[0])]
    for i in range(out_ref.shape[0]):
        out_ref[i] = piece


def pick_piece(offered, owner, shift, count):
    return pl.pallas_call(
        functools.partial(pick_kernel, shift),
        out_shape=jax.ShapeDtypeStruct((count,) + offered.shape[1:], offered.dtype),
        in_specs=[pl.BlockSpec(memory_space=pltpu.SMEM), pl.BlockSpec(memory_space=pltpu.VMEM)],
        out_specs=pl.BlockSpec(memory_space=pltpu.VMEM),
        compiler_params=pltpu.CompilerParams(vmem_limit_bytes=8 << 20),
        name="pick",
    )(owner, offered)


def fetch_window(whole, owner):
    channels, steps = whole.shape
    plane, along = lax.axis_size(ROW[1:]), lax.axis_size(ROW[0])
    shift = plane.bit_length() - 1
    rows = channels // 2 // plane

    def scatter(whole, owner):
        pieces = take_half(whole).reshape(plane, rows, steps)
        return pick_piece(lax.all_to_all(pieces, ROW[1:], 0, 0), owner, 0, along)

    def nothing(whole, owner):
        return jnp.zeros((along, rows, steps), whole.dtype)

    mine = lax.axis_index(ROW[0]) == lax.shift_right_logical(owner[0], shift)
    offered = lax.all_to_all(lax.cond(mine, scatter, nothing, whole, owner), ROW[0], 0, 0)
    whole_half = lax.all_to_all(pick_piece(offered, owner, shift, plane), ROW[1:], 0, 0)
    return lax.all_gather(whole_half.reshape(plane * rows, steps), "core", axis=0, tiled=True)


def body(load_windows, owner_id, participation, frequency, damping, recovery, pattern, plane_table):
    planes = plane_table[0, 0].T
    window = fetch_window(load_windows[0], owner_id)
    copies = make_history(window, participation, frequency[None], damping[None], lax.axis_size(FIRST))
    column = lax.all_to_all(copies, FIRST, 0, 0)
    hist = gather_over(column, THEN)
    own, come, coeffs = recover(hist, recovery[0, 0], pattern[0, 0].T, planes, lax.axis_size(("yh", "core")))
    parts = lax.all_to_all(pack_sums(own, come), "yh", 0, 0)
    stress, plane_range = finish(parts, coeffs, planes.shape[0])
    return (stress[None, None], plane_range[None, None])


def solution(mesh):
    fine = Mesh(mesh.devices.reshape(4, 2, 8, 2, 4), ("yh", "core") + ROW)
    mode = ("yh", "core")
    placed = (
        P(ROW, None, None),
        P(),
        P(mode + ROW, None),
        P(mode + ROW),
        P(mode + ROW),
        P(mode, ROW, None, None, None, None),
        P(mode, ROW, None, None),
        P(ROW, mode, None, None),
    )
    return jax.shard_map(
        body,
        mesh=fine,
        in_specs=placed,
        out_specs=(P(ROW, mode, None, None, None), P(ROW, mode, None, None)),
        check_vma=False,
    )
```

```python
import functools

import jax
import jax.numpy as jnp
from jax import lax
from jax.experimental import pallas as pl
from jax.experimental.pallas import tpu as pltpu
from jax.sharding import Mesh
from jax.sharding import PartitionSpec as P

ROW = ("z", "yl", "x")
FIRST, THEN = ROW[:1], ROW[1:]
CODE_ROWS = 8
LEVELS = 32760.0
PLANES = 64


def code_scale(code):
    return jnp.exp2(code * (1.0 / 32.0)) * (1.0 / LEVELS)


def quantize(values):
    largest = jnp.max(jnp.abs(values), axis=-1, keepdims=True)
    code = jnp.ceil(jnp.log2(jnp.maximum(largest, 1e-30)) * 32.0)
    inverse = jnp.exp2(code * (-1.0 / 32.0)) * LEVELS
    whole = jnp.round(values * inverse).astype(jnp.int32)
    return whole, code


def as_row(column):
    n = column.shape[0]
    at = lax.broadcasted_iota(jnp.int32, (n, 128), 0) == lax.broadcasted_iota(jnp.int32, (n, 128), 1)
    return jnp.sum(jnp.where(at, column, 0.0), axis=0, keepdims=True)


def mode_table(rates, decays, rows_ref):
    modes = rates.shape[1]
    shifts = (1 << lax.broadcasted_iota(jnp.int32, (8, modes), 0)).astype(jnp.float32)
    angle = rates * shifts
    cos, sin = jnp.cos(angle), jnp.sin(angle)
    shrink = jnp.exp(-decays * rates * shifts)
    rows_ref[0:8, :modes] = shrink * cos
    rows_ref[8:16, :modes] = shrink * sin
    rows_ref[16:24, :modes] = rates * jnp.broadcast_to(sin[0:1], (8, modes))
    rows_ref[24:32, :modes] = rates * jnp.broadcast_to(cos[0:1], (8, modes))
    return rows_ref[...].T[:modes]


def history_kernel(window_ref, *refs):
    part_ref, rate_ref, decay_ref, out_ref, rows_ref = refs
    table = mode_table(rate_ref[...], decay_ref[...], rows_ref)
    forces = jnp.dot(part_ref[...], window_ref[...], preferred_element_type=jnp.float32)
    modes, steps = forces.shape
    doublings = steps.bit_length() - 1
    lane = lax.broadcasted_iota(jnp.int32, forces.shape, 1)
    re, im = forces, jnp.zeros_like(forces)
    for d in range(doublings):
        shift = 1 << d
        p_re, p_im = table[:, d : d + 1], table[:, 8 + d : 9 + d]
        keep = lane >= shift
        old_re = jnp.where(keep, pltpu.roll(re, shift, 1), 0.0)
        if d == 0:
            re, im = re + p_re * old_re, p_im * old_re
            continue
        old_im = jnp.where(keep, pltpu.roll(im, shift, 1), 0.0)
        re, im = re + p_re * old_re - p_im * old_im, im + p_re * old_im + p_im * old_re
    hist = table[:, 16:17] * re + table[:, 24:25] * im
    whole, code = quantize(hist)
    codes = jnp.broadcast_to(as_row(code), (CODE_ROWS, 128)).astype(jnp.int32)
    block = jnp.concatenate([whole, codes], axis=0).astype(jnp.int16)
    for i in range(out_ref.shape[0]):
        out_ref[i] = block


def make_history(window, participation, frequency, damping, count):
    modes, channels = participation.shape
    steps = window.shape[1]
    return pl.pallas_call(
        history_kernel,
        out_shape=jax.ShapeDtypeStruct((count, modes + CODE_ROWS, steps), jnp.int16),
        in_specs=[pl.BlockSpec(memory_space=pltpu.VMEM)] * 4,
        out_specs=pl.BlockSpec(memory_space=pltpu.VMEM),
        scratch_shapes=[pltpu.VMEM((128, 128), jnp.float32)],
        compiler_params=pltpu.CompilerParams(vmem_limit_bytes=16 << 20),
        cost_estimate=pl.CostEstimate(
            flops=2 * modes * channels * steps, bytes_accessed=2 * (channels * (modes + steps)), transcendentals=0
        ),
        name="history",
    )(window, participation, frequency, damping)


def product(picks_ref, side, coeff_ref, split_ref, out_ref, fetches):
    groups, per_slab, picked, height, width = coeff_ref.shape
    steps = out_ref.shape[2]
    for g in range(groups):
        if fetches:
            fetches[g].wait()
        for r in range(per_slab):
            block = (2 * g + side) * per_slab + r
            left = jnp.concatenate([coeff_ref[g, r, k] for k in range(picked)], axis=1)
            starts = [pl.multiple_of(picks_ref[k, block] * width, width) for k in range(picked)]
            right = jnp.concatenate([split_ref[pl.ds(start, width), :] for start in starts], axis=0)
            both = jnp.dot(left, right, preferred_element_type=jnp.float32)
            out_ref[g, r * height : (r + 1) * height, :] = both[:, :steps] + both[:, steps:]


def first_kernel(hist_ref, picks_far, far_ref, other_ref, split_ref, mine_ref, theirs_ref, picks_ref, sems, picks_sem):
    core = lax.axis_index("core")
    groups = mine_ref.shape[0]
    fetches = [[], []]
    fetch_picks = pltpu.make_async_copy(picks_far, picks_ref, picks_sem)
    fetch_picks.start()
    for i, (near, side) in enumerate([(theirs_ref, 1 - core), (mine_ref, core)]):
        for g in range(groups):
            fetch = pltpu.make_async_copy(far_ref.at[2 * g + side], near.at[g], sems.at[i, g])
            fetch.start()
            fetches[i].append(fetch)
    across, along, rows, steps = hist_ref.shape
    sources = across * along
    modes = rows - CODE_ROWS
    sub = lax.broadcasted_iota(jnp.int32, (8, 128), 0)
    tiles = []
    for base in range(0, sources, 8):
        tile = jnp.zeros((8, 128), jnp.int32)
        for i in range(8):
            s = base + i
            codes = hist_ref[s % across, s // across, modes : modes + CODE_ROWS, :].astype(jnp.int32)[:8]
            tile = jnp.where(sub == i, codes, tile)
        tiles.append(tile)
    scales = code_scale(jnp.concatenate(tiles, axis=0).astype(jnp.float32))
    scales = jnp.concatenate([scales, jnp.zeros((128 - sources, 128), jnp.float32)], axis=0).T
    for s in range(sources):
        value = hist_ref[s % across, s // across, :modes, :].astype(jnp.int32).astype(jnp.float32)
        value = value * scales[:modes, s : s + 1]
        high = value.astype(jnp.bfloat16)
        low = (value - high.astype(jnp.float32)).astype(jnp.bfloat16)
        split_ref[s * modes : (s + 1) * modes, :steps] = high
        split_ref[s * modes : (s + 1) * modes, steps:] = low
    fetch_picks.wait()
    product(picks_ref, 1 - core, theirs_ref, split_ref, other_ref, fetches[0])
    for fetch in fetches[1]:
        fetch.wait()


def second_kernel(
    split_ref, mine_ref, planes_far, picks_far, own_ref, coeffs_ref, picks_ref, plane_ref, rows_ref, picks_sem, planes_sem
):
    fetch_picks = pltpu.make_async_copy(picks_far, picks_ref, picks_sem)
    fetch_planes = pltpu.make_async_copy(planes_far, plane_ref, planes_sem)
    fetch_picks.start()
    fetch_planes.start()
    fetch_planes.wait()
    plane_rows(plane_ref[...], rows_ref, coeffs_ref)
    fetch_picks.wait()
    product(picks_ref, lax.axis_index("core"), mine_ref, split_ref, own_ref, [])


def far(x):
    return pltpu.with_memory_space_constraint(x, pltpu.HBM)


def recover(hist, coeff_blocks, picks, planes, groups):
    across, along, rows, steps = hist.shape
    blocks, picked, height, width = coeff_blocks.shape
    slabs = coeff_blocks.reshape(groups, blocks // groups, picked, height, width)
    half = jax.ShapeDtypeStruct((groups // 2, blocks // groups * height, steps), jnp.float32)
    half_slabs = (groups // 2,) + slabs.shape[1:]
    cost = pl.CostEstimate(
        flops=2 * blocks * picked * height * width * steps,
        bytes_accessed=blocks * picked * height * width,
        transcendentals=0,
    )
    near, away = pl.BlockSpec(memory_space=pltpu.VMEM), pl.BlockSpec(memory_space=pl.ANY)
    scratch = [pltpu.SMEM(picks.shape, picks.dtype)]
    other, split, mine = pl.pallas_call(
        first_kernel,
        out_shape=(
            half,
            jax.ShapeDtypeStruct((across * along * (rows - CODE_ROWS), 2 * steps), jnp.bfloat16),
            jax.ShapeDtypeStruct(half_slabs, slabs.dtype),
        ),
        in_specs=[near, away, away],
        out_specs=(near,) * 3,
        scratch_shapes=[pltpu.VMEM(half_slabs, slabs.dtype)]
        + scratch
        + [pltpu.SemaphoreType.DMA((2, groups // 2)), pltpu.SemaphoreType.DMA],
        compiler_params=pltpu.CompilerParams(vmem_limit_bytes=24 << 20),
        cost_estimate=cost,
        name="first",
    )(hist, far(picks), far(slabs))
    come = lax.ppermute(other, "core", [(0, 1), (1, 0)])
    own, coeffs = pl.pallas_call(
        second_kernel,
        out_shape=(half, jax.ShapeDtypeStruct((6 * planes.shape[0], 128), jnp.float32)),
        in_specs=[near, near, away, away],
        out_specs=(near,) * 2,
        scratch_shapes=scratch
        + [
            pltpu.VMEM(planes.shape, planes.dtype),
            pltpu.VMEM((6 * planes.shape[0], 128), jnp.float32),
            pltpu.SemaphoreType.DMA,
            pltpu.SemaphoreType.DMA,
        ],
        compiler_params=pltpu.CompilerParams(vmem_limit_bytes=24 << 20),
        cost_estimate=cost,
        name="second",
    )(split, mine, far(planes), far(picks))
    return own, come, coeffs


def pack_kernel(own_ref, come_ref, out_ref):
    groups, rows, steps = out_ref.shape
    rows -= CODE_ROWS
    tiles = rows // 128
    for g in range(groups):
        sums, largest = [], []
        for i in range(tiles):
            here = pl.ds(i * 128, 128)
            turned = (own_ref[g, here, :] + come_ref[g, here, :]).T
            sums.append(turned)
            largest.append(jnp.max(jnp.abs(turned), axis=0, keepdims=True))
        largest.append(jnp.zeros((8 - tiles, 128), jnp.float32))
        code = jnp.ceil(jnp.log2(jnp.maximum(jnp.concatenate(largest, axis=0), 1e-30)) * 32.0)
        out_ref[g, rows:, :] = code.astype(jnp.int32).astype(jnp.int16)
        inverse = jnp.exp2(code * (-1.0 / 32.0)) * LEVELS
        for i in range(tiles):
            whole = jnp.round(sums[i] * inverse[i : i + 1])
            out_ref[g, i * 128 : (i + 1) * 128, :] = whole.astype(jnp.int32).astype(jnp.int16)


def pack_sums(own, come):
    groups, rows, steps = own.shape
    return pl.pallas_call(
        pack_kernel,
        out_shape=jax.ShapeDtypeStruct((groups, rows + CODE_ROWS, steps), jnp.int16),
        in_specs=[pl.BlockSpec(memory_space=pltpu.VMEM)] * 2,
        out_specs=pl.BlockSpec(memory_space=pltpu.VMEM),
        compiler_params=pltpu.CompilerParams(vmem_limit_bytes=16 << 20),
        name="pack",
    )(own, come)


def plane_rows(planes, pad_ref, out_ref):
    looked, elements = planes.shape
    index = planes.astype(jnp.float32)
    height = (index + 0.5) * (1.0 / PLANES)
    azimuth = index * 2.399963229728653
    radius = jnp.sqrt(1.0 - height * height)
    normal_x = radius * jnp.cos(azimuth)
    normal_y = radius * jnp.sin(azimuth)
    coeffs = [
        normal_x * normal_x,
        normal_y * normal_y,
        height * height,
        2.0 * normal_x * normal_y,
        2.0 * normal_y * height,
        2.0 * normal_x * height,
    ]
    pad_ref[...] = jnp.zeros_like(pad_ref)
    lane = lax.broadcasted_iota(jnp.int32, (looked, 128), 1)
    for q, coeff in enumerate(coeffs):
        pad_ref[q * looked : (q + 1) * looked, :elements] = coeff
        left = pad_ref[q * looked : (q + 1) * looked, :]
        right = pltpu.roll(pltpu.roll(left, elements, 1), looked // 2, 0)
        out_ref[q * looked : (q + 1) * looked, :] = jnp.where(lane < elements, left, right)


def range_kernel(parts_ref, coeffs_ref, stress_ref, range_ref):
    groups, rows, steps = parts_ref.shape
    rows -= CODE_ROWS
    components, elements, steps = stress_ref.shape
    looked = range_ref.shape[0]
    scales = [code_scale(parts_ref[g, rows:, :].astype(jnp.int32).astype(jnp.float32)) for g in range(groups)]
    low = lax.broadcasted_iota(jnp.int32, (steps, 128), 1) < elements
    twice = []
    for i in range(rows // 128):
        total = None
        for g in range(groups):
            value = parts_ref[g, i * 128 : (i + 1) * 128, :].astype(jnp.int32).astype(jnp.float32)
            value = value * scales[g][i : i + 1]
            total = value if total is None else total + value
        upright = total.T
        stress_ref[2 * i] = upright[:elements]
        stress_ref[2 * i + 1] = upright[elements:]
        swapped = pltpu.roll(total, elements, 1)
        twice.append(jnp.where(low, total, swapped))
        twice.append(jnp.where(low, swapped, total))
    spreads = []
    for k in range(looked // 2):
        normal = coeffs_ref[k : k + 1, :] * twice[0]
        for q in range(1, components):
            normal = normal + coeffs_ref[q * looked + k : q * looked + k + 1, :] * twice[q]
        spreads.append(jnp.max(normal, axis=0, keepdims=True) - jnp.min(normal, axis=0, keepdims=True))
    spread = jnp.concatenate(spreads + spreads, axis=0)
    first = lax.broadcasted_iota(jnp.int32, (looked, 128), 0) < looked // 2
    range_ref[...] = jnp.where(first, spread, pltpu.roll(spread, elements, 1))[:, :elements]


def finish(parts, coeffs, looked):
    groups, rows, steps = parts.shape
    rows -= CODE_ROWS
    elements = 128 // 2
    stress, ranges = pl.pallas_call(
        range_kernel,
        out_shape=(
            jax.ShapeDtypeStruct((rows // elements, elements, steps), jnp.float32),
            jax.ShapeDtypeStruct((looked, elements), jnp.float32),
        ),
        in_specs=[pl.BlockSpec(memory_space=pltpu.VMEM)] * 2,
        out_specs=(pl.BlockSpec(memory_space=pltpu.VMEM),) * 2,
        compiler_params=pltpu.CompilerParams(vmem_limit_bytes=8 << 20),
        name="ranges",
    )(parts, coeffs)
    return stress, ranges.T


def gather_over(part, axes):
    copies = jnp.broadcast_to(part[None], (lax.axis_size(axes),) + part.shape)
    return lax.all_to_all(copies, axes, 0, 0)


def half_kernel(whole_ref, half_ref, sem):
    rows = half_ref.shape[0]
    start = pl.multiple_of(lax.axis_index("core") * rows, rows)
    fetch = pltpu.make_async_copy(whole_ref.at[pl.ds(start, rows)], half_ref, sem)
    fetch.start()
    fetch.wait()


def take_half(whole):
    channels, steps = whole.shape
    return pl.pallas_call(
        half_kernel,
        out_shape=jax.ShapeDtypeStruct((channels // 2, steps), whole.dtype),
        in_specs=[pl.BlockSpec(memory_space=pl.ANY)],
        out_specs=pl.BlockSpec(memory_space=pltpu.VMEM),
        scratch_shapes=[pltpu.SemaphoreType.DMA],
        compiler_params=pltpu.CompilerParams(vmem_limit_bytes=8 << 20),
        name="half",
    )(far(whole))


def pick_kernel(shift, owner_ref, offered_ref, out_ref):
    piece = offered_ref[lax.rem(lax.shift_right_logical(owner_ref[0], shift), offered_ref.shape[0])]
    for i in range(out_ref.shape[0]):
        out_ref[i] = piece


def pick_piece(offered, owner, shift, count):
    return pl.pallas_call(
        functools.partial(pick_kernel, shift),
        out_shape=jax.ShapeDtypeStruct((count,) + offered.shape[1:], offered.dtype),
        in_specs=[pl.BlockSpec(memory_space=pltpu.SMEM), pl.BlockSpec(memory_space=pltpu.VMEM)],
        out_specs=pl.BlockSpec(memory_space=pltpu.VMEM),
        compiler_params=pltpu.CompilerParams(vmem_limit_bytes=8 << 20),
        name="pick",
    )(owner, offered)


def fetch_window(whole, owner):
    channels, steps = whole.shape
    plane, along = lax.axis_size(ROW[1:]), lax.axis_size(ROW[0])
    shift = plane.bit_length() - 1
    rows = channels // 2 // plane

    def scatter(whole, owner):
        pieces = take_half(whole).reshape(plane, rows, steps)
        return pick_piece(lax.all_to_all(pieces, ROW[1:], 0, 0), owner, 0, along)

    def nothing(whole, owner):
        return jnp.zeros((along, rows, steps), whole.dtype)

    mine = lax.axis_index(ROW[0]) == lax.shift_right_logical(owner[0], shift)
    offered = lax.all_to_all(lax.cond(mine, scatter, nothing, whole, owner), ROW[0], 0, 0)
    whole_half = lax.all_to_all(pick_piece(offered, owner, shift, plane), ROW[1:], 0, 0)
    return lax.all_gather(whole_half.reshape(plane * rows, steps), "core", axis=0, tiled=True)


def body(load_windows, owner_id, participation, frequency, damping, recovery, pattern, plane_table):
    planes = plane_table[0, 0].T
    window = fetch_window(load_windows[0], owner_id)
    copies = make_history(window, participation, frequency[None], damping[None], lax.axis_size(FIRST))
    column = lax.all_to_all(copies, FIRST, 0, 0)
    hist = gather_over(column, THEN)
    own, come, coeffs = recover(hist, recovery[0, 0], pattern[0, 0].T, planes, lax.axis_size(("yh", "core")))
    parts = lax.all_to_all(pack_sums(own, come), "yh", 0, 0)
    stress, plane_range = finish(parts, coeffs, planes.shape[0])
    return (stress[None, None], plane_range[None, None])


def solution(mesh):
    fine = Mesh(mesh.devices.reshape(4, 2, 8, 2, 4), ("yh", "core") + ROW)
    mode = ("yh", "core")
    placed = (
        P(ROW, None, None),
        P(),
        P(mode + ROW, None),
        P(mode + ROW),
        P(mode + ROW),
        P(mode, ROW, None, None, None, None),
        P(mode, ROW, None, None),
        P(ROW, mode, None, None),
    )
    return jax.shard_map(
        body,
        mesh=fine,
        in_specs=placed,
        out_specs=(P(ROW, mode, None, None, None), P(ROW, mode, None, None)),
        check_vma=False,
    )
```

```python
import functools

import jax
import jax.numpy as jnp
from jax import lax
from jax.experimental import pallas as pl
from jax.experimental.pallas import tpu as pltpu
from jax.sharding import Mesh
from jax.sharding import PartitionSpec as P

ROW = ("z", "yl", "x")
FIRST, THEN = ROW[:1], ROW[1:]
CODE_ROWS = 8
LEVELS = 32760.0
PLANES = 64


def code_scale(code):
    return jnp.exp2(code * (1.0 / 32.0)) * (1.0 / LEVELS)


def quantize(values):
    largest = jnp.max(jnp.abs(values), axis=-1, keepdims=True)
    code = jnp.ceil(jnp.log2(jnp.maximum(largest, 1e-30)) * 32.0)
    inverse = jnp.exp2(code * (-1.0 / 32.0)) * LEVELS
    whole = jnp.round(values * inverse).astype(jnp.int32)
    return whole, code


def as_row(column):
    n = column.shape[0]
    at = lax.broadcasted_iota(jnp.int32, (n, 128), 0) == lax.broadcasted_iota(jnp.int32, (n, 128), 1)
    return jnp.sum(jnp.where(at, column, 0.0), axis=0, keepdims=True)


def mode_table(rates, decays, rows_ref):
    modes = rates.shape[1]
    shifts = (1 << lax.broadcasted_iota(jnp.int32, (8, modes), 0)).astype(jnp.float32)
    angle = rates * shifts
    cos, sin = jnp.cos(angle), jnp.sin(angle)
    shrink = jnp.exp(-decays * rates * shifts)
    rows_ref[0:8, :modes] = shrink * cos
    rows_ref[8:16, :modes] = shrink * sin
    rows_ref[16:24, :modes] = rates * jnp.broadcast_to(sin[0:1], (8, modes))
    rows_ref[24:32, :modes] = rates * jnp.broadcast_to(cos[0:1], (8, modes))
    return rows_ref[...].T[:modes]


def history_kernel(window_ref, *refs):
    part_ref, rate_ref, decay_ref, out_ref, rows_ref = refs
    table = mode_table(rate_ref[...], decay_ref[...], rows_ref)
    forces = jnp.dot(part_ref[...], window_ref[...], preferred_element_type=jnp.float32)
    modes, steps = forces.shape
    doublings = steps.bit_length() - 1
    lane = lax.broadcasted_iota(jnp.int32, forces.shape, 1)
    re, im = forces, jnp.zeros_like(forces)
    for d in range(doublings):
        shift = 1 << d
        p_re, p_im = table[:, d : d + 1], table[:, 8 + d : 9 + d]
        keep = lane >= shift
        old_re = jnp.where(keep, pltpu.roll(re, shift, 1), 0.0)
        if d == 0:
            re, im = re + p_re * old_re, p_im * old_re
            continue
        old_im = jnp.where(keep, pltpu.roll(im, shift, 1), 0.0)
        re, im = re + p_re * old_re - p_im * old_im, im + p_re * old_im + p_im * old_re
    hist = table[:, 16:17] * re + table[:, 24:25] * im
    whole, code = quantize(hist)
    codes = jnp.broadcast_to(as_row(code), (CODE_ROWS, 128)).astype(jnp.int32)
    block = jnp.concatenate([whole, codes], axis=0).astype(jnp.int16)
    for i in range(out_ref.shape[0]):
        out_ref[i] = block


def make_history(window, participation, frequency, damping, count):
    modes, channels = participation.shape
    steps = window.shape[1]
    return pl.pallas_call(
        history_kernel,
        out_shape=jax.ShapeDtypeStruct((count, modes + CODE_ROWS, steps), jnp.int16),
        in_specs=[pl.BlockSpec(memory_space=pltpu.VMEM)] * 4,
        out_specs=pl.BlockSpec(memory_space=pltpu.VMEM),
        scratch_shapes=[pltpu.VMEM((128, 128), jnp.float32)],
        compiler_params=pltpu.CompilerParams(vmem_limit_bytes=16 << 20),
        cost_estimate=pl.CostEstimate(
            flops=2 * modes * channels * steps, bytes_accessed=2 * (channels * (modes + steps)), transcendentals=0
        ),
        name="history",
    )(window, participation, frequency, damping)


def product(picks_ref, side, coeff_ref, split_ref, out_ref):
    per_slab, picked, height, width = coeff_ref.shape[1:]
    groups, _, steps = out_ref.shape
    for g in range(groups):
        for r in range(per_slab):
            block = (2 * g + side) * per_slab + r
            left = jnp.concatenate([coeff_ref[2 * g + side, r, k] for k in range(picked)], axis=1)
            starts = [pl.multiple_of(picks_ref[k, block] * width, width) for k in range(picked)]
            right = jnp.concatenate([split_ref[pl.ds(start, width), :] for start in starts], axis=0)
            both = jnp.dot(left, right, preferred_element_type=jnp.float32)
            out_ref[g, r * height : (r + 1) * height, :] = both[:, :steps] + both[:, steps:]


def first_kernel(hist_ref, picks_far, coeff_ref, other_ref, split_ref, picks_ref, picks_sem):
    fetch_picks = pltpu.make_async_copy(picks_far, picks_ref, picks_sem)
    fetch_picks.start()
    across, along, rows, steps = hist_ref.shape
    sources = across * along
    modes = rows - CODE_ROWS
    sub = lax.broadcasted_iota(jnp.int32, (8, 128), 0)
    tiles = []
    for base in range(0, sources, 8):
        tile = jnp.zeros((8, 128), jnp.int32)
        for i in range(8):
            s = base + i
            codes = hist_ref[s % across, s // across, modes : modes + CODE_ROWS, :].astype(jnp.int32)[:8]
            tile = jnp.where(sub == i, codes, tile)
        tiles.append(tile)
    scales = code_scale(jnp.concatenate(tiles, axis=0).astype(jnp.float32))
    scales = jnp.concatenate([scales, jnp.zeros((128 - sources, 128), jnp.float32)], axis=0).T
    for s in range(sources):
        value = hist_ref[s % across, s // across, :modes, :].astype(jnp.int32).astype(jnp.float32)
        value = value * scales[:modes, s : s + 1]
        high = value.astype(jnp.bfloat16)
        low = (value - high.astype(jnp.float32)).astype(jnp.bfloat16)
        split_ref[s * modes : (s + 1) * modes, :steps] = high
        split_ref[s * modes : (s + 1) * modes, steps:] = low
    fetch_picks.wait()
    product(picks_ref, 1 - lax.axis_index("core"), coeff_ref, split_ref, other_ref)


def second_kernel(
    split_ref, coeff_ref, planes_far, picks_far, own_ref, coeffs_ref, picks_ref, plane_ref, rows_ref, picks_sem, planes_sem
):
    fetch_picks = pltpu.make_async_copy(picks_far, picks_ref, picks_sem)
    fetch_planes = pltpu.make_async_copy(planes_far, plane_ref, planes_sem)
    fetch_picks.start()
    fetch_planes.start()
    fetch_planes.wait()
    plane_rows(plane_ref[...], rows_ref, coeffs_ref)
    fetch_picks.wait()
    product(picks_ref, lax.axis_index("core"), coeff_ref, split_ref, own_ref)


def far(x):
    return pltpu.with_memory_space_constraint(x, pltpu.HBM)


def recover(hist, coeff_blocks, picks, planes, groups):
    across, along, rows, steps = hist.shape
    blocks, picked, height, width = coeff_blocks.shape
    slabs = coeff_blocks.reshape(groups, blocks // groups, picked, height, width)
    half = jax.ShapeDtypeStruct((groups // 2, blocks // groups * height, steps), jnp.float32)
    cost = pl.CostEstimate(
        flops=2 * blocks * picked * height * width * steps,
        bytes_accessed=blocks * picked * height * width,
        transcendentals=0,
    )
    near, away = pl.BlockSpec(memory_space=pltpu.VMEM), pl.BlockSpec(memory_space=pl.ANY)
    scratch = [pltpu.SMEM(picks.shape, picks.dtype)]
    other, split = pl.pallas_call(
        first_kernel,
        out_shape=(
            half,
            jax.ShapeDtypeStruct((across * along * (rows - CODE_ROWS), 2 * steps), jnp.bfloat16),
        ),
        in_specs=[near, away, near],
        out_specs=(near,) * 2,
        scratch_shapes=scratch + [pltpu.SemaphoreType.DMA],
        compiler_params=pltpu.CompilerParams(vmem_limit_bytes=24 << 20),
        cost_estimate=cost,
        name="first",
    )(hist, far(picks), slabs)
    come = lax.ppermute(other, "core", [(0, 1), (1, 0)])
    own, coeffs = pl.pallas_call(
        second_kernel,
        out_shape=(half, jax.ShapeDtypeStruct((6 * planes.shape[0], 128), jnp.float32)),
        in_specs=[near, near, away, away],
        out_specs=(near,) * 2,
        scratch_shapes=scratch
        + [
            pltpu.VMEM(planes.shape, planes.dtype),
            pltpu.VMEM((6 * planes.shape[0], 128), jnp.float32),
            pltpu.SemaphoreType.DMA,
            pltpu.SemaphoreType.DMA,
        ],
        compiler_params=pltpu.CompilerParams(vmem_limit_bytes=24 << 20),
        cost_estimate=cost,
        name="second",
    )(split, slabs, far(planes), far(picks))
    return own, come, coeffs


def pack_kernel(own_ref, come_ref, out_ref):
    groups, rows, steps = out_ref.shape
    rows -= CODE_ROWS
    tiles = rows // 128
    for g in range(groups):
        sums, largest = [], []
        for i in range(tiles):
            here = pl.ds(i * 128, 128)
            turned = (own_ref[g, here, :] + come_ref[g, here, :]).T
            sums.append(turned)
            largest.append(jnp.max(jnp.abs(turned), axis=0, keepdims=True))
        largest.append(jnp.zeros((8 - tiles, 128), jnp.float32))
        code = jnp.ceil(jnp.log2(jnp.maximum(jnp.concatenate(largest, axis=0), 1e-30)) * 32.0)
        out_ref[g, rows:, :] = code.astype(jnp.int32).astype(jnp.int16)
        inverse = jnp.exp2(code * (-1.0 / 32.0)) * LEVELS
        for i in range(tiles):
            whole = jnp.round(sums[i] * inverse[i : i + 1])
            out_ref[g, i * 128 : (i + 1) * 128, :] = whole.astype(jnp.int32).astype(jnp.int16)


def pack_sums(own, come):
    groups, rows, steps = own.shape
    return pl.pallas_call(
        pack_kernel,
        out_shape=jax.ShapeDtypeStruct((groups, rows + CODE_ROWS, steps), jnp.int16),
        in_specs=[pl.BlockSpec(memory_space=pltpu.VMEM)] * 2,
        out_specs=pl.BlockSpec(memory_space=pltpu.VMEM),
        compiler_params=pltpu.CompilerParams(vmem_limit_bytes=16 << 20),
        name="pack",
    )(own, come)


def plane_rows(planes, pad_ref, out_ref):
    looked, elements = planes.shape
    index = planes.astype(jnp.float32)
    height = (index + 0.5) * (1.0 / PLANES)
    azimuth = index * 2.399963229728653
    radius = jnp.sqrt(1.0 - height * height)
    normal_x = radius * jnp.cos(azimuth)
    normal_y = radius * jnp.sin(azimuth)
    coeffs = [
        normal_x * normal_x,
        normal_y * normal_y,
        height * height,
        2.0 * normal_x * normal_y,
        2.0 * normal_y * height,
        2.0 * normal_x * height,
    ]
    pad_ref[...] = jnp.zeros_like(pad_ref)
    lane = lax.broadcasted_iota(jnp.int32, (looked, 128), 1)
    for q, coeff in enumerate(coeffs):
        pad_ref[q * looked : (q + 1) * looked, :elements] = coeff
        left = pad_ref[q * looked : (q + 1) * looked, :]
        right = pltpu.roll(pltpu.roll(left, elements, 1), looked // 2, 0)
        out_ref[q * looked : (q + 1) * looked, :] = jnp.where(lane < elements, left, right)


def range_kernel(parts_ref, coeffs_ref, stress_ref, range_ref):
    groups, rows, steps = parts_ref.shape
    rows -= CODE_ROWS
    components, elements, steps = stress_ref.shape
    looked = range_ref.shape[0]
    scales = [code_scale(parts_ref[g, rows:, :].astype(jnp.int32).astype(jnp.float32)) for g in range(groups)]
    low = lax.broadcasted_iota(jnp.int32, (steps, 128), 1) < elements
    twice = []
    for i in range(rows // 128):
        total = None
        for g in range(groups):
            value = parts_ref[g, i * 128 : (i + 1) * 128, :].astype(jnp.int32).astype(jnp.float32)
            value = value * scales[g][i : i + 1]
            total = value if total is None else total + value
        upright = total.T
        stress_ref[2 * i] = upright[:elements]
        stress_ref[2 * i + 1] = upright[elements:]
        swapped = pltpu.roll(total, elements, 1)
        twice.append(jnp.where(low, total, swapped))
        twice.append(jnp.where(low, swapped, total))
    spreads = []
    for k in range(looked // 2):
        normal = coeffs_ref[k : k + 1, :] * twice[0]
        for q in range(1, components):
            normal = normal + coeffs_ref[q * looked + k : q * looked + k + 1, :] * twice[q]
        spreads.append(jnp.max(normal, axis=0, keepdims=True) - jnp.min(normal, axis=0, keepdims=True))
    spread = jnp.concatenate(spreads + spreads, axis=0)
    first = lax.broadcasted_iota(jnp.int32, (looked, 128), 0) < looked // 2
    range_ref[...] = jnp.where(first, spread, pltpu.roll(spread, elements, 1))[:, :elements]


def finish(parts, coeffs, looked):
    groups, rows, steps = parts.shape
    rows -= CODE_ROWS
    elements = 128 // 2
    stress, ranges = pl.pallas_call(
        range_kernel,
        out_shape=(
            jax.ShapeDtypeStruct((rows // elements, elements, steps), jnp.float32),
            jax.ShapeDtypeStruct((looked, elements), jnp.float32),
        ),
        in_specs=[pl.BlockSpec(memory_space=pltpu.VMEM)] * 2,
        out_specs=(pl.BlockSpec(memory_space=pltpu.VMEM),) * 2,
        compiler_params=pltpu.CompilerParams(vmem_limit_bytes=8 << 20),
        name="ranges",
    )(parts, coeffs)
    return stress, ranges.T


def gather_over(part, axes):
    copies = jnp.broadcast_to(part[None], (lax.axis_size(axes),) + part.shape)
    return lax.all_to_all(copies, axes, 0, 0)


def half_kernel(whole_ref, half_ref, sem):
    rows = half_ref.shape[0]
    start = pl.multiple_of(lax.axis_index("core") * rows, rows)
    fetch = pltpu.make_async_copy(whole_ref.at[pl.ds(start, rows)], half_ref, sem)
    fetch.start()
    fetch.wait()


def take_half(whole):
    channels, steps = whole.shape
    return pl.pallas_call(
        half_kernel,
        out_shape=jax.ShapeDtypeStruct((channels // 2, steps), whole.dtype),
        in_specs=[pl.BlockSpec(memory_space=pl.ANY)],
        out_specs=pl.BlockSpec(memory_space=pltpu.VMEM),
        scratch_shapes=[pltpu.SemaphoreType.DMA],
        compiler_params=pltpu.CompilerParams(vmem_limit_bytes=8 << 20),
        name="half",
    )(far(whole))


def pick_kernel(shift, owner_ref, offered_ref, out_ref):
    piece = offered_ref[lax.rem(lax.shift_right_logical(owner_ref[0], shift), offered_ref.shape[0])]
    for i in range(out_ref.shape[0]):
        out_ref[i] = piece


def pick_piece(offered, owner, shift, count):
    return pl.pallas_call(
        functools.partial(pick_kernel, shift),
        out_shape=jax.ShapeDtypeStruct((count,) + offered.shape[1:], offered.dtype),
        in_specs=[pl.BlockSpec(memory_space=pltpu.SMEM), pl.BlockSpec(memory_space=pltpu.VMEM)],
        out_specs=pl.BlockSpec(memory_space=pltpu.VMEM),
        compiler_params=pltpu.CompilerParams(vmem_limit_bytes=8 << 20),
        name="pick",
    )(owner, offered)


def fetch_window(whole, owner):
    channels, steps = whole.shape
    plane, along = lax.axis_size(ROW[1:]), lax.axis_size(ROW[0])
    shift = plane.bit_length() - 1
    rows = channels // 2 // plane

    def scatter(whole, owner):
        pieces = take_half(whole).reshape(plane, rows, steps)
        return pick_piece(lax.all_to_all(pieces, ROW[1:], 0, 0), owner, 0, along)

    def nothing(whole, owner):
        return jnp.zeros((along, rows, steps), whole.dtype)

    mine = lax.axis_index(ROW[0]) == lax.shift_right_logical(owner[0], shift)
    offered = lax.all_to_all(lax.cond(mine, scatter, nothing, whole, owner), ROW[0], 0, 0)
    whole_half = lax.all_to_all(pick_piece(offered, owner, shift, plane), ROW[1:], 0, 0)
    return lax.all_gather(whole_half.reshape(plane * rows, steps), "core", axis=0, tiled=True)


def body(load_windows, owner_id, participation, frequency, damping, recovery, pattern, plane_table):
    planes = plane_table[0, 0].T
    window = fetch_window(load_windows[0], owner_id)
    copies = make_history(window, participation, frequency[None], damping[None], lax.axis_size(FIRST))
    column = lax.all_to_all(copies, FIRST, 0, 0)
    hist = gather_over(column, THEN)
    own, come, coeffs = recover(hist, recovery[0, 0], pattern[0, 0].T, planes, lax.axis_size(("yh", "core")))
    parts = lax.all_to_all(pack_sums(own, come), "yh", 0, 0)
    stress, plane_range = finish(parts, coeffs, planes.shape[0])
    return (stress[None, None], plane_range[None, None])


def solution(mesh):
    fine = Mesh(mesh.devices.reshape(4, 2, 8, 2, 4), ("yh", "core") + ROW)
    mode = ("yh", "core")
    placed = (
        P(ROW, None, None),
        P(),
        P(mode + ROW, None),
        P(mode + ROW),
        P(mode + ROW),
        P(mode, ROW, None, None, None, None),
        P(mode, ROW, None, None),
        P(ROW, mode, None, None),
    )
    return jax.shard_map(
        body,
        mesh=fine,
        in_specs=placed,
        out_specs=(P(ROW, mode, None, None, None), P(ROW, mode, None, None)),
        check_vma=False,
    )
```
